32 devices in a mesh: dp: 4 (over y, core), expert: 2 (over x), shard: 4 (over z).
Axes of the slice: x: 2, y: 2, z: 4, core: 2. Of those that a mesh axis runs over, the one named last changes fastest.
Arguments:
- tokens: bfloat16 [32768, 768], P(('dp', 'expert', 'shard')), may hold values from -6 to 6
- segments: int32 [32, 1024], P(('dp', 'expert', 'shard')), may hold values from 0 to 7, never falling along the last dimension, each value on 1 to 768 neighbouring positions
- routes: int32 [32768, 1], P(('dp', 'expert', 'shard')), may hold values from 0 to 3; in each aligned block of 1024 rows (0 to 1023, 1024 to 2047, ...) at most 512 rows name the same one
- cotangent: bfloat16 [32768, 768], P(('dp', 'expert', 'shard')), may hold values from -6 to 6
- attn_in: bfloat16 [768, 2304], P('shard'), may hold values from -0.21875 to 0.21875
- attn_out: bfloat16 [768, 768], P('shard'), may hold values from -1.75 to 1.75
- router: bfloat16 [768, 4], P('shard'), may hold values from -0.109375 to 0.109375
- gain_one: bfloat16 [768], P('shard'), may hold values from 0.5 to 1.5
- gain_two: bfloat16 [768], P('shard'), may hold values from 0.5 to 1.5
- expert_in: bfloat16 [4, 768, 3072], P('expert'), may hold values from -0.21875 to 0.21875
- expert_out: bfloat16 [4, 3072, 768], P('expert'), may hold values from -0.75 to 0.75
Outputs:
- layer_out: bfloat16 [32768, 768], P(('dp', 'expert', 'shard'))
- grad_tokens: bfloat16 [32768, 768], P(('dp', 'expert', 'shard'))
- grad_attn_in: float32 [768, 2304], P('shard')
- grad_attn_out: float32 [768, 768], P('shard')
- grad_router: float32 [768, 4], P('shard')
- grad_gain_one: float32 [768], P('shard')
- grad_gain_two: float32 [768], P('shard')
- grad_expert_in: float32 [4, 768, 3072], P('expert', None, 'shard')
- grad_expert_out: float32 [4, 3072, 768], P('expert', 'shard')
The draws below stay inside these ranges and needn't reach their ends.
Inputs may be any that keep to these rules, and one draw needn't show every extreme that they name: `routes`: within the aligned blocks of 1024 token rows no expert is named by more than 512 rows, and in every draw some expert is named by exactly 512 rows of some block. `segments`: segment numbers never fall along a sequence; a document has at most 768 tokens, and some document has exactly that many.
All inputs are finite; a program needn't handle non-finite values.
Results may differ from the reference program's by a relative error of at most 0.022.
Values may be sent and summed in bfloat16 or wider, within the bound.
No kernel may reach another device: no remote copies, remote signals or barrier semaphores. Data moves between devices by JAX's collectives and lax.ppermute only.
A program may use at most 384 MiB of HBM per device.

```python
import math
import jax
import jax.numpy as jnp
import numpy as np
from jax import lax

D = 768
HEADS = 12
HEAD_DIM = 64
FF = 3072
LENGTH = 1024
SEQ_DEV = 1
TOK_DEV = 1024
SEQS = 32
TOKENS = 32768
EXPERTS = 4
CAP = 512
DOCS = 8
DOC_MOST = 768


def steps_of(stream_key, extent, cuts, least, high):
    def one(axis_at, blocks):
        steps = jax.random.uniform(jax.random.fold_in(jax.random.fold_in(stream_key, 6), axis_at), (blocks,), jnp.float32, least / len(cuts), high / len(cuts))
        return jnp.repeat(jnp.exp(steps), extent[axis_at] // blocks).reshape((-1,) + (1,) * (len(extent) - axis_at - 1))

    factor_of = one(*cuts[0])
    for cut in cuts[1:]:
        factor_of = factor_of * one(*cut)
    return factor_of


def length_profile(count, total, most, skew):
    portions = [(1 << 20) // math.isqrt(standing ** skew) + 1 for standing in range(2, count + 1)]
    rest, counts = total - most - (count - 1), [1] * (count - 1)
    while rest > 0:
        candidates = [i for i in range(count - 1) if counts[i] < most]
        mass, left = sum([portions[i] for i in candidates]), rest
        for i in candidates:
            more = min(most - counts[i], max(1, left * portions[i] // mass), rest)
            counts[i] = counts[i] + more
            rest = rest - more
    return np.array([most] + counts)


def uneven(key, amount, total, most, lean):
    if amount == 2:
        one = jax.random.randint(key, (), max(1, total - most), min(most, total - 1) + 1)
        return jnp.stack([one, total - one])
    sizes = jnp.asarray(length_profile(amount, total, most, lean), jnp.int32)
    couples = (amount - 1) // 2
    giver, receiver = sizes[1:1 + 2 * couples:2], sizes[2:2 + 2 * couples:2]
    slack = jnp.minimum(giver - 1, most - receiver)
    shifted = jax.random.randint(jax.random.fold_in(key, 1), (couples,), 0, 1 << 20) % (slack + 1)
    sizes = sizes.at[1:1 + 2 * couples:2].set(giver - shifted).at[2:2 + 2 * couples:2].set(receiver + shifted)
    return sizes[jax.random.permutation(jax.random.fold_in(key, 2), amount)]


def assign_block(own_key, own, number, rows, amount, top, limit, skew):
    sequence = jax.random.permutation(own_key, amount)
    heavy_load, ordinary = portions_of(amount, rows * top, limit, skew, True), portions_of(amount, rows * top, limit, skew, False)
    places = jnp.arange(amount)

    def named(lengths, rotation):
        used = int((lengths > 0).sum())
        fixed = max(1, used // 4)
        passed = fixed + (places - fixed + rotation * (used - fixed)) % max(1, amount - fixed)
        return jnp.zeros((amount,), jnp.int32).at[sequence[jnp.where(places < fixed, places, passed)]].set(jnp.asarray(lengths, jnp.int32))

    lengths = jnp.where(number % 4 == 0, named(heavy_load, number // 4), named(ordinary, number - number // 4 - 1))
    mixed = jax.random.permutation(jax.random.fold_in(own, 3), amount)
    donor, receiver = mixed[0:amount // 2 * 2:2], mixed[1:amount // 2 * 2:2]
    room = jnp.minimum(lengths[donor] - 1, limit - lengths[receiver]) // 2
    room = jnp.where((donor == sequence[0]) | (receiver == sequence[0]) | (lengths[receiver] == 0), 0, jnp.maximum(room, 0))
    passed = jax.random.randint(jax.random.fold_in(own, 4), (amount // 2,), 0, 1 << 20) % (room + 1)
    lengths = lengths.at[donor].add(-passed).at[receiver].add(passed)
    members = jnp.searchsorted(jnp.cumsum(lengths), jnp.arange(rows * top), side="right").astype(jnp.int32)
    table = members.reshape(top, rows).T
    table = table[jax.random.permutation(jax.random.fold_in(own, 1), rows)]
    rotation = jax.random.randint(jax.random.fold_in(own, 2), (rows, 1), 0, top)
    return jnp.take_along_axis(table, (jnp.arange(top)[None, :] + rotation) % top, axis=1)


def portions_of(number_of, total, limit, lean, full):
    loads = [(1 << 20) // math.isqrt(grade ** lean) + 1 for grade in range(1, number_of + 1)]
    largest = limit if full else min(limit, max(-(-total // number_of), total * loads[0] // sum(loads)))
    least = 1 if total - largest >= number_of - 1 else 0
    counts, rest = [largest] + [least] * (number_of - 1), total - largest - least * (number_of - 1)
    while rest > 0:
        candidates = [i for i in range(1, number_of) if counts[i] < largest] or [i for i in range(1, number_of) if counts[i] < limit]
        mass, left = sum([loads[i] for i in candidates]), rest
        for i in candidates:
            more = min(limit - counts[i], max(1, left * loads[i] // mass), rest)
            counts[i] = counts[i] + more
            rest = rest - more
    return np.array(counts)


def bell_draw(rng, shape, deviation, limit, cuts=(), held_as=jnp.bfloat16):
    values = deviation * jax.random.normal(rng, shape, jnp.float32)
    if cuts:
        values = values * steps_of(rng, shape, cuts, -0.22, 0.18)
    return jnp.clip(values, -limit, limit).astype(held_as)


def setup_inputs(seed: int = 0) -> dict:
    key_of = jax.random.split(jax.random.key(seed), 12)
    tokens = bell_draw(key_of[0], (TOKENS, D), 1.0, 6.0, ((0, 32),))
    segments = jax.vmap(lambda own: jnp.searchsorted(jnp.cumsum(uneven(own, DOCS, LENGTH, DOC_MOST, 1)), jnp.arange(LENGTH), side="right"))(jax.random.split(key_of[1], SEQS)).reshape((SEQS, LENGTH)).astype(jnp.int32)
    routes_keys = jax.random.split(jax.random.fold_in(key_of[2], 1), TOKENS // TOK_DEV)
    routes_turns = jax.random.permutation(jax.random.fold_in(key_of[2], 3), TOKENS // TOK_DEV)
    routes = jax.vmap(lambda own, number: assign_block(jax.random.fold_in(key_of[2], 2), own, number, TOK_DEV, EXPERTS, 1, CAP, 2))(routes_keys, routes_turns).reshape((TOKENS, 1))
    cotangent = bell_draw(key_of[3], (TOKENS, D), 1.0, 6.0, ((0, 32),))
    attn_in = bell_draw(key_of[4], (D, 3 * D), D ** -0.5, 0.21875, ((0, 4),))
    attn_out = bell_draw(key_of[5], (D, D), (max(1, D // 64)) ** -0.5, 1.75, ((0, 4),))
    router = bell_draw(key_of[6], (D, EXPERTS), (4 * D) ** -0.5, 0.109375, ((0, 4),))
    gain_one = jnp.clip(1.0 + 0.1 * jax.random.normal(key_of[7], (D,), jnp.float32), 0.5, 1.5).astype(jnp.bfloat16)
    gain_two = jnp.clip(1.0 + 0.1 * jax.random.normal(key_of[8], (D,), jnp.float32), 0.5, 1.5).astype(jnp.bfloat16)
    expert_in = bell_draw(key_of[9], (EXPERTS, D, FF), D ** -0.5, 0.21875, ((0, 2),))
    expert_out = bell_draw(key_of[10], (EXPERTS, FF, D), (max(1, FF // (3 * EXPERTS * EXPERTS))) ** -0.5, 0.75, ((0, 2),))
    return dict(tokens=tokens, segments=segments, routes=routes, cotangent=cotangent, attn_in=attn_in, attn_out=attn_out, router=router, gain_one=gain_one, gain_two=gain_two, expert_in=expert_in, expert_out=expert_out)


@jax.custom_vjp
def low(v):
    return lax.optimization_barrier(v.astype(jnp.bfloat16)).astype(jnp.float32)

@jax.custom_vjp
def low_back(v):
    return v

def low_keep(v):
    return (low(v), None)

def low_pass(kept, grad):
    return (grad,)

def back_keep(v):
    return (v, None)

def back_low(kept, grad):
    return (low(grad),)
low.defvjp(low_keep, low_pass)
low_back.defvjp(back_keep, back_low)
EPSILON = 1e-06
MASKED = -1e+30
PRECISE = lax.Precision.HIGHEST

def rms_gain(values, gain_row):
    return values * lax.rsqrt(lax.optimization_barrier(jnp.mean(values * values, axis=-1, keepdims=True)) + EPSILON) * gain_row

def attend_sequence(packed):
    triple, seg_row = packed
    parted = triple.reshape(LENGTH, 3, HEADS, HEAD_DIM)
    query_all = parted[:, 0]
    key_all = parted[:, 1]
    value_all = parted[:, 2]
    scores = jnp.einsum('qhd,khd->hqk', query_all, key_all, precision=PRECISE) * (1.0 / math.sqrt(HEAD_DIM))
    scores = low_back(scores)
    same_doc = seg_row[:, None] == seg_row[None, :]
    weights = low(jax.nn.softmax(jnp.where(same_doc[None], scores, MASKED), axis=-1))
    attended = jnp.einsum('hqk,khd->qhd', weights, value_all, precision=PRECISE)
    return low_back(low(attended.reshape(LENGTH, D)))

def layer_block(params, block_rows, seg_block, route_ids):
    attn_in, attn_out, router, gain_one, gain_two, expert_in, expert_out = params
    normed = low(rms_gain(block_rows, gain_one))
    triple = low_back(low(jnp.dot(normed, attn_in, precision=PRECISE)))
    attended = lax.map(attend_sequence, (triple.reshape(SEQ_DEV, LENGTH, 3 * D), seg_block)).reshape(TOK_DEV, D)
    hidden_one = block_rows + low_back(jnp.dot(attended, attn_out, precision=PRECISE))
    second = low(rms_gain(hidden_one, gain_two))
    logits = low_back(jnp.dot(second, router, precision=PRECISE))
    router_probs = jax.nn.softmax(logits, axis=-1)
    choose = route_ids[:, None] == jnp.arange(EXPERTS, dtype=jnp.int32)[None, :]
    gate_value = lax.optimization_barrier(jnp.sum(jnp.where(choose, router_probs, 0.0), axis=1))
    rank_inside = jnp.cumsum(choose.astype(jnp.int32), axis=0) - 1
    slot_index = (route_ids * CAP + lax.optimization_barrier(jnp.sum(jnp.where(choose, rank_inside, 0), axis=1))).astype(jnp.int32)
    sent_rows = low_back(second)
    slot_rows = jnp.zeros((EXPERTS * CAP, D), sent_rows.dtype).at[slot_index].set(sent_rows).reshape(EXPERTS, CAP, D)
    pre_act = low_back(jnp.einsum('ecd,edf->ecf', slot_rows, expert_in, precision=PRECISE))
    activated = low(jax.nn.gelu(pre_act, approximate=True))
    produced = low_back(low(jnp.einsum('ecf,efd->ecd', activated, expert_out, precision=PRECISE)))
    returned = produced.reshape(EXPERTS * CAP, D)[slot_index]
    return hidden_one + gate_value[:, None] * returned

def reference(tokens, segments, routes, cotangent, attn_in, attn_out, router, gain_one, gain_two, expert_in, expert_out):
    params = tuple((weight.astype(jnp.float32) for weight in (attn_in, attn_out, router, gain_one, gain_two, expert_in, expert_out)))
    block_count = TOKENS // TOK_DEV
    rows_all = tokens.astype(jnp.float32).reshape(block_count, TOK_DEV, D)
    seg_blocks = segments.reshape(block_count, SEQ_DEV, LENGTH)
    route_blocks = routes.reshape(block_count, TOK_DEV).astype(jnp.int32)
    step_fn = jax.checkpoint(layer_block)

    def forward(weights_all, rows_in):

        def one_block(carried, packed):
            return (carried, step_fn(weights_all, packed[0], packed[1], packed[2]))
        finished, outputs = lax.scan(one_block, jnp.zeros((), jnp.float32), (rows_in, seg_blocks, route_blocks))
        return outputs
    layer_out, pullback = jax.vjp(forward, params, rows_all)
    grad_params, grad_rows = pullback(cotangent.astype(jnp.float32).reshape(block_count, TOK_DEV, D))
    return (layer_out.reshape(TOKENS, D).astype(jnp.bfloat16), grad_rows.reshape(TOKENS, D).astype(jnp.bfloat16), grad_params[0], grad_params[1], grad_params[2], grad_params[3], grad_params[4], grad_params[5], grad_params[6])
```

```python
import functools
import math

import jax
import jax.numpy as jnp
from jax import lax
from jax.experimental import pallas as pl
from jax.experimental.pallas import tpu as pltpu
from jax.sharding import PartitionSpec as P

HEADS = 12
LANES = 128
EPSILON = 1e-06
MASKED = -1e30
BF16 = jnp.bfloat16
F32 = jnp.float32
NN = (((1,), (0,)), ((), ()))
NT = (((1,), (1,)), ((), ()))
TN = (((0,), (0,)), ((), ()))
CHUNKS = 2
GROUPS = 3
GATHERS = 2
SHARE = 0.12
GELU_C = math.sqrt(2.0 / math.pi)
GELU_A = 0.044715


def dot(left, right, dims=NN):
    return lax.dot_general(left, right, dims, preferred_element_type=F32)


def params(mebibytes=60):
    return pltpu.CompilerParams(vmem_limit_bytes=mebibytes << 20)


def lasting(microseconds):
    return pl.CostEstimate(
        flops=int(microseconds * SHARE * 1.15e9), bytes_accessed=0, transcendentals=0
    )


def whole_spec(shape, buffers=1):
    return pl.BlockSpec(
        shape, lambda *_: (0,) * len(shape), pipeline_mode=pl.Buffered(buffers)
    )


def lane_parts(value, lane):
    high = value.astype(BF16).astype(F32)
    middle = (value - high).astype(BF16).astype(F32)
    low = value - high - middle
    return jnp.where(lane < 16, high, jnp.where(lane < 32, middle, low))


def attend_kernel(q_ref, k_ref, v_ref, segq_ref, segk_ref, out_ref, qaug_ref, lse_ref, *, block):
    pair, pairs = pl.program_id(0), pl.num_programs(0)
    rows, keys = q_ref.shape[0], k_ref.shape[0]
    lane_k = lax.broadcasted_iota(jnp.int32, (keys, LANES), 1)
    lane_q = lax.broadcasted_iota(jnp.int32, (rows, LANES), 1)
    k_mark = jnp.where((lane_k - 48) == segk_ref[...], 1.0, 0.0).astype(BF16)
    zone = (lane_q >= 48) & (lane_q < 56)
    q_mark = jnp.where(zone & ((lane_q - 48) != segq_ref[...]), MASKED, 0.0)

    @pl.when(pair == 0)
    def _():
        lse_ref[...] = jnp.zeros_like(lse_ref)

    k_mark = jnp.where((lane_k >= 48) & (lane_k < 56), k_mark, jnp.asarray(0, BF16))
    k_wide = jnp.concatenate([k_ref[...], k_mark], axis=1)
    v_wide = jnp.concatenate([v_ref[...], jnp.ones((keys, LANES), BF16)], axis=1)
    lane = lane_q[:block]
    for start in range(0, rows, block):
        part = slice(start, start + block)
        query = q_ref[part] * jnp.asarray(0.125, BF16)
        outs = []
        stats = lse_ref[part]
        for side in range(2):
            own = (lane >= 64) if side else (lane < 64)
            picked = jnp.where(own, query, jnp.asarray(0, BF16))
            scores = dot(
                jnp.concatenate([picked, q_mark[part].astype(BF16)], axis=1), k_wide, NT
            )
            row_max = jnp.max(scores, axis=1, keepdims=True)
            raised = jnp.exp(scores - row_max).astype(BF16)
            summed = dot(raised, v_wide)
            total = summed[:, LANES:]
            outs.append(summed[:, :LANES] / total)
            mine = ((lane & 15) == 2 * pair + side) & (lane < 48)
            stats = jnp.where(mine, row_max + jnp.log(total), stats)
        out_ref[part] = jnp.where(lane < 64, outs[0], outs[1]).astype(BF16)
        lse_ref[part] = stats

    @pl.when(pair == pairs - 1)
    def _():
        stats = lane_parts(lse_ref[...], lane_q)
        qaug_ref[...] = jnp.where(lane_q < 48, stats, q_mark).astype(BF16)


def attend_forward(triple, segment_col, chunk, rows, block=256):
    keys, width = triple.shape[0], triple.shape[1] // 3
    pairs = width // LANES
    return pl.pallas_call(
        functools.partial(attend_kernel, block=block),
        grid=(pairs,),
        in_specs=[
            pl.BlockSpec((rows, LANES), lambda p: (chunk, p)),
            pl.BlockSpec((keys, LANES), lambda p: (0, pairs + p)),
            pl.BlockSpec((keys, LANES), lambda p: (0, 2 * pairs + p)),
            pl.BlockSpec((rows, 1), lambda p: (chunk, 0)),
            pl.BlockSpec((keys, 1), lambda p: (0, 0)),
        ],
        out_specs=[
            pl.BlockSpec((rows, LANES), lambda p: (0, p)),
            pl.BlockSpec((rows, LANES), lambda p: (0, 0)),
        ],
        out_shape=[
            jax.ShapeDtypeStruct((rows, width), BF16),
            jax.ShapeDtypeStruct((rows, LANES), BF16),
        ],
        scratch_shapes=[pltpu.VMEM((rows, LANES), F32)],
        compiler_params=params(),
        cost_estimate=lasting(14),
        name="attend_forward",
    )(triple, triple, triple, segment_col, segment_col)


def attend_back_kernel(q_ref, k_ref, v_ref, g_ref, seg_ref, qaug_ref, gaug_ref, out_ref, *, block, first_head):
    pair = pl.program_id(0)
    rows = q_ref.shape[0]
    lane = lax.broadcasted_iota(jnp.int32, (block, LANES), 1)
    zero = jnp.asarray(0, BF16)
    query = q_ref[...] * jnp.asarray(0.125, BF16)
    grad = g_ref[...]
    q_wide = jnp.concatenate([query, qaug_ref[...]], axis=1)
    g_wide = jnp.concatenate([grad, gaug_ref[...]], axis=1)
    zone = (lane >= 48) & (lane < 56)
    grad_q = [jnp.zeros((64, rows), F32), jnp.zeros((64, rows), F32)]
    for start in range(0, rows, block):
        part = slice(start, start + block)
        key, value = k_ref[part], v_ref[part]
        key_turned = key.T
        doc = zone & ((lane - 48) == seg_ref[part])
        grads_k, grads_v = [], []
        for side in range(2):
            own = (lane >= 64) if side else (lane < 64)
            stat = ((lane & 15) == first_head + 2 * pair + side) & (lane < 48)
            k_mark = jnp.where(stat, -1.0, jnp.where(doc, 1.0, 0.0)).astype(BF16)
            v_mark = jnp.where(stat, -1.0, 0.0).astype(BF16)
            k_wide = jnp.concatenate([jnp.where(own, key, zero), k_mark], axis=1)
            v_wide = jnp.concatenate([jnp.where(own, value, zero), v_mark], axis=1)
            probs = jnp.exp(dot(k_wide, q_wide, NT))
            grad_scores = (probs * dot(v_wide, g_wide, NT)).astype(BF16)
            grads_v.append(dot(probs.astype(BF16), grad))
            grads_k.append(dot(grad_scores, query))
            grad_q[side] = grad_q[side] + dot(
                key_turned[64 * side : 64 * side + 64], grad_scores
            )
        out_ref[1, part] = jnp.where(lane < 64, grads_k[0], grads_k[1]).astype(BF16)
        out_ref[2, part] = jnp.where(lane < 64, grads_v[0], grads_v[1]).astype(BF16)
    out_ref[0] = (jnp.concatenate(grad_q, axis=0) * 0.125).T.astype(BF16)


def attend_backward(triple, grad, segment_col, qaug, gaug, first_head, heads, block=512):
    rows, width = triple.shape[0], triple.shape[1] // 3
    pairs, first = width // LANES, first_head // 2
    pair_of = lambda offset: pl.BlockSpec((rows, LANES), lambda p: (0, offset + p))
    return pl.pallas_call(
        functools.partial(attend_back_kernel, block=block, first_head=first_head),
        grid=(heads // 2,),
        in_specs=[
            pair_of(first),
            pair_of(pairs + first),
            pair_of(2 * pairs + first),
            pair_of(first),
            pl.BlockSpec((rows, 1), lambda p: (0, 0)),
            pl.BlockSpec((rows, LANES), lambda p: (0, 0)),
            pl.BlockSpec((rows, LANES), lambda p: (0, 0)),
        ],
        out_specs=pl.BlockSpec((3, rows, LANES), lambda p: (0, 0, p)),
        out_shape=jax.ShapeDtypeStruct((3, rows, heads * 64), BF16),
        compiler_params=params(),
        cost_estimate=lasting(13),
        name="attend_backward",
    )(triple, triple, triple, grad, segment_col, qaug, gaug)


def qkv_kernel(tok_ref, gain_ref, *refs):
    weights, (normed_ref, triple_ref) = refs[:-2], refs[-2:]
    rows = tok_ref[...].astype(F32)
    scale = lax.rsqrt(jnp.mean(rows * rows, axis=1, keepdims=True) + EPSILON)
    normed = (rows * scale * gain_ref[...]).astype(BF16)
    normed_ref[...] = normed
    start = 0
    for weight in weights:
        stop = min(start + weight.shape[1], triple_ref.shape[1])
        triple_ref[:, start:stop] = dot(normed, weight[:, : stop - start]).astype(BF16)
        start = stop


def qkv(tokens, gain_row, weights, block=256):
    rows, width = tokens.shape
    return pl.pallas_call(
        qkv_kernel,
        grid=(rows // block,),
        in_specs=[pl.BlockSpec((block, width), lambda i: (i, 0)), whole_spec((1, width))]
        + [whole_spec(weight.shape) for weight in weights],
        out_specs=[
            pl.BlockSpec((block, width), lambda i: (i, 0)),
            pl.BlockSpec((block, 3 * width), lambda i: (i, 0)),
        ],
        out_shape=[
            jax.ShapeDtypeStruct((rows, width), BF16),
            jax.ShapeDtypeStruct((rows, 3 * width), BF16),
        ],
        compiler_params=params(),
        cost_estimate=lasting(8),
        name="qkv",
    )(tokens, gain_row, *weights)


def project_kernel(tok_ref, *refs):
    w_ref, gain_ref, hidden_ref, second_ref = refs[-4:]
    attended = jnp.concatenate([ref[...] for ref in refs[:-4]], axis=1)
    hidden = tok_ref[...].astype(F32) + dot(attended, w_ref[...])
    scale = lax.rsqrt(jnp.mean(hidden * hidden, axis=1, keepdims=True) + EPSILON)
    hidden_ref[...] = hidden
    second_ref[...] = (hidden * scale * gain_ref[...]).astype(BF16)


def project(tokens, attended, weights, gain_row, chunk, block=256):
    attended = [attended]
    rows, part = attended[0].shape
    width = tokens.shape[1]
    steps = rows // block
    here = lambda i: (i, 0)
    return pl.pallas_call(
        project_kernel,
        grid=(steps,),
        in_specs=[pl.BlockSpec((block, width), lambda i: (chunk * steps + i, 0))]
        + [pl.BlockSpec((block, part), here)] * len(attended)
        + [whole_spec((width, width)), whole_spec((1, width))],
        out_specs=[pl.BlockSpec((block, width), here), pl.BlockSpec((block, width), here)],
        out_shape=[
            jax.ShapeDtypeStruct((rows, width), F32),
            jax.ShapeDtypeStruct((rows, width), BF16),
        ],
        compiler_params=params(),
        cost_estimate=lasting(4),
        name="project",
    )(tokens, *attended, weights, gain_row)


def routed_gate(second, router, route_col, experts):
    logits = dot(second, router)
    lane = lax.broadcasted_iota(jnp.int32, logits.shape, 1)
    logits = jnp.where(lane < experts, logits, MASKED)
    raised = jnp.exp(logits - jnp.max(logits, axis=1, keepdims=True))
    probs = raised / jnp.sum(raised, axis=1, keepdims=True)
    chosen = lane == route_col
    gate = jnp.sum(jnp.where(chosen, probs, 0.0), axis=1, keepdims=True)
    return probs, chosen, gate


def on_rows(full, run, capacity):
    pl.when(full == 1)(functools.partial(run, capacity))
    pl.when(full == 0)(functools.partial(run, capacity // 2))


def expert_kernel(
    full_ref,
    rows_a,
    rows_b,
    cot_ref,
    route_ref,
    router_ref,
    place_ref,
    place_col_ref,
    w_in_ref,
    w_out_ref,
    act_ref,
    grad_pre_ref,
    x_ref,
    g_ref,
    ret_ref,
    back_ref,
    gate_ref,
    produced,
    grad_rows,
    *,
    experts,
):
    ff, expert = pl.program_id(0), pl.program_id(1)
    slots = x_ref.shape[0]
    capacity = slots // full_ref.shape[1]
    half = capacity // 2

    @pl.when((ff == 0) & (expert == 0))
    def _():
        produced[...] = jnp.zeros_like(produced)
        grad_rows[...] = jnp.zeros_like(grad_rows)
        second = jnp.concatenate([rows_a[...], rows_b[...]], axis=0)
        _, _, gate = routed_gate(second, router_ref[...], route_ref[...], experts)
        gated = (gate * cot_ref[...].astype(F32)).astype(BF16)

        def pack(start):
            part = slice(start, start + half)
            slot = start + lax.broadcasted_iota(jnp.int32, (half, second.shape[0]), 0)
            pick = jnp.where(slot == place_ref[...], 1.0, 0.0).astype(BF16)
            x_ref[part, :] = dot(pick, second).astype(BF16)
            g_ref[part, :] = dot(pick, gated).astype(BF16)

        for owner in range(slots // capacity):
            pack(owner * capacity)
            pl.when(full_ref[0, owner] == 1)(
                functools.partial(pack, owner * capacity + half)
            )

    def run(rows):
        part = pl.ds(pl.multiple_of(expert * capacity, capacity), rows)
        pre = dot(x_ref[part, :], w_in_ref[0])
        grad_act = dot(g_ref[part, :], w_out_ref[0], NT)
        square = pre * pre
        bend = jnp.tanh(pre * (GELU_C + GELU_C * GELU_A * square))
        upper = 0.5 + 0.5 * bend
        act = (pre * upper).astype(BF16)
        inner = pre * (GELU_C + 3.0 * GELU_C * GELU_A * square)
        slope = upper + inner * (0.5 - 0.5 * bend * bend)
        grad_pre = (grad_act * slope).astype(BF16)
        act_ref[part, :] = act
        grad_pre_ref[part, :] = grad_pre
        produced[part, :] += dot(act, w_out_ref[0])
        grad_rows[part, :] += dot(grad_pre, w_in_ref[0], NT)

    on_rows(full_ref[0, expert], run, capacity)

    @pl.when((ff == pl.num_programs(0) - 1) & (expert == pl.num_programs(1) - 1))
    def _():
        count = ret_ref.shape[0]
        slot = lax.broadcasted_iota(jnp.int32, (count, slots), 1)
        pick = jnp.where(slot == place_col_ref[...], 1.0, 0.0).astype(BF16)
        returned = dot(pick, produced[...].astype(BF16))
        ret_ref[...] = returned.astype(BF16)
        back_ref[...] = dot(pick, grad_rows[...].astype(BF16)).astype(BF16)
        inner = jnp.sum(cot_ref[...].astype(F32) * returned, axis=1, keepdims=True)
        gate_ref[...] = jnp.broadcast_to(inner, gate_ref.shape)


def expert_rows(full, rows, cot, route_col, router, place, w_in, w_out, capacity, experts, ff_block):
    count, width = cot.shape
    local, _, ff = w_in.shape
    slots = local * capacity
    column = lambda f, e, _: (0, f)
    return pl.pallas_call(
        functools.partial(expert_kernel, experts=experts),
        grid_spec=pltpu.PrefetchScalarGridSpec(
            num_scalar_prefetch=1,
            grid=(ff // ff_block, local),
            in_specs=[
                whole_spec(rows[0].shape),
                whole_spec(rows[1].shape),
                whole_spec((count, width)),
                whole_spec((count, 1)),
                whole_spec(router.shape),
                whole_spec((1, count)),
                whole_spec((count, 1)),
                pl.BlockSpec((1, width, ff_block), lambda f, e, _: (e, 0, f)),
                pl.BlockSpec((1, ff_block, width), lambda f, e, _: (e, f, 0)),
            ],
            out_specs=[
                pl.BlockSpec((slots, ff_block), column),
                pl.BlockSpec((slots, ff_block), column),
                whole_spec((slots, width)),
                whole_spec((slots, width)),
                whole_spec((count, width)),
                whole_spec((count, width)),
                whole_spec((count, LANES)),
            ],
            scratch_shapes=[
                pltpu.VMEM((slots, width), F32),
                pltpu.VMEM((slots, width), F32),
            ],
        ),
        out_shape=[
            jax.ShapeDtypeStruct((slots, ff), BF16),
            jax.ShapeDtypeStruct((slots, ff), BF16),
            jax.ShapeDtypeStruct((slots, width), BF16),
            jax.ShapeDtypeStruct((slots, width), BF16),
            jax.ShapeDtypeStruct((count, width), BF16),
            jax.ShapeDtypeStruct((count, width), BF16),
            jax.ShapeDtypeStruct((count, LANES), F32),
        ],
        compiler_params=params(),
        cost_estimate=lasting(28),
        name="expert_rows",
    )(full, *rows, cot, route_col, router, place[None, :], place[:, None], w_in, w_out)


def weight_grad_kernel(full_ref, expert_ref, left_a, left_b, right_a, right_b, out_ref):
    expert = expert_ref[0]
    capacity = left_a.shape[0]

    def run(rows_a, rows_b):
        out_ref[0] = (
            dot(left_a[:rows_a, :], right_a[:rows_a, :], TN)
            + dot(left_b[:rows_b, :], right_b[:rows_b, :], TN)
        ).astype(BF16)

    for full_a in range(2):
        for full_b in range(2):
            pl.when((full_ref[0, expert] == full_a) & (full_ref[1, expert] == full_b))(
                functools.partial(
                    run, capacity // (2 - full_a), capacity // (2 - full_b)
                )
            )


def weight_grad(full, expert, left, right, capacity, ff_block):
    slots, width = left[0].shape
    ff = max(width, right[0].shape[1])
    spec = lambda value: (
        pl.BlockSpec((capacity, ff_block), lambda f, _, e: (e[0], f))
        if value.shape[1] == ff
        else pl.BlockSpec(
            (capacity, value.shape[1]), lambda f, _, e: (e[0], 0), pipeline_mode=pl.Buffered(1)
        )
    )
    block = lambda value: ff_block if value.shape[1] == ff else value.shape[1]
    shape = (block(left[0]), block(right[0]))
    return pl.pallas_call(
        weight_grad_kernel,
        grid_spec=pltpu.PrefetchScalarGridSpec(
            num_scalar_prefetch=2,
            grid=(ff // ff_block,),
            in_specs=[spec(value) for value in (*left, *right)],
            out_specs=pl.BlockSpec((1,) + shape, lambda f, *_: (f, 0, 0)),
        ),
        out_shape=jax.ShapeDtypeStruct((ff // ff_block,) + shape, BF16),
        compiler_params=params(),
        cost_estimate=lasting(9),
        name="weight_grad",
    )(full, expert, *left, *right)


def hidden_back_kernel(
    hidden_a,
    hidden_b,
    second_a,
    second_b,
    cot_ref,
    own_ref,
    sent_ref,
    gate_ref,
    route_ref,
    att_ref,
    router_ref,
    w_ref,
    gain_ref,
    grad_hidden_ref,
    branch_ref,
    grad_att_ref,
    aug_ref,
    gate_out_ref,
    router_grad_ref,
    gain_grad_ref,
    *,
    experts,
):
    @pl.when(pl.program_id(0) == 0)
    def _():
        router_grad_ref[...] = jnp.zeros_like(router_grad_ref)
        gain_grad_ref[...] = jnp.zeros_like(gain_grad_ref)

    early = pl.program_id(0) < pl.num_programs(0) // 2
    hidden = jnp.where(early, hidden_a[...], hidden_b[...])
    second = jnp.where(early, second_a[...], second_b[...])
    cot = cot_ref[...].astype(F32)
    scale = lax.rsqrt(jnp.mean(hidden * hidden, axis=1, keepdims=True) + EPSILON)
    probs, chosen, gate = routed_gate(second, router_ref[...], route_ref[...], experts)
    inner = gate_ref[...]
    gate_out_ref[...] = jnp.broadcast_to(gate, gate_out_ref.shape)
    grad_logits = (probs * (jnp.where(chosen, inner, 0.0) - gate * inner)).astype(BF16)
    router_grad_ref[...] += dot(grad_logits.astype(F32).T.astype(BF16), second)
    grad_second = own_ref[...].astype(F32) + sent_ref[...].astype(F32)
    grad_second = grad_second + dot(grad_logits, router_ref[...], NT)
    scaled_hidden = hidden * scale
    gain_grad_ref[...] += jnp.sum(grad_second * scaled_hidden, axis=0, keepdims=True)
    scaled = grad_second * gain_ref[...]
    mean = jnp.mean(scaled * scaled_hidden, axis=1, keepdims=True)
    grad_hidden = cot + scale * (scaled - scaled_hidden * mean)
    branch = grad_hidden.astype(BF16)
    grad_hidden_ref[...] = grad_hidden
    branch_ref[...] = branch
    grad_att = dot(branch, w_ref[...], NT).astype(BF16)
    grad_att_ref[...] = grad_att
    product = grad_att.astype(F32) * att_ref[...].astype(F32)
    rows, width = product.shape
    feature = lax.broadcasted_iota(jnp.int32, (width, LANES), 0)
    lane = lax.broadcasted_iota(jnp.int32, (width, LANES), 1)
    head = (lane & 15) == feature // 64
    collect = jnp.where(head & (lane < 48), 1.0, 0.0).astype(BF16)
    high = product.astype(BF16)
    rest = product - high.astype(F32)
    middle = rest.astype(BF16)
    low = (rest - middle.astype(F32)).astype(BF16)
    inner = dot(high, collect) + dot(middle, collect) + dot(low, collect)
    row_lane = lax.broadcasted_iota(jnp.int32, (rows, LANES), 1)
    aug_ref[...] = jnp.where(row_lane < 48, lane_parts(inner, row_lane), 0.0).astype(BF16)


def hidden_back(hidden, second, cot, own, sent, inner, route, att, router, weights, gain, experts, block=256):
    rows, width = cot.shape
    steps = rows // block
    half = steps // 2
    here = lambda i: (i, 0)
    wide = lambda index: pl.BlockSpec((block, width), index)
    low = wide(lambda i: (jnp.minimum(i, half - 1), 0))
    high = wide(lambda i: (jnp.maximum(i - half, 0), 0))
    return pl.pallas_call(
        functools.partial(hidden_back_kernel, experts=experts),
        grid=(steps,),
        in_specs=[
            low,
            high,
            low,
            high,
            wide(here),
            wide(here),
            wide(here),
            pl.BlockSpec((block, 1), here),
            pl.BlockSpec((block, 1), here),
            wide(here),
            whole_spec(router.shape),
            whole_spec(weights.shape),
            whole_spec((1, width)),
        ],
        out_specs=[
            wide(here),
            wide(here),
            wide(here),
            pl.BlockSpec((block, LANES), here),
            pl.BlockSpec((block, LANES), here),
            whole_spec((LANES, width)),
            whole_spec((1, width)),
        ],
        out_shape=[
            jax.ShapeDtypeStruct((rows, width), F32),
            jax.ShapeDtypeStruct((rows, width), BF16),
            jax.ShapeDtypeStruct((rows, width), BF16),
            jax.ShapeDtypeStruct((rows, LANES), BF16),
            jax.ShapeDtypeStruct((rows, LANES), F32),
            jax.ShapeDtypeStruct((LANES, width), F32),
            jax.ShapeDtypeStruct((1, width), F32),
        ],
        compiler_params=params(),
        cost_estimate=lasting(12),
        name="hidden_back",
    )(*hidden, *second, cot, own, sent, inner, route, att, router, weights, gain)


def token_back_kernel(tok_ref, grad_ref, gain_ref, *refs):
    weights, triples = refs[:GATHERS], refs[GATHERS:-2]
    out_ref, gain_grad_ref = refs[-2:]

    @pl.when(pl.program_id(0) == 0)
    def _():
        gain_grad_ref[...] = jnp.zeros_like(gain_grad_ref)

    rows = tok_ref[...].astype(F32)
    scale = lax.rsqrt(jnp.mean(rows * rows, axis=1, keepdims=True) + EPSILON)
    grads = jnp.concatenate([t[p] for p in range(3) for t in triples], axis=1)
    grad_normed, start = jnp.zeros(rows.shape, F32), 0
    for weight in weights:
        stop = min(start + weight.shape[1], grads.shape[1])
        grad_normed += dot(grads[:, start:stop], weight[:, : stop - start], NT)
        start = stop
    scaled_rows = rows * scale
    gain_grad_ref[...] += jnp.sum(grad_normed * scaled_rows, axis=0, keepdims=True)
    scaled = grad_normed * gain_ref[...]
    mean = jnp.mean(scaled * scaled_rows, axis=1, keepdims=True)
    out_ref[...] = (grad_ref[...] + scale * (scaled - scaled_rows * mean)).astype(BF16)


def token_back(tokens, grad_hidden, grad_triples, weights, gain_row, block=256):
    rows, width = tokens.shape
    here = lambda i: (i, 0)
    return pl.pallas_call(
        token_back_kernel,
        grid=(rows // block,),
        in_specs=[
            pl.BlockSpec((block, width), here),
            pl.BlockSpec((block, width), here),
            whole_spec((1, width)),
        ]
        + [whole_spec(w.shape) for w in weights]
        + [pl.BlockSpec((3, block, t.shape[2]), lambda i: (0, i, 0)) for t in grad_triples],
        out_specs=[pl.BlockSpec((block, width), here), whole_spec((1, width))],
        out_shape=[
            jax.ShapeDtypeStruct((rows, width), BF16),
            jax.ShapeDtypeStruct((1, width), F32),
        ],
        compiler_params=params(),
        cost_estimate=lasting(9),
        name="token_back",
    )(tokens, grad_hidden, gain_row, *weights, *grad_triples)


def swap(value, axis, step=1):
    size = lax.axis_size(axis)
    return lax.ppermute(value, axis, [(i, i ^ step) for i in range(size)])


def bit_of(axis, step):
    return lax.axis_index(axis) // step % 2


def bits(size, first=1):
    return [1 << n for n in range(first.bit_length() - 1, size.bit_length() - 1)]


def rounded(parts):
    return sum(part.astype(F32) for part in parts).astype(BF16)


def exchange(parts, axis, step, pick):
    bit = bit_of(axis, step)
    give = rounded([pick(part, 1 - bit) for part in parts])
    return [pick(part, bit) for part in parts] + [swap(give, axis, step)]


def halve(parts, axis, step):
    def pick(part, bit):
        parted = part.reshape((part.shape[0], 2, part.shape[1] // 2) + part.shape[2:])
        return lax.dynamic_index_in_dim(parted, bit, 1, keepdims=False)

    return exchange(parts, axis, step, pick)


def to_owner(parts, steps):
    def pick(part, bit):
        parted = part.reshape((part.shape[0] // 2, 2) + part.shape[1:])
        return lax.dynamic_index_in_dim(parted, bit, 1, keepdims=False)

    for step in steps:
        parts = exchange(parts, "shard", step, pick)
    return parts


def to_owner_early(parts):
    return to_owner(parts, bits(lax.axis_size("shard"))[:-1])


def to_owner_last(parts):
    return to_owner(parts, bits(lax.axis_size("shard"))[-1:])


def both(parts, axis, step):
    mine = rounded(parts)
    return [mine, swap(mine, axis, step)]


def unhalve(value, axis, step, dim):
    other = swap(value, axis, step)
    first = bit_of(axis, step) == 0
    low = jnp.where(first, value, other)
    high = jnp.where(first, other, value)
    return jnp.concatenate([low, high], axis=dim)


def neighbours(parts):
    return halve(parts, "dp", 1) if lax.axis_size("dp") > 1 else parts


def spread(parts):
    for step in bits(lax.axis_size("dp"), 2):
        parts = halve(parts, "dp", step)
    return parts


def unspread(value):
    for step in reversed(bits(lax.axis_size("dp"), 2)):
        value = unhalve(value, "dp", step, 0)
    return value


def summed(parts):
    for step in bits(lax.axis_size("dp"), 2):
        parts = both(parts, "dp", step)
    return parts


def finish_expert(early, late, local):
    early, late = rounded(early)[0], rounded(late)[0]
    whole = jnp.concatenate([unspread(early), rounded(summed([late]))], axis=0)
    if lax.axis_size("dp") > 1:
        whole = unhalve(whole, "dp", 1, 0)
    return whole.reshape((local, -1) + whole.shape[1:]).astype(F32)


def tie(value, *sums):
    value, *last = lax.optimization_barrier((value,) + tuple(parts[-1] for parts in sums))
    return (value, *(parts[:-1] + [part] for parts, part in zip(sums, last)))


def dense_near(partial_sum):
    shards = lax.axis_size("shard")
    width, columns = partial_sum.shape
    return neighbours([partial_sum.reshape(shards, width // shards, columns)])


def dense_across(parts):
    return halve(parts, "expert", 1) if lax.axis_size("expert") > 1 else parts


def dense_finish(parts):
    parts = [rounded(to_owner_last(to_owner_early(parts)))[0]]
    for axis in ("expert", "dp"):
        for step in bits(lax.axis_size(axis), 2):
            parts = both(parts, axis, step)
    value = rounded(parts)
    for axis in ("expert", "dp"):
        if lax.axis_size(axis) > 1:
            value = unhalve(value, axis, 1, 0)
    return value.astype(F32)


def gather_rows(value):
    shards, parts = lax.axis_size("shard"), lax.axis_size("dp")
    rows, columns = value.shape
    parted = value.reshape(parts, rows // parts, columns)
    mine = lax.dynamic_index_in_dim(parted, lax.axis_index("dp"), 0, keepdims=False)
    me = lax.axis_index("shard")
    whole = lax.dynamic_update_index_in_dim(
        jnp.zeros((shards,) + mine.shape, value.dtype), mine, me, 0
    )
    for away in range(1, shards):
        piece = lax.ppermute(mine, "shard", [(i, (i + away) % shards) for i in range(shards)])
        whole = lax.dynamic_update_index_in_dim(whole, piece, (me - away) % shards, 0)
    whole = whole[:, None]
    for step in reversed(bits(parts)):
        other = swap(whole, "dp", step)
        first = bit_of("dp", step) == 0
        low, high = jnp.where(first, whole, other), jnp.where(first, other, whole)
        whole = jnp.stack([low, high], axis=2)
        whole = whole.reshape((shards, -1) + mine.shape)
    return whole.reshape(shards * rows, columns)


def places_of(route_ids, first, local, capacity):
    owned = route_ids - first
    choose = owned[:, None] == jnp.arange(local, dtype=jnp.int32)[None, :]
    rank = jnp.cumsum(choose.astype(jnp.int32), axis=0) - 1
    slot = jnp.sum(jnp.where(choose, rank, 0), axis=1) + owned * capacity
    full = (rank[-1] >= capacity // 2).astype(jnp.int32)
    return jnp.where(jnp.any(choose, axis=1), slot, -1), full


def experts_of_pairs(second, cotangent, routes, router, expert_in, expert_out, early):
    rows, width = cotangent.shape
    local, _, ff = expert_in.shape
    experts = router.shape[1]
    router = jnp.pad(router, ((0, 0), (0, LANES - experts)))
    capacity = 2 * rows // experts
    ff_block = ff // lax.axis_size("shard")
    other_cot, other_routes = early
    other_second = [swap(part, "expert") for part in second]
    first_own = lax.axis_index("expert") * local
    results, flags = [], []
    for rows_of, cot, route_ids in (
        (second, cotangent, routes[:, 0]),
        (other_second, other_cot, other_routes),
    ):
        place, full = places_of(route_ids, first_own, local, capacity)
        results.append(
            expert_rows(
                full[None],
                rows_of,
                cot,
                route_ids[:, None],
                router,
                place,
                expert_in,
                expert_out,
                capacity,
                experts,
                ff_block,
            )
        )
        flags.append(full)
    own, other = results
    full = jnp.stack(flags)
    back = [swap(part, "expert") for part in jnp.split(other[5], 2, axis=0)]
    inner = own[6][:, 0] + swap(other[6][:, 0], "expert")
    keep = bit_of("dp", 1)
    one = lambda expert: expert[None].astype(jnp.int32)
    grad = lambda expert, left, right: weight_grad(
        full, one(expert), left, right, capacity, ff_block
    )
    acts, grads = (own[0], other[0]), (own[3], other[3])
    xs, grad_pres = (own[2], other[2]), (own[1], other[1])
    out_give = grad(1 - keep, acts, grads)
    out_sent = swap(out_give, "dp")
    full, _ = lax.optimization_barrier((full, out_give))
    out_keep = grad(keep, acts, grads)
    full, _, back[0] = lax.optimization_barrier((full, out_keep, back[0]))
    in_give = grad(1 - keep, xs, grad_pres)
    in_sent = swap(in_give, "dp")
    full, _, out_sent = lax.optimization_barrier((full, in_give, out_sent))
    in_keep = grad(keep, xs, grad_pres)
    inner, _ = lax.optimization_barrier((inner, in_keep))
    returned = (own[4], swap(other[4], "expert"))
    back = jnp.concatenate(back, axis=0)
    return returned, (own[5], back), inner[:, None], [in_keep, in_sent], [out_keep, out_sent]


def experts_of_many(second, cotangent, routes, router, expert_in, expert_out):
    second = jnp.concatenate(second, axis=0)
    tok_rows, width = second.shape
    experts_all = router.shape[1]
    local, _, ff = expert_in.shape
    groups = lax.axis_size("expert")
    shards = lax.axis_size("shard")
    capacity = 2 * tok_rows // experts_all
    route_ids = routes[:, 0]
    choose = route_ids[:, None] == jnp.arange(experts_all, dtype=jnp.int32)[None, :]
    rank = jnp.cumsum(choose.astype(jnp.int32), axis=0) - 1
    slot_index = route_ids * capacity + jnp.sum(jnp.where(choose, rank, 0), axis=1)
    probs = jax.nn.softmax(dot(second, router), axis=-1)
    gate = jnp.sum(jnp.where(choose, probs, 0.0), axis=1)

    def across(value):
        return lax.all_to_all(value, "expert", split_axis=0, concat_axis=0, tiled=True)

    def to_slots(token_rows):
        filled = jnp.zeros((experts_all * capacity, width), token_rows.dtype)
        filled = filled.at[slot_index].set(token_rows)
        return across(filled.reshape(groups, local, capacity, width))

    def from_slots(value):
        return across(value).reshape(experts_all * capacity, width)[slot_index]

    def einsum(form, left, right):
        return jnp.einsum(form, left, right, preferred_element_type=F32)

    def gelu(value):
        return jax.nn.gelu(value, approximate=True)

    grad_out = cotangent.astype(F32)
    arrived = to_slots(second)
    pre_act, pull = jax.vjp(gelu, einsum("aecd,edf->aecf", arrived, expert_in))
    activated = pre_act.astype(BF16)
    produced = einsum("aecf,efd->aecd", activated, expert_out).astype(BF16)
    returned = from_slots(produced)
    inner = jnp.sum(grad_out * returned.astype(F32), axis=1)
    grad_arrived = to_slots((gate[:, None] * grad_out).astype(BF16))
    grad_act = einsum("aecd,efd->aecf", grad_arrived, expert_out)
    grad_pre = pull(grad_act)[0].astype(BF16)
    grad_w_out = einsum("aecf,aecd->efd", activated, grad_arrived).astype(BF16)
    grad_w_in = einsum("aecd,aecf->edf", arrived, grad_pre).astype(BF16)
    back = from_slots(einsum("aecf,edf->aecd", grad_pre, expert_in).astype(BF16))
    grad_w_in = grad_w_in.reshape(local, width, shards, ff // shards).transpose(2, 0, 1, 3)
    grad_w_out = grad_w_out.reshape(local, shards, ff // shards, width).transpose(1, 0, 2, 3)
    near = lambda value: neighbours([value.reshape((shards, -1) + value.shape[3:])])
    nothing = jnp.zeros_like(back)
    return (
        (returned, nothing),
        (back, nothing),
        inner[:, None],
        near(grad_w_in),
        near(grad_w_out),
    )


def body(
    tokens,
    segments,
    routes,
    cotangent,
    attn_in,
    attn_out,
    router,
    gain_one,
    gain_two,
    expert_in,
    expert_out,
):
    rows, width = tokens.shape
    experts = router.shape[1]
    local = expert_in.shape[0]
    chunk_rows = rows // CHUNKS
    lanes_of = lambda value: jnp.pad(value[:, None], ((0, 0), (0, LANES - 1)))
    padded = lambda value: jnp.pad(value, ((0, 0), (0, LANES - experts)))
    segment_col = segments[0][:, None]
    pairs_only = lax.axis_size("expert") == local == 2 and lax.axis_size("dp") > 1
    early = None

    span = 3 * width // GATHERS
    pieces = [attn_in[:, g * span : (g + 1) * span] for g in range(GATHERS)]
    pieces[-1] = jnp.concatenate([pieces[-1], lanes_of(gain_one)], axis=1)
    weights = [gather_rows(piece) for piece in pieces]
    first_gain = weights[-1][:, span].astype(F32)[None, :]
    if pairs_only:
        early = (swap(cotangent, "expert"), swap(routes[:, 0], "expert"))
    out_full = gather_rows(
        jnp.concatenate([attn_out, padded(router), lanes_of(gain_two)], axis=1)
    )
    full_out = out_full[:, :width]
    full_router = out_full[:, width : width + experts]
    lane_router = out_full[:, width : width + LANES]
    second_gain = out_full[:, width + LANES].astype(F32)[None, :]

    normed, triple = qkv(tokens, first_gain, weights)
    attended, qaug, hidden, second = [], [], [], []
    for chunk in range(CHUNKS):
        att, aug = attend_forward(triple, segment_col, chunk, chunk_rows)
        hid, sec = project(tokens, att, full_out, second_gain, chunk)
        attended.append(att)
        qaug.append(aug)
        hidden.append(hid)
        second.append(sec)
    if pairs_only:
        done = experts_of_pairs(
            second, cotangent, routes, full_router, expert_in, expert_out, early
        )
    else:
        done = experts_of_many(second, cotangent, routes, full_router, expert_in, expert_out)
    returned, backs, inner, in_near, out_near = done

    cut = out_near[0].shape[1] // 3 * 2
    first_part = lambda parts: [part[:, :cut] for part in parts]
    last_part = lambda parts: [part[:, cut:] for part in parts]
    attended_all = jnp.concatenate(attended, axis=0)
    inner, out_near = tie(inner, out_near)
    out_early = spread(first_part(out_near))
    out_late = to_owner_early(last_part(out_near))
    grad_hidden, branch, grad_att, gaug, gates, grad_router, grad_gain_two = hidden_back(
        hidden,
        second,
        cotangent,
        *backs,
        inner,
        routes,
        attended_all,
        lane_router,
        full_out,
        second_gain,
        experts,
    )
    qaug_all = jnp.concatenate(qaug, axis=0)
    heads = width // 64 // GROUPS
    back = lambda grad, g: attend_backward(
        triple, grad, segment_col, qaug_all, gaug, g * heads, heads
    )
    weigh = lambda grads: jnp.einsum(
        "td,pte->dpe", normed, grads, preferred_element_type=F32
    ).reshape(width, -1).astype(BF16)

    grad_att, in_near = tie(grad_att, in_near)
    in_late = to_owner_early(last_part(in_near))
    grads_0 = back(grad_att, 0)
    grad_attn_out = jnp.einsum("td,te->de", attended_all, branch, preferred_element_type=F32)
    dense_a = [
        grad_attn_out.astype(BF16),
        padded(grad_router[:experts].T.astype(BF16)),
        lanes_of(grad_gain_two[0].astype(BF16)),
        weigh(grads_0),
    ]
    dense_a = dense_near(jnp.concatenate(dense_a, axis=1))

    grad_att, out_late, (grads_0,) = tie(grad_att, out_late, [grads_0])
    out_late = to_owner_last(out_late)
    grads_1 = back(grad_att, 1)

    grad_att, out_early, dense_a, (grads_1,) = tie(grad_att, out_early, dense_a, [grads_1])
    out_early = to_owner_early(out_early)
    in_early = spread(first_part(in_near))
    dense_a = dense_across(dense_a)
    grads_2 = back(grad_att, 2)

    grad_hidden, out_early, out_late, in_late, dense_a, (grads_2,) = tie(
        grad_hidden, out_early, out_late, in_late, dense_a, [grads_2]
    )
    out_early = to_owner_last(out_early)
    in_late = to_owner_last(in_late)
    grad_tokens, grad_gain_one = token_back(
        tokens, grad_hidden, (grads_0, grads_1, grads_2), weights, first_gain
    )
    dense_b = [weigh(grads_1), weigh(grads_2), lanes_of(grad_gain_one[0].astype(BF16))]
    dense_b = dense_near(jnp.concatenate(dense_b, axis=1))
    dense_a = dense_finish(dense_a)
    dense_b = dense_finish(dense_across(dense_b))
    final_out = finish_expert(out_early, out_late, local)
    in_early = to_owner_last(to_owner_early(in_early))
    final_in = finish_expert(in_early, in_late, local)

    part = width // GROUPS
    start = width + 2 * LANES
    by_group = [dense_a[:, start:], dense_b[:, : 3 * part], dense_b[:, 3 * part : 6 * part]]
    grad_attn_in = jnp.concatenate(
        [value[:, p * part : (p + 1) * part] for p in range(3) for value in by_group], axis=1
    )

    wide = returned[0].astype(F32) + returned[1].astype(F32)
    layer = jnp.concatenate(hidden, axis=0) + gates[:, :1] * wide
    return (
        layer.astype(BF16),
        grad_tokens,
        grad_attn_in,
        dense_a[:, :width],
        dense_a[:, width : width + experts],
        dense_b[:, 6 * part],
        dense_a[:, width + LANES],
        final_in,
        final_out,
    )


def solution(mesh):
    everywhere = P(("dp", "expert", "shard"), None)
    placed = (everywhere,) * 4 + (P("shard", None),) * 3 + (P("shard"),) * 2
    placed = placed + (P("expert", None, None),) * 2
    outs = (everywhere,) * 2 + (P("shard", None),) * 3 + (P("shard"),) * 2
    outs = outs + (P("expert", None, "shard"), P("expert", "shard", None))
    return jax.shard_map(
        body, mesh=mesh, in_specs=placed, out_specs=outs, check_vma=False
    )
```

```python
import functools
import math

import jax
import jax.numpy as jnp
from jax import lax
from jax.experimental import pallas as pl
from jax.experimental.pallas import tpu as pltpu
from jax.sharding import PartitionSpec as P

HEADS = 12
LANES = 128
EPSILON = 1e-06
MASKED = -1e30
BF16 = jnp.bfloat16
F32 = jnp.float32
NN = (((1,), (0,)), ((), ()))
NT = (((1,), (1,)), ((), ()))
TN = (((0,), (0,)), ((), ()))
GROUPS = 3
GATHERS = 2
SHARE = 0.05
GELU_C = math.sqrt(2.0 / math.pi)
GELU_A = 0.044715


def dot(left, right, dims=NN):
    return lax.dot_general(left, right, dims, preferred_element_type=F32)


def column_of(row):
    wide = jnp.broadcast_to(row.astype(F32), (LANES, row.shape[1]))
    return wide.T.astype(jnp.int32)


def params(mebibytes=60):
    return pltpu.CompilerParams(vmem_limit_bytes=mebibytes << 20)


def lasting(microseconds):
    return pl.CostEstimate(
        flops=int(microseconds * SHARE * 1.15e9), bytes_accessed=0, transcendentals=0
    )


def whole_spec(shape, buffers=1):
    return pl.BlockSpec(
        shape, lambda *_: (0,) * len(shape), pipeline_mode=pl.Buffered(buffers)
    )


def lane_parts(value, lane):
    high = value.astype(BF16).astype(F32)
    middle = (value - high).astype(BF16).astype(F32)
    low = value - high - middle
    return jnp.where(lane < 16, high, jnp.where(lane < 32, middle, low))


def attend_kernel(q_ref, k_ref, v_ref, seg_ref, out_ref, qaug_ref, lse_ref, *, block):
    pair, pairs = pl.program_id(0), pl.num_programs(0)
    rows, keys = q_ref.shape[0], k_ref.shape[0]
    lane_k = lax.broadcasted_iota(jnp.int32, (keys, LANES), 1)
    lane_q = lax.broadcasted_iota(jnp.int32, (rows, LANES), 1)
    k_mark = jnp.where((lane_k - 48) == seg_ref[...], 1.0, 0.0).astype(BF16)
    zone = (lane_q >= 48) & (lane_q < 56)
    q_mark = jnp.where(zone & ((lane_q - 48) != seg_ref[...]), MASKED, 0.0)

    @pl.when(pair == 0)
    def _():
        lse_ref[...] = jnp.zeros_like(lse_ref)

    k_mark = jnp.where((lane_k >= 48) & (lane_k < 56), k_mark, jnp.asarray(0, BF16))
    k_wide = jnp.concatenate([k_ref[...], k_mark], axis=1)
    v_wide = jnp.concatenate([v_ref[...], jnp.ones((keys, LANES), BF16)], axis=1)
    lane = lane_q[:block]
    for start in range(0, rows, block):
        part = slice(start, start + block)
        query = q_ref[part] * jnp.asarray(0.125, BF16)
        outs = []
        stats = lse_ref[part]
        for side in range(2):
            own = (lane >= 64) if side else (lane < 64)
            picked = jnp.where(own, query, jnp.asarray(0, BF16))
            scores = dot(
                jnp.concatenate([picked, q_mark[part].astype(BF16)], axis=1), k_wide, NT
            )
            row_max = jnp.max(scores, axis=1, keepdims=True)
            raised = jnp.exp(scores - row_max).astype(BF16)
            summed = dot(raised, v_wide)
            total = summed[:, LANES:]
            outs.append(summed[:, :LANES] / total)
            mine = ((lane & 15) == 2 * pair + side) & (lane < 48)
            stats = jnp.where(mine, row_max + jnp.log(total), stats)
        out_ref[part] = jnp.where(lane < 64, outs[0], outs[1]).astype(BF16)
        lse_ref[part] = stats

    @pl.when(pair == pairs - 1)
    def _():
        stats = lane_parts(lse_ref[...], lane_q)
        qaug_ref[...] = jnp.where(lane_q < 48, stats, q_mark).astype(BF16)


def attend_forward(triple, segment_col, block=256):
    rows, width = triple.shape[0], triple.shape[1] // 3
    pairs = width // LANES
    return pl.pallas_call(
        functools.partial(attend_kernel, block=block),
        grid=(pairs,),
        in_specs=[
            pl.BlockSpec((rows, LANES), lambda p: (0, p)),
            pl.BlockSpec((rows, LANES), lambda p: (0, pairs + p)),
            pl.BlockSpec((rows, LANES), lambda p: (0, 2 * pairs + p)),
            whole_spec((rows, 1)),
        ],
        out_specs=[
            pl.BlockSpec((rows, LANES), lambda p: (0, p)),
            pl.BlockSpec((rows, LANES), lambda p: (0, 0)),
        ],
        out_shape=[
            jax.ShapeDtypeStruct((rows, width), BF16),
            jax.ShapeDtypeStruct((rows, LANES), BF16),
        ],
        scratch_shapes=[pltpu.VMEM((rows, LANES), F32)],
        compiler_params=params(),
        cost_estimate=lasting(24),
        name="attend_forward",
    )(triple, triple, triple, segment_col)


def keep_and_give(bit, result, keep_ref, give_ref):
    shards, half = keep_ref.shape[0], keep_ref.shape[1]
    result = result.astype(BF16)
    for shard in range(shards):
        low = result[2 * half * shard : 2 * half * shard + half]
        high = result[2 * half * shard + half : 2 * half * shard + 2 * half]
        keep_ref[shard] = jnp.where(bit == 0, low, high)
        give_ref[shard] = jnp.where(bit == 0, high, low)


def attend_back_kernel(
    bit_ref,
    q_ref,
    k_ref,
    v_ref,
    g_ref,
    seg_ref,
    qaug_ref,
    gaug_ref,
    normed_ref,
    out_ref,
    keep_ref,
    give_ref,
    *,
    block,
    first_head,
):
    pair = pl.program_id(0)
    rows = q_ref.shape[0]
    lane = lax.broadcasted_iota(jnp.int32, (block, LANES), 1)
    zero = jnp.asarray(0, BF16)
    query = q_ref[...] * jnp.asarray(0.125, BF16)
    grad = g_ref[...]
    q_wide = jnp.concatenate([query, qaug_ref[...]], axis=1)
    g_wide = jnp.concatenate([grad, gaug_ref[...]], axis=1)
    zone = (lane >= 48) & (lane < 56)
    grad_q = [jnp.zeros((64, rows), F32), jnp.zeros((64, rows), F32)]
    for start in range(0, rows, block):
        part = slice(start, start + block)
        key, value = k_ref[part], v_ref[part]
        key_turned = key.T
        doc = zone & ((lane - 48) == seg_ref[part])
        grads_k, grads_v = [], []
        for side in range(2):
            own = (lane >= 64) if side else (lane < 64)
            stat = ((lane & 15) == first_head + 2 * pair + side) & (lane < 48)
            k_mark = jnp.where(stat, -1.0, jnp.where(doc, 1.0, 0.0)).astype(BF16)
            v_mark = jnp.where(stat, -1.0, 0.0).astype(BF16)
            k_wide = jnp.concatenate([jnp.where(own, key, zero), k_mark], axis=1)
            v_wide = jnp.concatenate([jnp.where(own, value, zero), v_mark], axis=1)
            probs = jnp.exp(dot(k_wide, q_wide, NT))
            grad_scores = (probs * dot(v_wide, g_wide, NT)).astype(BF16)
            grads_v.append(dot(probs.astype(BF16), grad))
            grads_k.append(dot(grad_scores, query))
            grad_q[side] = grad_q[side] + dot(
                key_turned[64 * side : 64 * side + 64], grad_scores
            )
        out_ref[1, part] = jnp.where(lane < 64, grads_k[0], grads_k[1]).astype(BF16)
        out_ref[2, part] = jnp.where(lane < 64, grads_v[0], grads_v[1]).astype(BF16)
    out_ref[0] = (jnp.concatenate(grad_q, axis=0) * 0.125).T.astype(BF16)
    grads = jnp.concatenate([out_ref[0], out_ref[1], out_ref[2]], axis=1)
    keep_and_give(bit_ref[0], dot(normed_ref[...], grads, TN), keep_ref, give_ref)


def attend_backward(bit, triple, grad, segment_col, qaug, gaug, normed, shards, first_head, heads, block=512):
    rows, width = normed.shape
    pairs, first, half = width // LANES, first_head // 2, width // shards // 2
    pair_of = lambda offset: pl.BlockSpec((rows, LANES), lambda p, _: (0, offset + p))
    weight_half = pl.BlockSpec((shards, half, 3 * LANES), lambda p, _: (0, 0, p))
    return pl.pallas_call(
        functools.partial(attend_back_kernel, block=block, first_head=first_head),
        grid_spec=pltpu.PrefetchScalarGridSpec(
            num_scalar_prefetch=1,
            grid=(heads // 2,),
            in_specs=[
                pair_of(first),
                pair_of(pairs + first),
                pair_of(2 * pairs + first),
                pair_of(first),
                whole_spec((rows, 1)),
                whole_spec((rows, LANES)),
                whole_spec((rows, LANES)),
                whole_spec((rows, width)),
            ],
            out_specs=[
                pl.BlockSpec((3, rows, LANES), lambda p, _: (0, 0, p)),
                weight_half,
                weight_half,
            ],
        ),
        out_shape=[
            jax.ShapeDtypeStruct((3, rows, heads * 64), BF16),
            jax.ShapeDtypeStruct((shards, half, heads // 2 * 3 * LANES), BF16),
            jax.ShapeDtypeStruct((shards, half, heads // 2 * 3 * LANES), BF16),
        ],
        compiler_params=params(),
        cost_estimate=lasting(14),
        name="attend_backward",
    )(bit, triple, triple, triple, grad, segment_col, qaug, gaug, normed)


def qkv_kernel(tok_ref, gain_ref, *refs):
    weights, (normed_ref, triple_ref) = refs[:-2], refs[-2:]
    rows = tok_ref[...].astype(F32)
    scale = lax.rsqrt(jnp.mean(rows * rows, axis=1, keepdims=True) + EPSILON)
    normed = (rows * scale * gain_ref[...]).astype(BF16)
    normed_ref[...] = normed
    span = triple_ref.shape[1] // len(weights)
    for at, weight in enumerate(weights):
        triple_ref[:, at * span : (at + 1) * span] = dot(normed, weight[...]).astype(BF16)


def qkv(tokens, gain_row, weights, span, block=256):
    rows, width = tokens.shape
    return pl.pallas_call(
        qkv_kernel,
        grid=(rows // block,),
        in_specs=[pl.BlockSpec((block, width), lambda i: (i, 0)), whole_spec((1, width))]
        + [whole_spec((width, span)) for weight in weights],
        out_specs=[
            pl.BlockSpec((block, width), lambda i: (i, 0)),
            pl.BlockSpec((block, 3 * width), lambda i: (i, 0)),
        ],
        out_shape=[
            jax.ShapeDtypeStruct((rows, width), BF16),
            jax.ShapeDtypeStruct((rows, 3 * width), BF16),
        ],
        compiler_params=params(),
        cost_estimate=lasting(8),
        name="qkv",
    )(tokens, gain_row, *weights)


def project_kernel(tok_ref, att_ref, w_ref, gain_ref, hidden_ref, second_ref):
    hidden = tok_ref[...].astype(F32) + dot(att_ref[...], w_ref[...])
    scale = lax.rsqrt(jnp.mean(hidden * hidden, axis=1, keepdims=True) + EPSILON)
    hidden_ref[...] = hidden
    second_ref[...] = (hidden * scale * gain_ref[...]).astype(BF16)


def project(tokens, attended, out_full, gain_row, block=256):
    rows, width = tokens.shape
    wide = pl.BlockSpec((block, width), lambda i: (i, 0))
    return pl.pallas_call(
        project_kernel,
        grid=(rows // block,),
        in_specs=[wide, wide, whole_spec((width, width)), whole_spec((1, width))],
        out_specs=[wide, wide],
        out_shape=[
            jax.ShapeDtypeStruct((rows, width), F32),
            jax.ShapeDtypeStruct((rows, width), BF16),
        ],
        compiler_params=params(),
        cost_estimate=lasting(7),
        name="project",
    )(tokens, attended, out_full, gain_row)


def routed_gate(second, router, route_wide, experts):
    logits = dot(second, router)
    lane = lax.broadcasted_iota(jnp.int32, logits.shape, 1)
    logits = jnp.where(lane < experts, logits, MASKED)
    raised = jnp.exp(logits - jnp.max(logits, axis=1, keepdims=True))
    probs = raised / jnp.sum(raised, axis=1, keepdims=True)
    chosen = lane == route_wide
    gate = jnp.sum(jnp.where(chosen, probs, 0.0), axis=1, keepdims=True)
    return probs, chosen, gate


def on_rows(full, run, capacity):
    pl.when(full == 1)(functools.partial(run, capacity))
    pl.when(full == 0)(functools.partial(run, capacity // 2))


def expert_kernel(
    full_ref,
    rows_ref,
    cot_ref,
    route_ref,
    router_ref,
    place_ref,
    w_in_ref,
    w_out_ref,
    act_ref,
    grad_pre_ref,
    x_ref,
    g_ref,
    ret_ref,
    back_a,
    back_b,
    gate_ref,
    produced,
    grad_rows,
    *,
    experts,
):
    ff, expert = pl.program_id(0), pl.program_id(1)
    slots = x_ref.shape[0]
    capacity = slots // full_ref.shape[1]
    half = capacity // 2

    @pl.when((ff == 0) & (expert == 0))
    def _():
        produced[...] = jnp.zeros_like(produced)
        grad_rows[...] = jnp.zeros_like(grad_rows)
        second = rows_ref[...]
        _, _, gate = routed_gate(second, router_ref[...], column_of(route_ref[...]), experts)
        gated = (gate * cot_ref[...].astype(F32)).astype(BF16)

        def pack(start):
            part = slice(start, start + half)
            slot = start + lax.broadcasted_iota(jnp.int32, (half, second.shape[0]), 0)
            pick = jnp.where(slot == place_ref[...], 1.0, 0.0).astype(BF16)
            x_ref[part, :] = dot(pick, second).astype(BF16)
            g_ref[part, :] = dot(pick, gated).astype(BF16)

        for owner in range(slots // capacity):
            pack(owner * capacity)
            pl.when(full_ref[0, owner] == 1)(
                functools.partial(pack, owner * capacity + half)
            )

    def run(rows):
        part = pl.ds(pl.multiple_of(expert * capacity, capacity), rows)
        pre = dot(x_ref[part, :], w_in_ref[0])
        grad_act = dot(g_ref[part, :], w_out_ref[0], NT)
        square = pre * pre
        bend = jnp.tanh(pre * (GELU_C + GELU_C * GELU_A * square))
        upper = 0.5 + 0.5 * bend
        act = (pre * upper).astype(BF16)
        inner = pre * (GELU_C + 3.0 * GELU_C * GELU_A * square)
        slope = upper + inner * (0.5 - 0.5 * bend * bend)
        grad_pre = (grad_act * slope).astype(BF16)
        act_ref[part, :] = act
        grad_pre_ref[part, :] = grad_pre
        produced[part, :] += dot(act, w_out_ref[0])
        grad_rows[part, :] += dot(grad_pre, w_in_ref[0], NT)

    on_rows(full_ref[0, expert], run, capacity)

    @pl.when((ff == pl.num_programs(0) - 1) & (expert == pl.num_programs(1) - 1))
    def _():
        count = ret_ref.shape[0]
        slot = lax.broadcasted_iota(jnp.int32, (count, slots), 1)
        place_col = column_of(place_ref[...])[:, :1]
        pick = jnp.where(slot == place_col, 1.0, 0.0).astype(BF16)
        returned = dot(pick, produced[...].astype(BF16))
        ret_ref[...] = returned.astype(BF16)
        grads = grad_rows[...].astype(BF16)
        back_a[...] = dot(pick[: count // 2], grads).astype(BF16)
        back_b[...] = dot(pick[count // 2 :], grads).astype(BF16)
        inner = jnp.sum(cot_ref[...].astype(F32) * returned, axis=1, keepdims=True)
        gate_ref[...] = jnp.broadcast_to(inner, (count, LANES)).T[:8]


def expert_rows(full, rows, cot, route_row, router, place, w_in, w_out, capacity, experts, ff_block):
    count, width = cot.shape
    local, _, ff = w_in.shape
    slots = local * capacity
    column = lambda f, e, _: (0, f)
    return pl.pallas_call(
        functools.partial(expert_kernel, experts=experts),
        grid_spec=pltpu.PrefetchScalarGridSpec(
            num_scalar_prefetch=1,
            grid=(ff // ff_block, local),
            in_specs=[
                whole_spec((count, width)),
                whole_spec((count, width)),
                whole_spec((1, count)),
                pl.BlockSpec((width, LANES), lambda *_: (0, width // LANES)),
                whole_spec((1, count)),
                pl.BlockSpec((1, width, ff_block), lambda f, e, _: (e, 0, f)),
                pl.BlockSpec((1, ff_block, width), lambda f, e, _: (e, f, 0)),
            ],
            out_specs=[
                pl.BlockSpec((slots, ff_block), column),
                pl.BlockSpec((slots, ff_block), column),
                whole_spec((slots, width)),
                whole_spec((slots, width)),
                whole_spec((count, width)),
                whole_spec((count // 2, width)),
                whole_spec((count // 2, width)),
                whole_spec((8, count)),
            ],
            scratch_shapes=[
                pltpu.VMEM((slots, width), F32),
                pltpu.VMEM((slots, width), F32),
            ],
        ),
        out_shape=[
            jax.ShapeDtypeStruct((slots, ff), BF16),
            jax.ShapeDtypeStruct((slots, ff), BF16),
            jax.ShapeDtypeStruct((slots, width), BF16),
            jax.ShapeDtypeStruct((slots, width), BF16),
            jax.ShapeDtypeStruct((count, width), BF16),
            jax.ShapeDtypeStruct((count // 2, width), BF16),
            jax.ShapeDtypeStruct((count // 2, width), BF16),
            jax.ShapeDtypeStruct((8, count), F32),
        ],
        compiler_params=params(),
        cost_estimate=lasting(28),
        name="expert_rows",
    )(full, rows, cot, route_row, router, place[None, :], w_in, w_out)


def weight_grad_kernel(full_ref, expert_ref, left_a, left_b, right_a, right_b, early_ref, late_ref):
    expert = expert_ref[0]
    capacity = left_a.shape[0]

    def run(rows_a, rows_b):
        total = (
            dot(left_a[:rows_a, :], right_a[:rows_a, :], TN)
            + dot(left_b[:rows_b, :], right_b[:rows_b, :], TN)
        ).astype(BF16)
        early_ref[0] = total[: early_ref.shape[1]]
        late_ref[0] = total[early_ref.shape[1] :]

    for full_a in range(2):
        for full_b in range(2):
            pl.when((full_ref[0, expert] == full_a) & (full_ref[1, expert] == full_b))(
                functools.partial(
                    run, capacity // (2 - full_a), capacity // (2 - full_b)
                )
            )


def early_rows(rows):
    return rows // 3 * 2


def weight_grad(full, expert, left, right, capacity, ff_block):
    slots, width = left[0].shape
    ff = max(width, right[0].shape[1])
    spec = lambda value: (
        pl.BlockSpec((capacity, ff_block), lambda f, _, e: (e[0], f))
        if value.shape[1] == ff
        else pl.BlockSpec(
            (capacity, value.shape[1]), lambda f, _, e: (e[0], 0), pipeline_mode=pl.Buffered(1)
        )
    )
    block = lambda value: ff_block if value.shape[1] == ff else value.shape[1]
    shape = (block(left[0]), block(right[0]))
    counts = (early_rows(shape[0]), shape[0] - early_rows(shape[0]))
    return pl.pallas_call(
        weight_grad_kernel,
        grid_spec=pltpu.PrefetchScalarGridSpec(
            num_scalar_prefetch=2,
            grid=(ff // ff_block,),
            in_specs=[spec(value) for value in (*left, *right)],
            out_specs=[
                pl.BlockSpec((1, count, shape[1]), lambda f, *_: (f, 0, 0)) for count in counts
            ],
        ),
        out_shape=[
            jax.ShapeDtypeStruct((ff // ff_block, count, shape[1]), BF16) for count in counts
        ],
        compiler_params=params(),
        cost_estimate=lasting(9),
        name="weight_grad",
    )(full, expert, *left, *right)


def hidden_back_kernel(
    bit_ref,
    own_a,
    own_b,
    sent_a,
    sent_b,
    hidden_ref,
    second_ref,
    att_ref,
    cot_ref,
    own_gate,
    sent_gate,
    route_ref,
    router_ref,
    w_ref,
    gain_ref,
    grad_hidden_ref,
    grad_att_ref,
    aug_ref,
    gate_out_ref,
    router_grad_ref,
    gain_grad_ref,
    keep_ref,
    give_ref,
    total,
    *,
    experts,
):
    step, steps = pl.program_id(0), pl.num_programs(0)

    @pl.when(step == 0)
    def _():
        router_grad_ref[...] = jnp.zeros_like(router_grad_ref)
        gain_grad_ref[...] = jnp.zeros_like(gain_grad_ref)
        total[...] = jnp.zeros_like(total)

    early = step < steps // 2
    of = lambda low, high: jnp.where(early, low[...], high[...])
    hidden, second, attended = hidden_ref[...], second_ref[...], att_ref[...]
    cot = cot_ref[...].astype(F32)
    scale = lax.rsqrt(jnp.mean(hidden * hidden, axis=1, keepdims=True) + EPSILON)
    probs, chosen, gate = routed_gate(
        second, router_ref[...], column_of(route_ref[...]), experts
    )
    inner = own_gate[0:1, :] + sent_gate[0:1, :]
    inner = jnp.broadcast_to(inner, (LANES, inner.shape[1])).T
    gate_out_ref[...] = jnp.broadcast_to(gate, gate_out_ref.shape)
    grad_logits = (probs * (jnp.where(chosen, inner, 0.0) - gate * inner)).astype(BF16)
    router_grad_ref[...] += dot(grad_logits, second, TN)
    grad_second = of(own_a, own_b).astype(F32) + of(sent_a, sent_b).astype(F32)
    grad_second = grad_second + dot(grad_logits, router_ref[...], NT)
    scaled_hidden = hidden * scale
    gain_grad_ref[...] += jnp.sum(grad_second * scaled_hidden, axis=0, keepdims=True)
    scaled = grad_second * gain_ref[...]
    mean = jnp.mean(scaled * scaled_hidden, axis=1, keepdims=True)
    grad_hidden = cot + scale * (scaled - scaled_hidden * mean)
    branch = grad_hidden.astype(BF16)
    grad_hidden_ref[...] = grad_hidden
    grad_att = dot(branch, w_ref[...], NT).astype(BF16)
    grad_att_ref[...] = grad_att
    total[...] += dot(attended, branch, TN)
    product = grad_att.astype(F32) * attended.astype(F32)
    rows, width = product.shape
    feature = lax.broadcasted_iota(jnp.int32, (width, LANES), 0)
    lane = lax.broadcasted_iota(jnp.int32, (width, LANES), 1)
    head = (lane & 15) == feature // 64
    collect = jnp.where(head & (lane < 48), 1.0, 0.0).astype(BF16)
    high = product.astype(BF16)
    rest = product - high.astype(F32)
    middle = rest.astype(BF16)
    low = (rest - middle.astype(F32)).astype(BF16)
    stats = dot(high, collect) + dot(middle, collect) + dot(low, collect)
    row_lane = lax.broadcasted_iota(jnp.int32, (rows, LANES), 1)
    aug_ref[...] = jnp.where(row_lane < 48, lane_parts(stats, row_lane), 0.0).astype(BF16)

    @pl.when(step == steps - 1)
    def _():
        keep_and_give(bit_ref[0], total[...], keep_ref, give_ref)


def hidden_back(bit, hidden, second, own, sent, att, cot, gates, route_row, out_full, gain, shards, experts, block=256):
    rows, width = cot.shape
    steps = rows // block
    half = steps // 2
    part = width // shards // 2
    here = lambda i, _: (i, 0)
    wide = lambda index: pl.BlockSpec((block, width), index)
    low = wide(lambda i, _: (jnp.minimum(i, half - 1), 0))
    high = wide(lambda i, _: (jnp.maximum(i - half, 0), 0))
    along = lambda height: pl.BlockSpec((height, block), lambda i, _: (0, i))
    return pl.pallas_call(
        functools.partial(hidden_back_kernel, experts=experts),
        grid_spec=pltpu.PrefetchScalarGridSpec(
            num_scalar_prefetch=1,
            grid=(steps,),
            in_specs=[low, high] * 2
            + [wide(here)] * 4
            + [
                along(8),
                along(8),
                along(1),
                pl.BlockSpec((width, LANES), lambda *_: (0, width // LANES)),
                pl.BlockSpec((width, width), lambda *_: (0, 0)),
                whole_spec((1, width)),
            ],
            out_specs=[
                wide(here),
                wide(here),
                pl.BlockSpec((block, LANES), here),
                pl.BlockSpec((block, LANES), here),
                whole_spec((LANES, width)),
                whole_spec((1, width)),
                whole_spec((shards, part, width)),
                whole_spec((shards, part, width)),
            ],
            scratch_shapes=[pltpu.VMEM((width, width), F32)],
        ),
        out_shape=[
            jax.ShapeDtypeStruct((rows, width), F32),
            jax.ShapeDtypeStruct((rows, width), BF16),
            jax.ShapeDtypeStruct((rows, LANES), BF16),
            jax.ShapeDtypeStruct((rows, LANES), F32),
            jax.ShapeDtypeStruct((LANES, width), F32),
            jax.ShapeDtypeStruct((1, width), F32),
            jax.ShapeDtypeStruct((shards, part, width), BF16),
            jax.ShapeDtypeStruct((shards, part, width), BF16),
        ],
        compiler_params=params(),
        cost_estimate=lasting(12),
        name="hidden_back",
    )(bit, *own, *sent, hidden, second, att, cot, *gates, route_row, out_full, out_full, gain)


def token_back_kernel(tok_ref, grad_ref, gain_ref, *refs):
    weights, triples, out_ref = refs[:GATHERS], refs[GATHERS:-1], refs[-1]
    rows = tok_ref[...].astype(F32)
    scale = lax.rsqrt(jnp.mean(rows * rows, axis=1, keepdims=True) + EPSILON)
    grads = jnp.concatenate([t[p] for p in range(3) for t in triples], axis=1)
    span = grads.shape[1] // len(weights)
    grad_normed = jnp.zeros(rows.shape, F32)
    for at, weight in enumerate(weights):
        grad_normed += dot(grads[:, at * span : (at + 1) * span], weight[...], NT)
    scaled_rows = rows * scale
    scaled = grad_normed * gain_ref[...]
    mean = jnp.mean(scaled * scaled_rows, axis=1, keepdims=True)
    out_ref[...] = (grad_ref[...] + scale * (scaled - scaled_rows * mean)).astype(BF16)


def token_back(tokens, grad_hidden, grad_triples, weights, gain_row, block=256):
    rows, width = tokens.shape
    here = lambda i: (i, 0)
    return pl.pallas_call(
        token_back_kernel,
        grid=(rows // block,),
        in_specs=[
            pl.BlockSpec((block, width), here),
            pl.BlockSpec((block, width), here),
            whole_spec((1, width)),
        ]
        + [whole_spec((width, 3 * width // len(weights))) for w in weights]
        + [pl.BlockSpec((3, block, t.shape[2]), lambda i: (0, i, 0)) for t in grad_triples],
        out_specs=pl.BlockSpec((block, width), here),
        out_shape=jax.ShapeDtypeStruct((rows, width), BF16),
        compiler_params=params(),
        cost_estimate=lasting(9),
        name="token_back",
    )(tokens, grad_hidden, gain_row, *weights, *grad_triples)


def swap(value, axis, step=1):
    size = lax.axis_size(axis)
    return lax.ppermute(value, axis, [(i, i ^ step) for i in range(size)])


def bit_of(axis, step):
    return lax.axis_index(axis) // step % 2


def bits(size, first=1):
    return [1 << n for n in range(first.bit_length() - 1, size.bit_length() - 1)]


def rounded(parts):
    return sum(part.astype(F32) for part in parts).astype(BF16)


def exchange(parts, axis, step, pick):
    bit = bit_of(axis, step)
    give = rounded([pick(part, 1 - bit) for part in parts])
    return [pick(part, bit) for part in parts] + [swap(give, axis, step)]


def halve(parts, axis, step):
    def pick(part, bit):
        parted = part.reshape((part.shape[0], 2, part.shape[1] // 2) + part.shape[2:])
        return lax.dynamic_index_in_dim(parted, bit, 1, keepdims=False)

    return exchange(parts, axis, step, pick)


def to_owner(parts, steps):
    def pick(part, bit):
        parted = part.reshape((part.shape[0] // 2, 2) + part.shape[1:])
        return lax.dynamic_index_in_dim(parted, bit, 1, keepdims=False)

    for step in steps:
        parts = exchange(parts, "shard", step, pick)
    return parts


def to_owner_early(parts):
    return to_owner(parts, bits(lax.axis_size("shard"))[:-1])


def to_owner_last(parts):
    return to_owner(parts, bits(lax.axis_size("shard"))[-1:])


def both(parts, axis, step):
    mine = rounded(parts)
    return [mine, swap(mine, axis, step)]


def unhalve(value, axis, step, dim):
    other = swap(value, axis, step)
    first = bit_of(axis, step) == 0
    low = jnp.where(first, value, other)
    high = jnp.where(first, other, value)
    return jnp.concatenate([low, high], axis=dim)


def neighbours(parts):
    return halve(parts, "dp", 1) if lax.axis_size("dp") > 1 else parts


def spread(parts):
    for step in bits(lax.axis_size("dp"), 2):
        parts = halve(parts, "dp", step)
    return parts


def unspread(value):
    for step in reversed(bits(lax.axis_size("dp"), 2)):
        value = unhalve(value, "dp", step, 0)
    return value


def summed(parts):
    for step in bits(lax.axis_size("dp"), 2):
        parts = both(parts, "dp", step)
    return parts


def finish_expert(early, late, local):
    early, late = rounded(early)[0], rounded(late)[0]
    whole = jnp.concatenate([unspread(early), rounded(summed([late]))], axis=0)
    if lax.axis_size("dp") > 1:
        whole = unhalve(whole, "dp", 1, 0)
    return whole.reshape((local, -1) + whole.shape[1:]).astype(F32)


def tie(value, *sums):
    value, *last = lax.optimization_barrier((value,) + tuple(parts[-1] for parts in sums))
    return (value, *(parts[:-1] + [part] for parts, part in zip(sums, last)))


def dense_across(parts):
    return halve(parts, "expert", 1) if lax.axis_size("expert") > 1 else parts


def dense_finish(parts):
    parts = [rounded(parts)[0]]
    for axis in ("expert", "dp"):
        for step in bits(lax.axis_size(axis), 2):
            parts = both(parts, axis, step)
    value = rounded(parts)
    for axis in ("expert", "dp"):
        if lax.axis_size(axis) > 1:
            value = unhalve(value, axis, 1, 0)
    return value.astype(F32)


def gather_far(value):
    shards, parts = lax.axis_size("shard"), lax.axis_size("dp")
    rows, columns = value.shape
    parted = value.reshape(parts, rows // parts, columns)
    mine = lax.dynamic_index_in_dim(parted, lax.axis_index("dp"), 0, keepdims=False)
    me = lax.axis_index("shard")
    whole = lax.dynamic_update_index_in_dim(
        jnp.zeros((shards,) + mine.shape, value.dtype), mine, me, 0
    )
    for away in range(1, shards):
        piece = lax.ppermute(mine, "shard", [(i, (i + away) % shards) for i in range(shards)])
        whole = lax.dynamic_update_index_in_dim(whole, piece, (me - away) % shards, 0)
    return whole


def gather_near(share):
    shards, rows, columns = share.shape
    whole = share[:, None]
    for step in reversed(bits(lax.axis_size("dp"))):
        other = swap(whole, "dp", step)
        first = bit_of("dp", step) == 0
        low, high = jnp.where(first, whole, other), jnp.where(first, other, whole)
        whole = jnp.stack([low, high], axis=2)
        whole = whole.reshape(shards, -1, rows, columns)
    return whole.reshape(-1, columns)


def places_of(route_ids, first, local, capacity):
    owned = route_ids - first
    choose = owned[:, None] == jnp.arange(local, dtype=jnp.int32)[None, :]
    rank = jnp.cumsum(choose.astype(jnp.int32), axis=0) - 1
    slot = jnp.sum(jnp.where(choose, rank, 0), axis=1) + owned * capacity
    full = (rank[-1] >= capacity // 2).astype(jnp.int32)
    return jnp.where(jnp.any(choose, axis=1), slot, -1), full


def experts_of_pairs(second, cotangent, routes, out_full, expert_in, expert_out, experts, early):
    rows, width = cotangent.shape
    local, _, ff = expert_in.shape
    capacity = 2 * rows // experts
    ff_block = ff // lax.axis_size("shard")
    other_cot, other_routes = early
    other_second = swap(second, "expert")
    first_own = lax.axis_index("expert") * local
    results, flags = [], []
    for rows_of, cot, route_ids in (
        (second, cotangent, routes),
        (other_second, other_cot, other_routes),
    ):
        place, full = places_of(route_ids, first_own, local, capacity)
        if results:
            rows_of, _ = lax.optimization_barrier((rows_of, results[0][7]))
        results.append(
            expert_rows(
                full[None],
                rows_of,
                cot,
                route_ids[None, :],
                out_full,
                place,
                expert_in,
                expert_out,
                capacity,
                experts,
                ff_block,
            )
        )
        flags.append(full)
    own, other = results
    full = jnp.stack(flags)
    keep = bit_of("dp", 1)
    one = lambda expert: expert[None].astype(jnp.int32)
    grad = lambda expert, left, right: weight_grad(
        full, one(expert), left, right, capacity, ff_block
    )
    acts, grads = (own[0], other[0]), (own[3], other[3])
    xs, grad_pres = (own[2], other[2]), (own[1], other[1])
    back_a = swap(other[5], "expert")
    sent_gate = swap(other[7], "expert")
    out_give = grad(1 - keep, acts, grads)
    full, *out_give = lax.optimization_barrier((full, *out_give))
    out_keep = grad(keep, acts, grads)
    full, back_a, sent_gate, back_b, *out_both = lax.optimization_barrier(
        (full, back_a, sent_gate, other[6], *out_keep, *out_give)
    )
    back_b = swap(back_b, "expert")
    out_keep, out_sent = out_both[:2], [swap(part, "dp") for part in out_both[2:]]
    in_give = grad(1 - keep, xs, grad_pres)
    full, *out_sent = lax.optimization_barrier((full, *out_sent, *in_give))
    out_sent, in_give = out_sent[:2], out_sent[2:]
    in_sent = [swap(part, "dp") for part in in_give]
    out_early = spread([out_keep[0], out_sent[0]])
    out_late = to_owner_early([out_keep[1], out_sent[1]])
    in_keep = grad(keep, xs, grad_pres)
    gate, *in_keep = lax.optimization_barrier((own[7], *in_keep))
    in_near = tuple([mine, sent] for mine, sent in zip(in_keep, in_sent))
    return (own[4], other[4]), (own[5:7], (back_a, back_b)), (gate, sent_gate), in_near, (out_early, out_late)


def experts_of_many(second, cotangent, route_ids, router, expert_in, expert_out):
    tok_rows, width = second.shape
    experts_all = router.shape[1]
    local, _, ff = expert_in.shape
    groups = lax.axis_size("expert")
    shards = lax.axis_size("shard")
    capacity = 2 * tok_rows // experts_all
    choose = route_ids[:, None] == jnp.arange(experts_all, dtype=jnp.int32)[None, :]
    rank = jnp.cumsum(choose.astype(jnp.int32), axis=0) - 1
    slot_index = route_ids * capacity + jnp.sum(jnp.where(choose, rank, 0), axis=1)
    probs = jax.nn.softmax(dot(second, router), axis=-1)
    gate = jnp.sum(jnp.where(choose, probs, 0.0), axis=1)

    def across(value):
        return lax.all_to_all(value, "expert", split_axis=0, concat_axis=0, tiled=True)

    def to_slots(token_rows):
        filled = jnp.zeros((experts_all * capacity, width), token_rows.dtype)
        filled = filled.at[slot_index].set(token_rows)
        return across(filled.reshape(groups, local, capacity, width))

    def from_slots(value):
        return across(value).reshape(experts_all * capacity, width)[slot_index]

    def einsum(form, left, right):
        return jnp.einsum(form, left, right, preferred_element_type=F32)

    def gelu(value):
        return jax.nn.gelu(value, approximate=True)

    grad_out = cotangent.astype(F32)
    arrived = to_slots(second)
    pre_act, pull = jax.vjp(gelu, einsum("aecd,edf->aecf", arrived, expert_in))
    activated = pre_act.astype(BF16)
    produced = einsum("aecf,efd->aecd", activated, expert_out).astype(BF16)
    returned = from_slots(produced)
    inner = jnp.sum(grad_out * returned.astype(F32), axis=1)
    grad_arrived = to_slots((gate[:, None] * grad_out).astype(BF16))
    grad_act = einsum("aecd,efd->aecf", grad_arrived, expert_out)
    grad_pre = pull(grad_act)[0].astype(BF16)
    grad_w_out = einsum("aecf,aecd->efd", activated, grad_arrived).astype(BF16)
    grad_w_in = einsum("aecd,aecf->edf", arrived, grad_pre).astype(BF16)
    back = from_slots(einsum("aecf,edf->aecd", grad_pre, expert_in).astype(BF16))
    grad_w_in = grad_w_in.reshape(local, width, shards, ff // shards).transpose(2, 0, 1, 3)
    grad_w_out = grad_w_out.reshape(local, shards, ff // shards, width).transpose(1, 0, 2, 3)
    def near(value):
        parts = neighbours([value.reshape((shards, -1) + value.shape[3:])])
        cut = early_rows(parts[0].shape[1])
        return [part[:, :cut] for part in parts], [part[:, cut:] for part in parts]

    out_early, out_late = near(grad_w_out)
    back = jnp.split(back, 2, axis=0)
    nothing = [jnp.zeros_like(part) for part in back]
    inner = jnp.broadcast_to(inner[None, :], (8, tok_rows))
    return (
        (returned, jnp.zeros_like(returned)),
        (back, nothing),
        (inner, jnp.zeros_like(inner)),
        near(grad_w_in),
        (spread(out_early), to_owner_early(out_late)),
    )


def body(
    tokens,
    segments,
    routes,
    cotangent,
    attn_in,
    attn_out,
    router,
    gain_one,
    gain_two,
    expert_in,
    expert_out,
):
    rows, width = tokens.shape
    experts = router.shape[1]
    local = expert_in.shape[0]
    lanes_of = lambda value: jnp.pad(value[:, None], ((0, 0), (0, LANES - 1)))
    padded = lambda value: jnp.pad(value, ((0, 0), (0, LANES - experts)))
    segment_col = segments[0][:, None]
    route_ids = routes.reshape(rows)
    bit = bit_of("dp", 1)[None].astype(jnp.int32)
    shards = lax.axis_size("shard")
    pairs_only = lax.axis_size("expert") == local == 2
    early = None

    span = 3 * width // GATHERS
    pieces = [attn_in[:, g * span : (g + 1) * span] for g in range(GATHERS)]
    pieces[0] = jnp.concatenate([pieces[0], lanes_of(gain_one)], axis=1)
    shares = [gather_far(piece) for piece in pieces]
    source = jnp.concatenate([attn_out, padded(router), lanes_of(gain_two)], axis=1)
    weights = [gather_near(share) for share in shares]
    source, *weights = lax.optimization_barrier((source, *weights))
    first_gain = weights[0][:, span].astype(F32)[None, :]
    if pairs_only:
        early = (swap(cotangent, "expert"), swap(route_ids, "expert"))
    share = gather_far(source)

    normed, triple = qkv(tokens, first_gain, weights, span)
    triple, share = lax.optimization_barrier((triple, share))
    out_full = gather_near(share)
    second_gain = out_full[:, width + LANES].astype(F32)[None, :]
    attended, qaug = attend_forward(triple, segment_col)
    hidden, second = project(tokens, attended, out_full, second_gain)
    if pairs_only:
        done = experts_of_pairs(
            second, cotangent, route_ids, out_full, expert_in, expert_out, experts, early
        )
    else:
        full_router = out_full[:, width : width + experts]
        done = experts_of_many(
            second, cotangent, route_ids, full_router, expert_in, expert_out
        )
    returned, (own_back, sent_back), inner, in_near, (out_early, out_late) = done

    in_early, in_late = in_near
    gate, out_late, in_early, in_late = tie(inner[0], out_late, in_early, in_late)
    out_late = to_owner_last(out_late)
    in_late = to_owner_early(in_late)
    (
        grad_hidden,
        grad_att,
        gaug,
        gates,
        grad_router,
        grad_gain_two,
        keep_out,
        give_out,
    ) = hidden_back(
        bit,
        hidden,
        second,
        own_back,
        sent_back,
        attended,
        cotangent,
        (gate, inner[1]),
        route_ids[None, :],
        out_full,
        second_gain,
        shards,
        experts,
    )
    heads = width // 64 // GROUPS
    back = lambda grad, g: attend_backward(
        bit, triple, grad, segment_col, qaug, gaug, normed, shards, g * heads, heads
    )

    grad_att, out_early, (made,) = tie(grad_att, out_early, [returned[1]])
    made = swap(made, "expert") if pairs_only else made
    out_early = to_owner_early(out_early)
    in_early = spread(in_early)
    grads_0, keep_0, give_0 = back(grad_att, 0)
    small = padded(grad_router[:experts].T.astype(BF16))
    small = jnp.concatenate([small, lanes_of(grad_gain_two[0].astype(BF16))], axis=1)
    small = small.reshape(shards, 2, width // shards // 2, 2 * LANES)
    pick = lambda half: lax.dynamic_index_in_dim(small, half, 1, keepdims=False)
    keep_a = jnp.concatenate([keep_out, pick(bit[0]), keep_0], axis=2)
    give_a = jnp.concatenate([give_out, pick(1 - bit[0]), give_0], axis=2)
    dense_a = [keep_a, swap(give_a, "dp")]

    grad_att, out_early, out_late, in_late, (grads_0,) = tie(
        grad_att, out_early, out_late, in_late, [grads_0]
    )
    out_early = to_owner_last(out_early)
    in_late = to_owner_last(in_late)
    grads_1, keep_1, give_1 = back(grad_att, 1)

    grad_att, in_early, dense_a, (grads_1,) = tie(grad_att, in_early, dense_a, [grads_1])
    in_early = to_owner_early(in_early)
    dense_a = dense_across(dense_a)
    grads_2, keep_2, give_2 = back(grad_att, 2)
    keep_b = jnp.concatenate([keep_1, keep_2], axis=2)
    dense_b = [keep_b, swap(jnp.concatenate([give_1, give_2], axis=2), "dp")]

    grad_hidden, in_early, out_early, in_late, dense_a, (grads_2,) = tie(
        grad_hidden, in_early, out_early, in_late, dense_a, [grads_2]
    )
    in_early = to_owner_last(in_early)
    final_out = finish_expert(out_early, out_late, local)
    dense_a = to_owner_early(dense_a)
    grad_tokens = token_back(
        tokens, grad_hidden, (grads_0, grads_1, grads_2), weights, first_gain
    )
    dense_b = dense_across(dense_b)
    dense_a = dense_finish(to_owner_last(dense_a))
    dense_b = dense_finish(to_owner_last(to_owner_early(dense_b)))
    final_in = finish_expert(in_early, in_late, local)

    start = width + 2 * LANES
    pair_columns = lambda value, start: [
        value[:, c : c + LANES] for c in range(start, value.shape[1], LANES)
    ]
    columns = pair_columns(dense_a, start) + pair_columns(dense_b, 0)
    grad_attn_in = jnp.concatenate(columns[0::3] + columns[1::3] + columns[2::3], axis=1)
    grad_gain_one = jnp.sum(attn_in.astype(F32) * grad_attn_in, axis=1) / gain_one.astype(F32)

    wide = returned[0].astype(F32) + made.astype(F32)
    layer = hidden + gates[:, :1] * wide
    return (
        layer.astype(BF16),
        grad_tokens,
        grad_attn_in,
        dense_a[:, :width],
        dense_a[:, width : width + experts],
        grad_gain_one,
        dense_a[:, width + LANES],
        final_in,
        final_out,
    )


def solution(mesh):
    everywhere = P(("dp", "expert", "shard"), None)
    placed = (everywhere,) * 4 + (P("shard", None),) * 3 + (P("shard"),) * 2
    placed = placed + (P("expert", None, None),) * 2
    outs = (everywhere,) * 2 + (P("shard", None),) * 3 + (P("shard"),) * 2
    outs = outs + (P("expert", None, "shard"), P("expert", "shard", None))
    return jax.shard_map(
        body, mesh=mesh, in_specs=placed, out_specs=outs, check_vma=False
    )
```

```python
import functools
import math

import jax
import jax.numpy as jnp
from jax import lax
from jax.experimental import pallas as pl
from jax.experimental.pallas import tpu as pltpu
from jax.sharding import PartitionSpec as P

HEADS = 12
LANES = 128
EPSILON = 1e-06
MASKED = -1e30
BF16 = jnp.bfloat16
F32 = jnp.float32
NN = (((1,), (0,)), ((), ()))
NT = (((1,), (1,)), ((), ()))
TN = (((0,), (0,)), ((), ()))
GROUPS = 3
GATHERS = 2
SHARE = 0.05
GELU_C = math.sqrt(2.0 / math.pi)
GELU_A = 0.044715


def dot(left, right, dims=NN):
    return lax.dot_general(left, right, dims, preferred_element_type=F32)


def column_of(row):
    wide = jnp.broadcast_to(row.astype(F32), (LANES, row.shape[1]))
    return wide.T.astype(jnp.int32)


def params(mebibytes=60):
    return pltpu.CompilerParams(vmem_limit_bytes=mebibytes << 20)


def lasting(microseconds):
    return pl.CostEstimate(
        flops=int(microseconds * SHARE * 1.15e9), bytes_accessed=0, transcendentals=0
    )


def whole_spec(shape, buffers=1):
    return pl.BlockSpec(
        shape, lambda *_: (0,) * len(shape), pipeline_mode=pl.Buffered(buffers)
    )


def lane_parts(value, lane):
    high = value.astype(BF16).astype(F32)
    middle = (value - high).astype(BF16).astype(F32)
    low = value - high - middle
    return jnp.where(lane < 16, high, jnp.where(lane < 32, middle, low))


def attend_kernel(q_ref, k_ref, v_ref, seg_ref, out_ref, qaug_ref, lse_ref, *, block):
    pair, pairs = pl.program_id(0), pl.num_programs(0)
    rows, keys = q_ref.shape[0], k_ref.shape[0]
    lane_k = lax.broadcasted_iota(jnp.int32, (keys, LANES), 1)
    lane_q = lax.broadcasted_iota(jnp.int32, (rows, LANES), 1)
    k_mark = jnp.where((lane_k - 48) == seg_ref[...], 1.0, 0.0).astype(BF16)
    zone = (lane_q >= 48) & (lane_q < 56)
    q_mark = jnp.where(zone & ((lane_q - 48) != seg_ref[...]), MASKED, 0.0)

    @pl.when(pair == 0)
    def _():
        lse_ref[...] = jnp.zeros_like(lse_ref)

    k_mark = jnp.where((lane_k >= 48) & (lane_k < 56), k_mark, jnp.asarray(0, BF16))
    k_wide = jnp.concatenate([k_ref[...], k_mark], axis=1)
    v_wide = jnp.concatenate([v_ref[...], jnp.ones((keys, LANES), BF16)], axis=1)
    lane = lane_q[:block]
    for start in range(0, rows, block):
        part = slice(start, start + block)
        query = q_ref[part] * jnp.asarray(0.125, BF16)
        outs = []
        stats = lse_ref[part]
        for side in range(2):
            own = (lane >= 64) if side else (lane < 64)
            picked = jnp.where(own, query, jnp.asarray(0, BF16))
            scores = dot(
                jnp.concatenate([picked, q_mark[part].astype(BF16)], axis=1), k_wide, NT
            )
            row_max = jnp.max(scores, axis=1, keepdims=True)
            raised = jnp.exp(scores - row_max).astype(BF16)
            summed = dot(raised, v_wide)
            total = summed[:, LANES:]
            outs.append(summed[:, :LANES] / total)
            mine = ((lane & 15) == 2 * pair + side) & (lane < 48)
            stats = jnp.where(mine, row_max + jnp.log(total), stats)
        out_ref[part] = jnp.where(lane < 64, outs[0], outs[1]).astype(BF16)
        lse_ref[part] = stats

    @pl.when(pair == pairs - 1)
    def _():
        stats = lane_parts(lse_ref[...], lane_q)
        qaug_ref[...] = jnp.where(lane_q < 48, stats, q_mark).astype(BF16)


def attend_forward(triple, segment_col, block=256):
    rows, width = triple.shape[0], triple.shape[1] // 3
    pairs = width // LANES
    return pl.pallas_call(
        functools.partial(attend_kernel, block=block),
        grid=(pairs,),
        in_specs=[
            pl.BlockSpec((rows, LANES), lambda p: (0, p)),
            pl.BlockSpec((rows, LANES), lambda p: (0, pairs + p)),
            pl.BlockSpec((rows, LANES), lambda p: (0, 2 * pairs + p)),
            whole_spec((rows, 1)),
        ],
        out_specs=[
            pl.BlockSpec((rows, LANES), lambda p: (0, p)),
            pl.BlockSpec((rows, LANES), lambda p: (0, 0)),
        ],
        out_shape=[
            jax.ShapeDtypeStruct((rows, width), BF16),
            jax.ShapeDtypeStruct((rows, LANES), BF16),
        ],
        scratch_shapes=[pltpu.VMEM((rows, LANES), F32)],
        compiler_params=params(),
        cost_estimate=lasting(24),
        name="attend_forward",
    )(triple, triple, triple, segment_col)


def keep_and_give(bit, result, keep_ref, give_ref, start=0):
    shards, half = keep_ref.shape[0], keep_ref.shape[1]
    result = result.astype(BF16)
    part = slice(start, start + result.shape[1])
    for shard in range(shards):
        low = result[2 * half * shard : 2 * half * shard + half]
        high = result[2 * half * shard + half : 2 * half * shard + 2 * half]
        keep_ref[shard, :, part] = jnp.where(bit == 0, low, high)
        give_ref[shard, :, part] = jnp.where(bit == 0, high, low)


def attend_back_kernel(
    bit_ref,
    q_ref,
    k_ref,
    v_ref,
    g_ref,
    seg_ref,
    qaug_ref,
    gaug_ref,
    normed_ref,
    *refs,
    block,
    first_head,
):
    out_ref, keep_ref, give_ref = refs[-3:]
    pair = pl.program_id(0)
    rows = q_ref.shape[0]
    lane = lax.broadcasted_iota(jnp.int32, (block, LANES), 1)
    zero = jnp.asarray(0, BF16)
    query = q_ref[...] * jnp.asarray(0.125, BF16)
    grad = g_ref[...]
    q_wide = jnp.concatenate([query, qaug_ref[...]], axis=1)
    g_wide = jnp.concatenate([grad, gaug_ref[...]], axis=1)
    zone = (lane >= 48) & (lane < 56)
    grad_q = [jnp.zeros((64, rows), F32), jnp.zeros((64, rows), F32)]
    for start in range(0, rows, block):
        part = slice(start, start + block)
        key, value = k_ref[part], v_ref[part]
        key_turned = key.T
        doc = zone & ((lane - 48) == seg_ref[part])
        grads_k, grads_v = [], []
        for side in range(2):
            own = (lane >= 64) if side else (lane < 64)
            stat = ((lane & 15) == first_head + 2 * pair + side) & (lane < 48)
            k_mark = jnp.where(stat, -1.0, jnp.where(doc, 1.0, 0.0)).astype(BF16)
            v_mark = jnp.where(stat, -1.0, 0.0).astype(BF16)
            k_wide = jnp.concatenate([jnp.where(own, key, zero), k_mark], axis=1)
            v_wide = jnp.concatenate([jnp.where(own, value, zero), v_mark], axis=1)
            probs = jnp.exp(dot(k_wide, q_wide, NT))
            grad_scores = (probs * dot(v_wide, g_wide, NT)).astype(BF16)
            grads_v.append(dot(probs.astype(BF16), grad))
            grads_k.append(dot(grad_scores, query))
            grad_q[side] = grad_q[side] + dot(
                key_turned[64 * side : 64 * side + 64], grad_scores
            )
        out_ref[1, part] = jnp.where(lane < 64, grads_k[0], grads_k[1]).astype(BF16)
        out_ref[2, part] = jnp.where(lane < 64, grads_v[0], grads_v[1]).astype(BF16)
    out_ref[0] = (jnp.concatenate(grad_q, axis=0) * 0.125).T.astype(BF16)
    grads = jnp.concatenate([out_ref[0], out_ref[1], out_ref[2]], axis=1)
    keep_and_give(bit_ref[0], dot(normed_ref[...], grads, TN), keep_ref, give_ref)


def attend_backward(
    bit, triple, grad, segment_col, qaug, gaug, normed, shards, first_head, heads, place, room, halves=(), block=512
):
    rows, width = normed.shape
    pairs, first, half = width // LANES, first_head // 2, width // shards // 2
    pair_of = lambda offset: pl.BlockSpec((rows, LANES), lambda p, _: (0, offset + p))
    weight_half = pl.BlockSpec((shards, half, 3 * LANES), lambda p, _: (0, 0, place + p))
    kept = jax.ShapeDtypeStruct((shards, half, room * 3 * LANES), BF16)
    return pl.pallas_call(
        functools.partial(attend_back_kernel, block=block, first_head=first_head),
        grid_spec=pltpu.PrefetchScalarGridSpec(
            num_scalar_prefetch=1,
            grid=(heads // 2,),
            in_specs=[
                pair_of(first),
                pair_of(pairs + first),
                pair_of(2 * pairs + first),
                pair_of(first),
                whole_spec((rows, 1)),
                whole_spec((rows, LANES)),
                whole_spec((rows, LANES)),
                whole_spec((rows, width)),
            ]
            + [pl.BlockSpec(memory_space=pl.ANY)] * len(halves),
            out_specs=[
                pl.BlockSpec((3, rows, LANES), lambda p, _: (0, 0, p)),
                weight_half,
                weight_half,
            ],
        ),
        out_shape=[
            jax.ShapeDtypeStruct((3, rows, heads * 64), BF16),
            kept,
            kept,
        ],
        input_output_aliases={9 + n: 1 + n for n in range(len(halves))},
        compiler_params=params(),
        cost_estimate=lasting(14),
        name="attend_backward",
    )(bit, triple, triple, triple, grad, segment_col, qaug, gaug, normed, *halves)


def qkv_kernel(tok_ref, gain_ref, *refs):
    weights, (normed_ref, triple_ref) = refs[:-2], refs[-2:]
    rows = tok_ref[...].astype(F32)
    scale = lax.rsqrt(jnp.mean(rows * rows, axis=1, keepdims=True) + EPSILON)
    normed = (rows * scale * gain_ref[...]).astype(BF16)
    normed_ref[...] = normed
    span = triple_ref.shape[1] // len(weights)
    for at, weight in enumerate(weights):
        triple_ref[:, at * span : (at + 1) * span] = dot(normed, weight[...]).astype(BF16)


def qkv(tokens, gain_row, weights, span, block=256):
    rows, width = tokens.shape
    return pl.pallas_call(
        qkv_kernel,
        grid=(rows // block,),
        in_specs=[pl.BlockSpec((block, width), lambda i: (i, 0)), whole_spec((1, width))]
        + [whole_spec((width, span)) for weight in weights],
        out_specs=[
            pl.BlockSpec((block, width), lambda i: (i, 0)),
            pl.BlockSpec((block, 3 * width), lambda i: (i, 0)),
        ],
        out_shape=[
            jax.ShapeDtypeStruct((rows, width), BF16),
            jax.ShapeDtypeStruct((rows, 3 * width), BF16),
        ],
        compiler_params=params(),
        cost_estimate=lasting(8),
        name="qkv",
    )(tokens, gain_row, *weights)


def project_kernel(tok_ref, att_ref, w_ref, gain_ref, hidden_ref, second_ref):
    hidden = tok_ref[...].astype(F32) + dot(att_ref[...], w_ref[...])
    scale = lax.rsqrt(jnp.mean(hidden * hidden, axis=1, keepdims=True) + EPSILON)
    hidden_ref[...] = hidden
    second_ref[...] = (hidden * scale * gain_ref[...]).astype(BF16)


def project(tokens, attended, out_full, gain_row, block=256):
    rows, width = tokens.shape
    wide = pl.BlockSpec((block, width), lambda i: (i, 0))
    return pl.pallas_call(
        project_kernel,
        grid=(rows // block,),
        in_specs=[wide, wide, whole_spec((width, width)), whole_spec((1, width))],
        out_specs=[wide, wide],
        out_shape=[
            jax.ShapeDtypeStruct((rows, width), F32),
            jax.ShapeDtypeStruct((rows, width), BF16),
        ],
        compiler_params=params(),
        cost_estimate=lasting(7),
        name="project",
    )(tokens, attended, out_full, gain_row)


def routed_gate(second, router, route_wide, experts):
    logits = dot(second, router)
    lane = lax.broadcasted_iota(jnp.int32, logits.shape, 1)
    logits = jnp.where(lane < experts, logits, MASKED)
    raised = jnp.exp(logits - jnp.max(logits, axis=1, keepdims=True))
    probs = raised / jnp.sum(raised, axis=1, keepdims=True)
    chosen = lane == route_wide
    gate = jnp.sum(jnp.where(chosen, probs, 0.0), axis=1, keepdims=True)
    return probs, chosen, gate


def on_rows(full, run, capacity):
    pl.when(full == 1)(functools.partial(run, capacity))
    pl.when(full == 0)(functools.partial(run, capacity // 2))


def expert_kernel(
    full_ref,
    rows_ref,
    cot_ref,
    route_ref,
    router_ref,
    place_ref,
    w_in_ref,
    w_out_ref,
    act_ref,
    grad_pre_ref,
    x_ref,
    g_ref,
    ret_ref,
    back_a,
    back_b,
    gate_ref,
    produced,
    grad_rows,
    *,
    experts,
):
    ff, expert = pl.program_id(0), pl.program_id(1)
    slots = x_ref.shape[0]
    capacity = slots // full_ref.shape[1]
    half = capacity // 2

    @pl.when((ff == 0) & (expert == 0))
    def _():
        produced[...] = jnp.zeros_like(produced)
        grad_rows[...] = jnp.zeros_like(grad_rows)
        second = rows_ref[...]
        _, _, gate = routed_gate(second, router_ref[...], column_of(route_ref[...]), experts)
        gated = (gate * cot_ref[...].astype(F32)).astype(BF16)

        def pack(start):
            part = slice(start, start + half)
            slot = start + lax.broadcasted_iota(jnp.int32, (half, second.shape[0]), 0)
            pick = jnp.where(slot == place_ref[...], 1.0, 0.0).astype(BF16)
            x_ref[part, :] = dot(pick, second).astype(BF16)
            g_ref[part, :] = dot(pick, gated).astype(BF16)

        for owner in range(slots // capacity):
            pack(owner * capacity)
            pl.when(full_ref[0, owner] == 1)(
                functools.partial(pack, owner * capacity + half)
            )

    def run(rows):
        part = pl.ds(pl.multiple_of(expert * capacity, capacity), rows)
        pre = dot(x_ref[part, :], w_in_ref[0])
        grad_act = dot(g_ref[part, :], w_out_ref[0], NT)
        square = pre * pre
        bend = jnp.tanh(pre * (GELU_C + GELU_C * GELU_A * square))
        upper = 0.5 + 0.5 * bend
        act = (pre * upper).astype(BF16)
        inner = pre * (GELU_C + 3.0 * GELU_C * GELU_A * square)
        slope = upper + inner * (0.5 - 0.5 * bend * bend)
        grad_pre = (grad_act * slope).astype(BF16)
        act_ref[part, :] = act
        grad_pre_ref[part, :] = grad_pre
        produced[part, :] += dot(act, w_out_ref[0])
        grad_rows[part, :] += dot(grad_pre, w_in_ref[0], NT)

    on_rows(full_ref[0, expert], run, capacity)

    @pl.when((ff == pl.num_programs(0) - 1) & (expert == pl.num_programs(1) - 1))
    def _():
        count = ret_ref.shape[0]
        slot = lax.broadcasted_iota(jnp.int32, (count, slots), 1)
        place_col = column_of(place_ref[...])[:, :1]
        pick = jnp.where(slot == place_col, 1.0, 0.0).astype(BF16)
        returned = dot(pick, produced[...].astype(BF16))
        ret_ref[...] = returned.astype(BF16)
        grads = grad_rows[...].astype(BF16)
        back_a[...] = dot(pick[: count // 2], grads).astype(BF16)
        back_b[...] = dot(pick[count // 2 :], grads).astype(BF16)
        inner = jnp.sum(cot_ref[...].astype(F32) * returned, axis=1, keepdims=True)
        gate_ref[...] = jnp.broadcast_to(inner, (count, LANES)).T[:8]


def expert_rows(full, rows, cot, route_row, router, place, w_in, w_out, capacity, experts, ff_block):
    count, width = cot.shape
    local, _, ff = w_in.shape
    slots = local * capacity
    column = lambda f, e, _: (0, f)
    return pl.pallas_call(
        functools.partial(expert_kernel, experts=experts),
        grid_spec=pltpu.PrefetchScalarGridSpec(
            num_scalar_prefetch=1,
            grid=(ff // ff_block, local),
            in_specs=[
                whole_spec((count, width)),
                whole_spec((count, width)),
                whole_spec((1, count)),
                pl.BlockSpec((width, LANES), lambda *_: (0, width // LANES)),
                whole_spec((1, count)),
                pl.BlockSpec((1, width, ff_block), lambda f, e, _: (e, 0, f)),
                pl.BlockSpec((1, ff_block, width), lambda f, e, _: (e, f, 0)),
            ],
            out_specs=[
                pl.BlockSpec((slots, ff_block), column),
                pl.BlockSpec((slots, ff_block), column),
                whole_spec((slots, width)),
                whole_spec((slots, width)),
                whole_spec((count, width)),
                whole_spec((count // 2, width)),
                whole_spec((count // 2, width)),
                whole_spec((8, count)),
            ],
            scratch_shapes=[
                pltpu.VMEM((slots, width), F32),
                pltpu.VMEM((slots, width), F32),
            ],
        ),
        out_shape=[
            jax.ShapeDtypeStruct((slots, ff), BF16),
            jax.ShapeDtypeStruct((slots, ff), BF16),
            jax.ShapeDtypeStruct((slots, width), BF16),
            jax.ShapeDtypeStruct((slots, width), BF16),
            jax.ShapeDtypeStruct((count, width), BF16),
            jax.ShapeDtypeStruct((count // 2, width), BF16),
            jax.ShapeDtypeStruct((count // 2, width), BF16),
            jax.ShapeDtypeStruct((8, count), F32),
        ],
        compiler_params=params(),
        cost_estimate=lasting(28),
        name="expert_rows",
    )(full, rows, cot, route_row, router, place[None, :], w_in, w_out)


def weight_grad_kernel(full_ref, expert_ref, left_a, left_b, right_a, right_b, early_ref, late_ref):
    expert = expert_ref[0]
    capacity = left_a.shape[0]

    def run(rows_a, rows_b):
        total = (
            dot(left_a[:rows_a, :], right_a[:rows_a, :], TN)
            + dot(left_b[:rows_b, :], right_b[:rows_b, :], TN)
        ).astype(BF16)
        early_ref[0] = total[: early_ref.shape[1]]
        late_ref[0] = total[early_ref.shape[1] :]

    for full_a in range(2):
        for full_b in range(2):
            pl.when((full_ref[0, expert] == full_a) & (full_ref[1, expert] == full_b))(
                functools.partial(
                    run, capacity // (2 - full_a), capacity // (2 - full_b)
                )
            )


def early_rows(rows):
    return rows // 3 * 2


def weight_grad(full, expert, left, right, capacity, ff_block):
    slots, width = left[0].shape
    ff = max(width, right[0].shape[1])
    spec = lambda value: (
        pl.BlockSpec((capacity, ff_block), lambda f, _, e: (e[0], f))
        if value.shape[1] == ff
        else pl.BlockSpec(
            (capacity, value.shape[1]), lambda f, _, e: (e[0], 0), pipeline_mode=pl.Buffered(1)
        )
    )
    block = lambda value: ff_block if value.shape[1] == ff else value.shape[1]
    shape = (block(left[0]), block(right[0]))
    counts = (early_rows(shape[0]), shape[0] - early_rows(shape[0]))
    return pl.pallas_call(
        weight_grad_kernel,
        grid_spec=pltpu.PrefetchScalarGridSpec(
            num_scalar_prefetch=2,
            grid=(ff // ff_block,),
            in_specs=[spec(value) for value in (*left, *right)],
            out_specs=[
                pl.BlockSpec((1, count, shape[1]), lambda f, *_: (f, 0, 0)) for count in counts
            ],
        ),
        out_shape=[
            jax.ShapeDtypeStruct((ff // ff_block, count, shape[1]), BF16) for count in counts
        ],
        compiler_params=params(),
        cost_estimate=lasting(9),
        name="weight_grad",
    )(full, expert, *left, *right)


def hidden_back_kernel(
    bit_ref,
    own_a,
    own_b,
    sent_a,
    sent_b,
    hidden_ref,
    second_ref,
    att_ref,
    cot_ref,
    own_gate,
    sent_gate,
    route_ref,
    router_ref,
    w_ref,
    gain_ref,
    grad_hidden_ref,
    grad_att_ref,
    aug_ref,
    gate_out_ref,
    keep_ref,
    give_ref,
    total,
    router_grad_ref,
    gain_grad_ref,
    *,
    experts,
):
    step, steps = pl.program_id(0), pl.num_programs(0)

    @pl.when(step == 0)
    def _():
        router_grad_ref[...] = jnp.zeros_like(router_grad_ref)
        gain_grad_ref[...] = jnp.zeros_like(gain_grad_ref)
        total[...] = jnp.zeros_like(total)

    early = step < steps // 2
    of = lambda low, high: jnp.where(early, low[...], high[...])
    hidden, second, attended = hidden_ref[...], second_ref[...], att_ref[...]
    cot = cot_ref[...].astype(F32)
    scale = lax.rsqrt(jnp.mean(hidden * hidden, axis=1, keepdims=True) + EPSILON)
    probs, chosen, gate = routed_gate(
        second, router_ref[...], column_of(route_ref[...]), experts
    )
    inner = own_gate[0:1, :] + sent_gate[0:1, :]
    inner = jnp.broadcast_to(inner, (LANES, inner.shape[1])).T
    gate_out_ref[...] = jnp.broadcast_to(gate, gate_out_ref.shape)
    grad_logits = (probs * (jnp.where(chosen, inner, 0.0) - gate * inner)).astype(BF16)
    router_grad_ref[...] += dot(grad_logits, second, TN)
    grad_second = of(own_a, own_b).astype(F32) + of(sent_a, sent_b).astype(F32)
    grad_second = grad_second + dot(grad_logits, router_ref[...], NT)
    scaled_hidden = hidden * scale
    gain_grad_ref[...] += jnp.sum(grad_second * scaled_hidden, axis=0, keepdims=True)
    scaled = grad_second * gain_ref[...]
    mean = jnp.mean(scaled * scaled_hidden, axis=1, keepdims=True)
    grad_hidden = cot + scale * (scaled - scaled_hidden * mean)
    branch = grad_hidden.astype(BF16)
    grad_hidden_ref[...] = grad_hidden
    grad_att = dot(branch, w_ref[...], NT).astype(BF16)
    grad_att_ref[...] = grad_att
    total[...] += dot(attended, branch, TN)
    product = grad_att.astype(F32) * attended.astype(F32)
    rows, width = product.shape
    feature = lax.broadcasted_iota(jnp.int32, (width, LANES), 0)
    lane = lax.broadcasted_iota(jnp.int32, (width, LANES), 1)
    head = (lane & 15) == feature // 64
    collect = jnp.where(head & (lane < 48), 1.0, 0.0).astype(BF16)
    high = product.astype(BF16)
    rest = product - high.astype(F32)
    middle = rest.astype(BF16)
    low = (rest - middle.astype(F32)).astype(BF16)
    stats = dot(high, collect) + dot(middle, collect) + dot(low, collect)
    row_lane = lax.broadcasted_iota(jnp.int32, (rows, LANES), 1)
    aug_ref[...] = jnp.where(row_lane < 48, lane_parts(stats, row_lane), 0.0).astype(BF16)

    @pl.when(step == steps - 1)
    def _():
        keep_and_give(bit_ref[0], total[...], keep_ref, give_ref)
        lane = lax.broadcasted_iota(jnp.int32, (width, LANES), 1)
        gains = jnp.broadcast_to(gain_grad_ref[...], (LANES, width)).T
        small = jnp.where(lane == LANES - 1, gains, router_grad_ref[...].T)
        keep_and_give(bit_ref[0], small, keep_ref, give_ref, width)


def hidden_back(bit, hidden, second, own, sent, att, cot, gates, route_row, out_full, gain, shards, experts, room, block=256):
    rows, width = cot.shape
    steps = rows // block
    half = steps // 2
    part = width // shards // 2
    own_columns = width + 3 * LANES
    here = lambda i, _: (i, 0)
    wide = lambda index: pl.BlockSpec((block, width), index)
    low = wide(lambda i, _: (jnp.minimum(i, half - 1), 0))
    high = wide(lambda i, _: (jnp.maximum(i - half, 0), 0))
    along = lambda height: pl.BlockSpec((height, block), lambda i, _: (0, i))
    return pl.pallas_call(
        functools.partial(hidden_back_kernel, experts=experts),
        grid_spec=pltpu.PrefetchScalarGridSpec(
            num_scalar_prefetch=1,
            grid=(steps,),
            in_specs=[low, high] * 2
            + [wide(here)] * 4
            + [
                along(8),
                along(8),
                along(1),
                pl.BlockSpec((width, LANES), lambda *_: (0, width // LANES)),
                pl.BlockSpec((width, width), lambda *_: (0, 0)),
                whole_spec((1, width)),
            ],
            out_specs=[
                wide(here),
                wide(here),
                pl.BlockSpec((block, LANES), here),
                pl.BlockSpec((block, LANES), here),
                whole_spec((shards, part, own_columns)),
                whole_spec((shards, part, own_columns)),
            ],
            scratch_shapes=[
                pltpu.VMEM((width, width), F32),
                pltpu.VMEM((LANES, width), F32),
                pltpu.VMEM((1, width), F32),
            ],
        ),
        out_shape=[
            jax.ShapeDtypeStruct((rows, width), F32),
            jax.ShapeDtypeStruct((rows, width), BF16),
            jax.ShapeDtypeStruct((rows, LANES), BF16),
            jax.ShapeDtypeStruct((rows, LANES), F32),
            jax.ShapeDtypeStruct((shards, part, room * 3 * LANES), BF16),
            jax.ShapeDtypeStruct((shards, part, room * 3 * LANES), BF16),
        ],
        compiler_params=params(),
        cost_estimate=lasting(12),
        name="hidden_back",
    )(bit, *own, *sent, hidden, second, att, cot, *gates, route_row, out_full, out_full, gain)


def token_back_kernel(tok_ref, grad_ref, gain_ref, *refs):
    weights, triples, out_ref = refs[:GATHERS], refs[GATHERS:-1], refs[-1]
    rows = tok_ref[...].astype(F32)
    scale = lax.rsqrt(jnp.mean(rows * rows, axis=1, keepdims=True) + EPSILON)
    grads = jnp.concatenate([t[p] for p in range(3) for t in triples], axis=1)
    span = grads.shape[1] // len(weights)
    grad_normed = jnp.zeros(rows.shape, F32)
    for at, weight in enumerate(weights):
        grad_normed += dot(grads[:, at * span : (at + 1) * span], weight[...], NT)
    scaled_rows = rows * scale
    scaled = grad_normed * gain_ref[...]
    mean = jnp.mean(scaled * scaled_rows, axis=1, keepdims=True)
    out_ref[...] = (grad_ref[...] + scale * (scaled - scaled_rows * mean)).astype(BF16)


def token_back(tokens, grad_hidden, grad_triples, weights, gain_row, block=256):
    rows, width = tokens.shape
    here = lambda i: (i, 0)
    return pl.pallas_call(
        token_back_kernel,
        grid=(rows // block,),
        in_specs=[
            pl.BlockSpec((block, width), here),
            pl.BlockSpec((block, width), here),
            whole_spec((1, width)),
        ]
        + [whole_spec((width, 3 * width // len(weights))) for w in weights]
        + [pl.BlockSpec((3, block, t.shape[2]), lambda i: (0, i, 0)) for t in grad_triples],
        out_specs=pl.BlockSpec((block, width), here),
        out_shape=jax.ShapeDtypeStruct((rows, width), BF16),
        compiler_params=params(),
        cost_estimate=lasting(9),
        name="token_back",
    )(tokens, grad_hidden, gain_row, *weights, *grad_triples)


def swap(value, axis, step=1):
    size = lax.axis_size(axis)
    return lax.ppermute(value, axis, [(i, i ^ step) for i in range(size)])


def bit_of(axis, step):
    return lax.axis_index(axis) // step % 2


def bits(size, first=1):
    return [1 << n for n in range(first.bit_length() - 1, size.bit_length() - 1)]


def rounded(parts):
    return sum(part.astype(F32) for part in parts).astype(BF16)


def exchange(parts, axis, step, pick):
    bit = bit_of(axis, step)
    give = rounded([pick(part, 1 - bit) for part in parts])
    return [pick(part, bit) for part in parts] + [swap(give, axis, step)]


def halve(parts, axis, step):
    def pick(part, bit):
        parted = part.reshape((part.shape[0], 2, part.shape[1] // 2) + part.shape[2:])
        return lax.dynamic_index_in_dim(parted, bit, 1, keepdims=False)

    return exchange(parts, axis, step, pick)


def to_owner(parts, steps):
    def pick(part, bit):
        parted = part.reshape((part.shape[0] // 2, 2) + part.shape[1:])
        return lax.dynamic_index_in_dim(parted, bit, 1, keepdims=False)

    for step in steps:
        parts = exchange(parts, "shard", step, pick)
    return parts


def to_owner_early(parts):
    return to_owner(parts, bits(lax.axis_size("shard"))[:-1])


def to_owner_last(parts):
    return to_owner(parts, bits(lax.axis_size("shard"))[-1:])


def both(parts, axis, step):
    mine = rounded(parts)
    return [mine, swap(mine, axis, step)]


def unhalve(value, axis, step, dim):
    other = swap(value, axis, step)
    first = bit_of(axis, step) == 0
    low = jnp.where(first, value, other)
    high = jnp.where(first, other, value)
    return jnp.concatenate([low, high], axis=dim)


def neighbours(parts):
    return halve(parts, "dp", 1) if lax.axis_size("dp") > 1 else parts


def spread(parts):
    for step in bits(lax.axis_size("dp"), 2):
        parts = halve(parts, "dp", step)
    return parts


def unspread(value):
    for step in reversed(bits(lax.axis_size("dp"), 2)):
        value = unhalve(value, "dp", step, 0)
    return value


def summed(parts):
    for step in bits(lax.axis_size("dp"), 2):
        parts = both(parts, "dp", step)
    return parts


def finish_expert(early, late, local):
    early, late = rounded(early)[0], rounded(late)[0]
    whole = jnp.concatenate([unspread(early), rounded(summed([late]))], axis=0)
    if lax.axis_size("dp") > 1:
        whole = unhalve(whole, "dp", 1, 0)
    return whole.reshape((local, -1) + whole.shape[1:]).astype(F32)


def tie(value, *sums):
    value, *last = lax.optimization_barrier((value,) + tuple(parts[-1] for parts in sums))
    return (value, *(parts[:-1] + [part] for parts, part in zip(sums, last)))


def plane_axes():
    return [(axis, step) for axis, step in (("dp", 2), ("expert", 1)) if lax.axis_size(axis) > step]


def plane_send(value, other):
    sizes = [lax.axis_size("dp"), lax.axis_size("expert")]
    flips = [0, 0]
    for n, (axis, step) in enumerate(plane_axes()):
        flips[axis == "expert"] |= step * (other >> n & 1)
    perm = [
        (d * sizes[1] + e, (d ^ flips[0]) * sizes[1] + (e ^ flips[1]))
        for d in range(sizes[0])
        for e in range(sizes[1])
    ]
    return lax.ppermute(value, ("dp", "expert"), perm)


def plane_index():
    return sum(bit_of(axis, step) << n for n, (axis, step) in enumerate(plane_axes()))


def dense_across(parts):
    count = 1 << len(plane_axes())
    me = plane_index()

    def pick(part, index):
        parted = part.reshape((part.shape[0], count, -1) + part.shape[2:])
        return lax.dynamic_index_in_dim(parted, index, 1, keepdims=False)

    got = [
        plane_send(rounded([pick(part, me ^ other) for part in parts]), other)
        for other in range(1, count)
    ]
    return [pick(part, me) for part in parts] + got


def dense_owner(parts):
    me, count = lax.axis_index("shard"), lax.axis_size("shard")
    pick = lambda part, index: lax.dynamic_index_in_dim(part, index, 0, keepdims=False)
    got = []
    for other in range(1, count):
        give = rounded([pick(part, me ^ other) for part in parts])
        got.append(swap(give, "shard", other))
    return [pick(part, me) for part in parts] + got


def dense_finish(parts):
    for step in bits(lax.axis_size("expert"), 2):
        parts = both(parts, "expert", step)
    for step in bits(lax.axis_size("dp"), 4):
        parts = both(parts, "dp", step)
    mine = rounded(parts)
    count = 1 << len(plane_axes())
    me = plane_index()
    pieces = [mine] + [plane_send(mine, other) for other in range(1, count)]
    rows = []
    for index in range(count):
        row = pieces[0]
        for other in range(1, count):
            row = jnp.where(me ^ index == other, pieces[other], row)
        rows.append(row)
    value = jnp.concatenate(rows, axis=0)
    return unhalve(value, "dp", 1, 0).astype(F32)


def gather_far(value):
    shards, parts = lax.axis_size("shard"), lax.axis_size("dp")
    rows, columns = value.shape
    parted = value.reshape(parts, rows // parts, columns)
    mine = lax.dynamic_index_in_dim(parted, lax.axis_index("dp"), 0, keepdims=False)
    me = lax.axis_index("shard")
    whole = lax.dynamic_update_index_in_dim(
        jnp.zeros((shards,) + mine.shape, value.dtype), mine, me, 0
    )
    for away in range(1, shards):
        piece = lax.ppermute(mine, "shard", [(i, (i + away) % shards) for i in range(shards)])
        whole = lax.dynamic_update_index_in_dim(whole, piece, (me - away) % shards, 0)
    return whole[:, None]


def gather_step(whole, step):
    other = swap(whole, "dp", step)
    first = bit_of("dp", step) == 0
    low, high = jnp.where(first, whole, other), jnp.where(first, other, whole)
    whole = jnp.stack([low, high], axis=2)
    return whole.reshape((whole.shape[0], -1) + whole.shape[3:])


def gather_near(whole, steps):
    for step in steps:
        whole = gather_step(whole, step)
    return whole


def places_of(route_ids, first, local, capacity):
    owned = route_ids - first
    choose = owned[:, None] == jnp.arange(local, dtype=jnp.int32)[None, :]
    rank = jnp.cumsum(choose.astype(jnp.int32), axis=0) - 1
    slot = jnp.sum(jnp.where(choose, rank, 0), axis=1) + owned * capacity
    full = (rank[-1] >= capacity // 2).astype(jnp.int32)
    return jnp.where(jnp.any(choose, axis=1), slot, -1), full


def experts_of_pairs(second, cotangent, routes, out_full, expert_in, expert_out, experts, early):
    rows, width = cotangent.shape
    local, _, ff = expert_in.shape
    capacity = 2 * rows // experts
    ff_block = ff // lax.axis_size("shard")
    other_cot, other_routes = early
    other_second = swap(second, "expert")
    first_own = lax.axis_index("expert") * local
    results, flags = [], []
    for rows_of, cot, route_ids in (
        (second, cotangent, routes),
        (other_second, other_cot, other_routes),
    ):
        place, full = places_of(route_ids, first_own, local, capacity)
        if results:
            rows_of, _ = lax.optimization_barrier((rows_of, results[0][7]))
        results.append(
            expert_rows(
                full[None],
                rows_of,
                cot,
                route_ids[None, :],
                out_full,
                place,
                expert_in,
                expert_out,
                capacity,
                experts,
                ff_block,
            )
        )
        flags.append(full)
    own, other = results
    full = jnp.stack(flags)
    keep = bit_of("dp", 1)
    one = lambda expert: expert[None].astype(jnp.int32)
    grad = lambda expert, left, right: weight_grad(
        full, one(expert), left, right, capacity, ff_block
    )
    acts, grads = (own[0], other[0]), (own[3], other[3])
    xs, grad_pres = (own[2], other[2]), (own[1], other[1])
    back_a = swap(other[5], "expert")
    sent_gate = swap(other[7], "expert")
    out_give = grad(1 - keep, acts, grads)
    full, *out_give = lax.optimization_barrier((full, *out_give))
    out_keep = grad(keep, acts, grads)
    full, back_a, sent_gate, back_b, *out_both = lax.optimization_barrier(
        (full, back_a, sent_gate, other[6], *out_keep, *out_give)
    )
    back_b = swap(back_b, "expert")
    out_keep, out_sent = out_both[:2], [swap(part, "dp") for part in out_both[2:]]
    in_give = grad(1 - keep, xs, grad_pres)
    full, *out_sent = lax.optimization_barrier((full, *out_sent, *in_give))
    out_sent, in_give = out_sent[:2], out_sent[2:]
    in_sent = [swap(part, "dp") for part in in_give]
    out_early = spread([out_keep[0], out_sent[0]])
    out_late = to_owner_early([out_keep[1], out_sent[1]])
    in_keep = grad(keep, xs, grad_pres)
    gate, *in_keep = lax.optimization_barrier((own[7], *in_keep))
    in_near = tuple([mine, sent] for mine, sent in zip(in_keep, in_sent))
    return (own[4], other[4]), (own[5:7], (back_a, back_b)), (gate, sent_gate), in_near, (out_early, out_late)


def experts_of_many(second, cotangent, route_ids, router, expert_in, expert_out):
    tok_rows, width = second.shape
    experts_all = router.shape[1]
    local, _, ff = expert_in.shape
    groups = lax.axis_size("expert")
    shards = lax.axis_size("shard")
    capacity = 2 * tok_rows // experts_all
    choose = route_ids[:, None] == jnp.arange(experts_all, dtype=jnp.int32)[None, :]
    rank = jnp.cumsum(choose.astype(jnp.int32), axis=0) - 1
    slot_index = route_ids * capacity + jnp.sum(jnp.where(choose, rank, 0), axis=1)
    probs = jax.nn.softmax(dot(second, router), axis=-1)
    gate = jnp.sum(jnp.where(choose, probs, 0.0), axis=1)

    def across(value):
        return lax.all_to_all(value, "expert", split_axis=0, concat_axis=0, tiled=True)

    def to_slots(token_rows):
        filled = jnp.zeros((experts_all * capacity, width), token_rows.dtype)
        filled = filled.at[slot_index].set(token_rows)
        return across(filled.reshape(groups, local, capacity, width))

    def from_slots(value):
        return across(value).reshape(experts_all * capacity, width)[slot_index]

    def einsum(form, left, right):
        return jnp.einsum(form, left, right, preferred_element_type=F32)

    def gelu(value):
        return jax.nn.gelu(value, approximate=True)

    grad_out = cotangent.astype(F32)
    arrived = to_slots(second)
    pre_act, pull = jax.vjp(gelu, einsum("aecd,edf->aecf", arrived, expert_in))
    activated = pre_act.astype(BF16)
    produced = einsum("aecf,efd->aecd", activated, expert_out).astype(BF16)
    returned = from_slots(produced)
    inner = jnp.sum(grad_out * returned.astype(F32), axis=1)
    grad_arrived = to_slots((gate[:, None] * grad_out).astype(BF16))
    grad_act = einsum("aecd,efd->aecf", grad_arrived, expert_out)
    grad_pre = pull(grad_act)[0].astype(BF16)
    grad_w_out = einsum("aecf,aecd->efd", activated, grad_arrived).astype(BF16)
    grad_w_in = einsum("aecd,aecf->edf", arrived, grad_pre).astype(BF16)
    back = from_slots(einsum("aecf,edf->aecd", grad_pre, expert_in).astype(BF16))
    grad_w_in = grad_w_in.reshape(local, width, shards, ff // shards).transpose(2, 0, 1, 3)
    grad_w_out = grad_w_out.reshape(local, shards, ff // shards, width).transpose(1, 0, 2, 3)
    def near(value):
        parts = neighbours([value.reshape((shards, -1) + value.shape[3:])])
        cut = early_rows(parts[0].shape[1])
        return [part[:, :cut] for part in parts], [part[:, cut:] for part in parts]

    out_early, out_late = near(grad_w_out)
    back = jnp.split(back, 2, axis=0)
    nothing = [jnp.zeros_like(part) for part in back]
    inner = jnp.broadcast_to(inner[None, :], (8, tok_rows))
    return (
        (returned, jnp.zeros_like(returned)),
        (back, nothing),
        (inner, jnp.zeros_like(inner)),
        near(grad_w_in),
        (spread(out_early), to_owner_early(out_late)),
    )


def body(
    tokens,
    segments,
    routes,
    cotangent,
    attn_in,
    attn_out,
    router,
    gain_one,
    gain_two,
    expert_in,
    expert_out,
):
    rows, width = tokens.shape
    experts = router.shape[1]
    local = expert_in.shape[0]
    lanes_of = lambda value: jnp.pad(value[:, None], ((0, 0), (0, LANES - 1)))
    padded = lambda value: jnp.pad(value, ((0, 0), (0, LANES - experts)))
    segment_col = segments[0][:, None]
    route_ids = routes.reshape(rows)
    bit = bit_of("dp", 1)[None].astype(jnp.int32)
    shards = lax.axis_size("shard")
    pairs_only = lax.axis_size("expert") == local == 2
    early = None

    span = 3 * width // GATHERS
    pieces = [attn_in[:, g * span : (g + 1) * span] for g in range(GATHERS)]
    pieces[0] = jnp.concatenate([pieces[0], lanes_of(gain_one)], axis=1)
    shares = [gather_far(piece) for piece in pieces]
    source = jnp.concatenate([attn_out, padded(router), lanes_of(gain_two)], axis=1)
    source, *shares = lax.optimization_barrier((source, *shares))
    near_steps = bits(lax.axis_size("dp"))[::-1]
    join = lambda whole: whole.reshape(-1, whole.shape[-1])
    weights = [join(gather_near(share, near_steps)) for share in shares]
    share = gather_far(source)
    first_gain = weights[0][:, span].astype(F32)[None, :]
    share, *weights = lax.optimization_barrier((share, *weights))
    share = gather_near(share, near_steps[:-1])
    if pairs_only:
        early = (swap(cotangent, "expert"), swap(route_ids, "expert"))

    normed, triple = qkv(tokens, first_gain, weights, span)
    triple, share = lax.optimization_barrier((triple, share))
    out_full = join(gather_near(share, near_steps[-1:]))
    second_gain = out_full[:, width + LANES].astype(F32)[None, :]
    attended, qaug = attend_forward(triple, segment_col)
    hidden, second = project(tokens, attended, out_full, second_gain)
    if pairs_only:
        done = experts_of_pairs(
            second, cotangent, route_ids, out_full, expert_in, expert_out, experts, early
        )
    else:
        full_router = out_full[:, width : width + experts]
        done = experts_of_many(
            second, cotangent, route_ids, full_router, expert_in, expert_out
        )
    returned, (own_back, sent_back), inner, in_near, (out_early, out_late) = done

    in_early, in_late = in_near
    gate, out_late, in_early, in_late = tie(inner[0], out_late, in_early, in_late)
    out_late = to_owner_last(out_late)
    in_late = to_owner_early(in_late)
    heads = width // 64 // GROUPS
    pieces = heads // 2
    rooms = (width // LANES // 3 + 1 + pieces, (GROUPS - 1) * pieces)
    grad_hidden, grad_att, gaug, gates, *dense_a = hidden_back(
        bit,
        hidden,
        second,
        own_back,
        sent_back,
        attended,
        cotangent,
        (gate, inner[1]),
        route_ids[None, :],
        out_full,
        second_gain,
        shards,
        experts,
        rooms[0],
    )

    def back(grad, group, place, room, halves=()):
        return attend_backward(
            bit, triple, grad, segment_col, qaug, gaug, normed, shards, group * heads, heads, place, room, halves
        )

    grad_att, out_early, in_late, (made,) = tie(grad_att, out_early, in_late, [returned[1]])
    made = swap(made, "expert") if pairs_only else made
    out_early = to_owner_early(out_early)
    in_early = spread(in_early)
    grads_0, *dense_a = back(grad_att, 0, rooms[0] - pieces, rooms[0], dense_a)

    grad_att, out_early, out_late, *dense_a = tie(grad_att, out_early, out_late, *([d] for d in (*dense_a, grads_0)))
    (keep_a,), (give_a,), (grads_0,) = dense_a
    dense_a = [keep_a, swap(give_a, "dp")]
    out_early = to_owner_last(out_early)
    in_late = to_owner_last(in_late)
    grads_1, *dense_b = back(grad_att, 1, 0, rooms[1])

    grad_att, in_early, dense_a, (grads_1,) = tie(grad_att, in_early, dense_a, [grads_1])
    in_early = to_owner_early(in_early)
    dense_a = dense_across(dense_a)
    grads_2, *dense_b = back(grad_att, 2, pieces, rooms[1], dense_b)
    dense_b = [dense_b[0], swap(dense_b[1], "dp")]

    grad_hidden, in_early, out_early, in_late, dense_a, (grads_2,) = tie(
        grad_hidden, in_early, out_early, in_late, dense_a, [grads_2]
    )
    in_early = to_owner_last(in_early)
    final_out = finish_expert(out_early, out_late, local)
    dense_a = dense_owner(dense_a)
    grad_tokens = token_back(
        tokens, grad_hidden, (grads_0, grads_1, grads_2), weights, first_gain
    )
    dense_b = dense_across(dense_b)
    dense_a = dense_finish(dense_a)
    dense_b = dense_finish(dense_owner(dense_b))
    final_in = finish_expert(in_early, in_late, local)

    start = width + 3 * LANES
    pair_columns = lambda value, start: [
        value[:, c : c + LANES] for c in range(start, value.shape[1], LANES)
    ]
    columns = pair_columns(dense_a, start) + pair_columns(dense_b, 0)
    grad_attn_in = jnp.concatenate(columns[0::3] + columns[1::3] + columns[2::3], axis=1)
    grad_gain_one = jnp.sum(attn_in.astype(F32) * grad_attn_in, axis=1) / gain_one.astype(F32)

    wide = returned[0].astype(F32) + made.astype(F32)
    layer = hidden + gates[:, :1] * wide
    return (
        layer.astype(BF16),
        grad_tokens,
        grad_attn_in,
        dense_a[:, :width],
        dense_a[:, width : width + experts],
        grad_gain_one,
        dense_a[:, width + LANES - 1],
        final_in,
        final_out,
    )


def solution(mesh):
    everywhere = P(("dp", "expert", "shard"), None)
    placed = (everywhere,) * 4 + (P("shard", None),) * 3 + (P("shard"),) * 2
    placed = placed + (P("expert", None, None),) * 2
    outs = (everywhere,) * 2 + (P("shard", None),) * 3 + (P("shard"),) * 2
    outs = outs + (P("expert", None, "shard"), P("expert", "shard", None))
    return jax.shard_map(
        body, mesh=mesh, in_specs=placed, out_specs=outs, check_vma=False
    )
```

```python
import functools
import math

import jax
import jax.numpy as jnp
from jax import lax
from jax.experimental import pallas as pl
from jax.experimental.pallas import tpu as pltpu
from jax.sharding import PartitionSpec as P

HEADS = 12
LANES = 128
EPSILON = 1e-06
MASKED = -1e30
BF16 = jnp.bfloat16
F32 = jnp.float32
NN = (((1,), (0,)), ((), ()))
NT = (((1,), (1,)), ((), ()))
TN = (((0,), (0,)), ((), ()))
GROUPS = 3
GATHERS = 2
SHARE = 0.05
GELU_C = math.sqrt(2.0 / math.pi)
GELU_A = 0.044715


def dot(left, right, dims=NN):
    return lax.dot_general(left, right, dims, preferred_element_type=F32)


def column_of(row):
    wide = jnp.broadcast_to(row.astype(F32), (LANES, row.shape[1]))
    return wide.T.astype(jnp.int32)


def params(mebibytes=60):
    return pltpu.CompilerParams(vmem_limit_bytes=mebibytes << 20)


def lasting(microseconds):
    return pl.CostEstimate(
        flops=int(microseconds * SHARE * 1.15e9), bytes_accessed=0, transcendentals=0
    )


def whole_spec(shape, buffers=1):
    return pl.BlockSpec(
        shape, lambda *_: (0,) * len(shape), pipeline_mode=pl.Buffered(buffers)
    )


def lane_parts(value, lane):
    high = value.astype(BF16).astype(F32)
    middle = (value - high).astype(BF16).astype(F32)
    low = value - high - middle
    return jnp.where(lane < 16, high, jnp.where(lane < 32, middle, low))


def attend_kernel(q_ref, k_ref, v_ref, seg_ref, out_ref, qaug_ref, lse_ref, *, block):
    pair, pairs = pl.program_id(0), pl.num_programs(0)
    rows, keys = q_ref.shape[0], k_ref.shape[0]
    lane_k = lax.broadcasted_iota(jnp.int32, (keys, LANES), 1)
    lane_q = lax.broadcasted_iota(jnp.int32, (rows, LANES), 1)
    k_mark = jnp.where((lane_k - 48) == seg_ref[...], 1.0, 0.0).astype(BF16)
    zone = (lane_q >= 48) & (lane_q < 56)
    q_mark = jnp.where(zone & ((lane_q - 48) != seg_ref[...]), MASKED, 0.0)

    @pl.when(pair == 0)
    def _():
        lse_ref[...] = jnp.zeros_like(lse_ref)

    k_mark = jnp.where((lane_k >= 48) & (lane_k < 56), k_mark, jnp.asarray(0, BF16))
    k_wide = jnp.concatenate([k_ref[...], k_mark], axis=1)
    v_wide = jnp.concatenate([v_ref[...], jnp.ones((keys, LANES), BF16)], axis=1)
    lane = lane_q[:block]
    for start in range(0, rows, block):
        part = slice(start, start + block)
        query = q_ref[part] * jnp.asarray(0.125, BF16)
        outs = []
        stats = lse_ref[part]
        for side in range(2):
            own = (lane >= 64) if side else (lane < 64)
            picked = jnp.where(own, query, jnp.asarray(0, BF16))
            scores = dot(
                jnp.concatenate([picked, q_mark[part].astype(BF16)], axis=1), k_wide, NT
            )
            row_max = jnp.max(scores, axis=1, keepdims=True)
            raised = jnp.exp(scores - row_max).astype(BF16)
            summed = dot(raised, v_wide)
            total = summed[:, LANES:]
            outs.append(summed[:, :LANES] / total)
            mine = ((lane & 15) == 2 * pair + side) & (lane < 48)
            stats = jnp.where(mine, row_max + jnp.log(total), stats)
        out_ref[part] = jnp.where(lane < 64, outs[0], outs[1]).astype(BF16)
        lse_ref[part] = stats

    @pl.when(pair == pairs - 1)
    def _():
        stats = lane_parts(lse_ref[...], lane_q)
        qaug_ref[...] = jnp.where(lane_q < 48, stats, q_mark).astype(BF16)


def attend_forward(triple, segment_col, block=256):
    rows, width = triple.shape[0], triple.shape[1] // 3
    pairs = width // LANES
    return pl.pallas_call(
        functools.partial(attend_kernel, block=block),
        grid=(pairs,),
        in_specs=[
            pl.BlockSpec((rows, LANES), lambda p: (0, p)),
            pl.BlockSpec((rows, LANES), lambda p: (0, pairs + p)),
            pl.BlockSpec((rows, LANES), lambda p: (0, 2 * pairs + p)),
            whole_spec((rows, 1)),
        ],
        out_specs=[
            pl.BlockSpec((rows, LANES), lambda p: (0, p)),
            pl.BlockSpec((rows, LANES), lambda p: (0, 0)),
        ],
        out_shape=[
            jax.ShapeDtypeStruct((rows, width), BF16),
            jax.ShapeDtypeStruct((rows, LANES), BF16),
        ],
        scratch_shapes=[pltpu.VMEM((rows, LANES), F32)],
        compiler_params=params(60),
        cost_estimate=lasting(24),
        name="attend_forward",
    )(triple, triple, triple, segment_col)


def keep_and_give(bit, result, keep_ref, give_ref, start=0):
    shards, half = keep_ref.shape[0], keep_ref.shape[1]
    result = result.astype(BF16)
    part = slice(start, start + result.shape[1])
    for shard in range(shards):
        low = result[2 * half * shard : 2 * half * shard + half]
        high = result[2 * half * shard + half : 2 * half * shard + 2 * half]
        keep_ref[shard, :, part] = jnp.where(bit == 0, low, high)
        give_ref[shard, :, part] = jnp.where(bit == 0, high, low)


def attend_back_kernel(
    bit_ref,
    q_ref,
    k_ref,
    v_ref,
    g_ref,
    seg_ref,
    qaug_ref,
    gaug_ref,
    normed_ref,
    *refs,
    block,
    first_head,
):
    out_ref, keep_ref, give_ref = refs[-3:]
    pair = pl.program_id(0)
    rows = q_ref.shape[0]
    lane = lax.broadcasted_iota(jnp.int32, (block, LANES), 1)
    zero = jnp.asarray(0, BF16)
    query = q_ref[...] * jnp.asarray(0.125, BF16)
    grad = g_ref[...]
    q_wide = jnp.concatenate([query, qaug_ref[...]], axis=1)
    g_wide = jnp.concatenate([grad, gaug_ref[...]], axis=1)
    zone = (lane >= 48) & (lane < 56)
    grad_q = [jnp.zeros((64, rows), F32), jnp.zeros((64, rows), F32)]
    for start in range(0, rows, block):
        part = slice(start, start + block)
        key, value = k_ref[part], v_ref[part]
        key_turned = key.T
        doc = zone & ((lane - 48) == seg_ref[part])
        grads_k, grads_v = [], []
        for side in range(2):
            own = (lane >= 64) if side else (lane < 64)
            stat = ((lane & 15) == first_head + 2 * pair + side) & (lane < 48)
            k_mark = jnp.where(stat, -1.0, jnp.where(doc, 1.0, 0.0)).astype(BF16)
            v_mark = jnp.where(stat, -1.0, 0.0).astype(BF16)
            k_wide = jnp.concatenate([jnp.where(own, key, zero), k_mark], axis=1)
            v_wide = jnp.concatenate([jnp.where(own, value, zero), v_mark], axis=1)
            probs = jnp.exp(dot(k_wide, q_wide, NT))
            grad_scores = (probs * dot(v_wide, g_wide, NT)).astype(BF16)
            grads_v.append(dot(probs.astype(BF16), grad))
            grads_k.append(dot(grad_scores, query))
            grad_q[side] = grad_q[side] + dot(
                key_turned[64 * side : 64 * side + 64], grad_scores
            )
        out_ref[1, part] = jnp.where(lane < 64, grads_k[0], grads_k[1]).astype(BF16)
        out_ref[2, part] = jnp.where(lane < 64, grads_v[0], grads_v[1]).astype(BF16)
    out_ref[0] = (jnp.concatenate(grad_q, axis=0) * 0.125).T.astype(BF16)
    grads = jnp.concatenate([out_ref[0], out_ref[1], out_ref[2]], axis=1)
    keep_and_give(bit_ref[0], dot(normed_ref[...], grads, TN), keep_ref, give_ref)


def attend_backward(
    bit, triple, grad, segment_col, qaug, gaug, normed, shards, first_head, heads, place, room, halves=(), block=512
):
    rows, width = normed.shape
    pairs, first, half = width // LANES, first_head // 2, width // shards // 2
    pair_of = lambda offset: pl.BlockSpec((rows, LANES), lambda p, _: (0, offset + p))
    weight_half = pl.BlockSpec((shards, half, 3 * LANES), lambda p, _: (0, 0, place + p))
    kept = jax.ShapeDtypeStruct((shards, half, room * 3 * LANES), BF16)
    return pl.pallas_call(
        functools.partial(attend_back_kernel, block=block, first_head=first_head),
        grid_spec=pltpu.PrefetchScalarGridSpec(
            num_scalar_prefetch=1,
            grid=(heads // 2,),
            in_specs=[
                pair_of(first),
                pair_of(pairs + first),
                pair_of(2 * pairs + first),
                pair_of(first),
                whole_spec((rows, 1)),
                whole_spec((rows, LANES)),
                whole_spec((rows, LANES)),
                whole_spec((rows, width)),
            ]
            + [pl.BlockSpec(memory_space=pl.ANY)] * len(halves),
            out_specs=[
                pl.BlockSpec((3, rows, LANES), lambda p, _: (0, 0, p)),
                weight_half,
                weight_half,
            ],
        ),
        out_shape=[
            jax.ShapeDtypeStruct((3, rows, heads * 64), BF16),
            kept,
            kept,
        ],
        input_output_aliases={9 + n: 1 + n for n in range(len(halves))},
        compiler_params=params(30),
        cost_estimate=lasting(14),
        name="attend_backward",
    )(bit, triple, triple, triple, grad, segment_col, qaug, gaug, normed, *halves)


def qkv_kernel(tok_ref, gain_ref, *refs):
    weights, (normed_ref, triple_ref) = refs[:-2], refs[-2:]
    rows = tok_ref[...].astype(F32)
    scale = lax.rsqrt(jnp.mean(rows * rows, axis=1, keepdims=True) + EPSILON)
    normed = (rows * scale * gain_ref[...]).astype(BF16)
    normed_ref[...] = normed
    span = triple_ref.shape[1] // len(weights)
    for at, weight in enumerate(weights):
        triple_ref[:, at * span : (at + 1) * span] = dot(normed, weight[...]).astype(BF16)


def qkv(tokens, gain_row, weights, span, block=256):
    rows, width = tokens.shape
    return pl.pallas_call(
        qkv_kernel,
        grid=(rows // block,),
        in_specs=[pl.BlockSpec((block, width), lambda i: (i, 0)), whole_spec((1, width))]
        + [whole_spec((width, span)) for weight in weights],
        out_specs=[
            pl.BlockSpec((block, width), lambda i: (i, 0)),
            pl.BlockSpec((block, 3 * width), lambda i: (i, 0)),
        ],
        out_shape=[
            jax.ShapeDtypeStruct((rows, width), BF16),
            jax.ShapeDtypeStruct((rows, 3 * width), BF16),
        ],
        compiler_params=params(14),
        cost_estimate=lasting(8),
        name="qkv",
    )(tokens, gain_row, *weights)


def project_kernel(tok_ref, att_ref, w_ref, gain_ref, hidden_ref, second_ref):
    hidden = tok_ref[...].astype(F32) + dot(att_ref[...], w_ref[...])
    scale = lax.rsqrt(jnp.mean(hidden * hidden, axis=1, keepdims=True) + EPSILON)
    hidden_ref[...] = hidden
    second_ref[...] = (hidden * scale * gain_ref[...]).astype(BF16)


def project(tokens, attended, out_full, gain_row, block=256):
    rows, width = tokens.shape
    wide = pl.BlockSpec((block, width), lambda i: (i, 0))
    return pl.pallas_call(
        project_kernel,
        grid=(rows // block,),
        in_specs=[wide, wide, whole_spec((width, width)), whole_spec((1, width))],
        out_specs=[wide, wide],
        out_shape=[
            jax.ShapeDtypeStruct((rows, width), F32),
            jax.ShapeDtypeStruct((rows, width), BF16),
        ],
        compiler_params=params(10),
        cost_estimate=lasting(7),
        name="project",
    )(tokens, attended, out_full, gain_row)


def routed_gate(second, router, route_wide, experts):
    logits = dot(second, router)
    lane = lax.broadcasted_iota(jnp.int32, logits.shape, 1)
    logits = jnp.where(lane < experts, logits, MASKED)
    raised = jnp.exp(logits - jnp.max(logits, axis=1, keepdims=True))
    probs = raised / jnp.sum(raised, axis=1, keepdims=True)
    chosen = lane == route_wide
    gate = jnp.sum(jnp.where(chosen, probs, 0.0), axis=1, keepdims=True)
    return probs, chosen, gate


def on_rows(full, run, capacity):
    pl.when(full == 1)(functools.partial(run, capacity))
    pl.when(full == 0)(functools.partial(run, capacity // 2))


def expert_kernel(
    full_ref,
    rows_ref,
    cot_ref,
    route_ref,
    router_ref,
    place_ref,
    w_in_ref,
    w_out_ref,
    act_ref,
    grad_pre_ref,
    x_ref,
    g_ref,
    ret_ref,
    back_a,
    back_b,
    gate_ref,
    produced,
    grad_rows,
    *,
    experts,
):
    ff, expert = pl.program_id(0), pl.program_id(1)
    slots = x_ref.shape[0]
    capacity = slots // full_ref.shape[1]
    half = capacity // 2

    @pl.when((ff == 0) & (expert == 0))
    def _():
        produced[...] = jnp.zeros_like(produced)
        grad_rows[...] = jnp.zeros_like(grad_rows)
        second = rows_ref[...]
        _, _, gate = routed_gate(second, router_ref[...], column_of(route_ref[...]), experts)
        gated = (gate * cot_ref[...].astype(F32)).astype(BF16)

        def pack(start):
            part = slice(start, start + half)
            slot = start + lax.broadcasted_iota(jnp.int32, (half, second.shape[0]), 0)
            pick = jnp.where(slot == place_ref[...], 1.0, 0.0).astype(BF16)
            x_ref[part, :] = dot(pick, second).astype(BF16)
            g_ref[part, :] = dot(pick, gated).astype(BF16)

        for owner in range(slots // capacity):
            pack(owner * capacity)
            pl.when(full_ref[0, owner] == 1)(
                functools.partial(pack, owner * capacity + half)
            )

    def run(rows):
        part = pl.ds(pl.multiple_of(expert * capacity, capacity), rows)
        pre = dot(x_ref[part, :], w_in_ref[0])
        grad_act = dot(g_ref[part, :], w_out_ref[0], NT)
        square = pre * pre
        bend = jnp.tanh(pre * (GELU_C + GELU_C * GELU_A * square))
        upper = 0.5 + 0.5 * bend
        act = (pre * upper).astype(BF16)
        inner = pre * (GELU_C + 3.0 * GELU_C * GELU_A * square)
        slope = upper + inner * (0.5 - 0.5 * bend * bend)
        grad_pre = (grad_act * slope).astype(BF16)
        act_ref[part, :] = act
        grad_pre_ref[part, :] = grad_pre
        produced[part, :] += dot(act, w_out_ref[0])
        grad_rows[part, :] += dot(grad_pre, w_in_ref[0], NT)

    on_rows(full_ref[0, expert], run, capacity)

    @pl.when((ff == pl.num_programs(0) - 1) & (expert == pl.num_programs(1) - 1))
    def _():
        count = ret_ref.shape[0]
        slot = lax.broadcasted_iota(jnp.int32, (count, slots), 1)
        place_col = column_of(place_ref[...])[:, :1]
        pick = jnp.where(slot == place_col, 1.0, 0.0).astype(BF16)
        returned = dot(pick, produced[...].astype(BF16))
        ret_ref[...] = returned.astype(BF16)
        grads = grad_rows[...].astype(BF16)
        back_a[...] = dot(pick[: count // 2], grads).astype(BF16)
        back_b[...] = dot(pick[count // 2 :], grads).astype(BF16)
        inner = jnp.sum(cot_ref[...].astype(F32) * returned, axis=1, keepdims=True)
        gate_ref[...] = jnp.broadcast_to(inner, (count, LANES)).T[:8]


def expert_rows(full, rows, cot, route_row, router, place, w_in, w_out, capacity, experts, ff_block):
    count, width = cot.shape
    local, _, ff = w_in.shape
    slots = local * capacity
    column = lambda f, e, _: (0, f)
    return pl.pallas_call(
        functools.partial(expert_kernel, experts=experts),
        grid_spec=pltpu.PrefetchScalarGridSpec(
            num_scalar_prefetch=1,
            grid=(ff // ff_block, local),
            in_specs=[
                whole_spec((count, width)),
                whole_spec((count, width)),
                whole_spec((1, count)),
                pl.BlockSpec((width, LANES), lambda *_: (0, width // LANES)),
                whole_spec((1, count)),
                pl.BlockSpec((1, width, ff_block), lambda f, e, _: (e, 0, f)),
                pl.BlockSpec((1, ff_block, width), lambda f, e, _: (e, f, 0)),
            ],
            out_specs=[
                pl.BlockSpec((slots, ff_block), column),
                pl.BlockSpec((slots, ff_block), column),
                whole_spec((slots, width)),
                whole_spec((slots, width)),
                whole_spec((count, width)),
                whole_spec((count // 2, width)),
                whole_spec((count // 2, width)),
                whole_spec((8, count)),
            ],
            scratch_shapes=[
                pltpu.VMEM((slots, width), F32),
                pltpu.VMEM((slots, width), F32),
            ],
        ),
        out_shape=[
            jax.ShapeDtypeStruct((slots, ff), BF16),
            jax.ShapeDtypeStruct((slots, ff), BF16),
            jax.ShapeDtypeStruct((slots, width), BF16),
            jax.ShapeDtypeStruct((slots, width), BF16),
            jax.ShapeDtypeStruct((count, width), BF16),
            jax.ShapeDtypeStruct((count // 2, width), BF16),
            jax.ShapeDtypeStruct((count // 2, width), BF16),
            jax.ShapeDtypeStruct((8, count), F32),
        ],
        compiler_params=params(),
        cost_estimate=lasting(28),
        name="expert_rows",
    )(full, rows, cot, route_row, router, place[None, :], w_in, w_out)


def weight_grad_kernel(full_ref, expert_ref, left_a, left_b, right_a, right_b, early_ref, late_ref):
    expert = expert_ref[0]
    capacity = left_a.shape[0]

    def run(rows_a, rows_b):
        total = (
            dot(left_a[:rows_a, :], right_a[:rows_a, :], TN)
            + dot(left_b[:rows_b, :], right_b[:rows_b, :], TN)
        ).astype(BF16)
        early_ref[0] = total[: early_ref.shape[1]]
        late_ref[0] = total[early_ref.shape[1] :]

    for full_a in range(2):
        for full_b in range(2):
            pl.when((full_ref[0, expert] == full_a) & (full_ref[1, expert] == full_b))(
                functools.partial(
                    run, capacity // (2 - full_a), capacity // (2 - full_b)
                )
            )


def early_rows(rows):
    return rows // 3 * 2


def weight_grad(full, expert, left, right, capacity, ff_block):
    slots, width = left[0].shape
    ff = max(width, right[0].shape[1])
    spec = lambda value: (
        pl.BlockSpec((capacity, ff_block), lambda f, _, e: (e[0], f))
        if value.shape[1] == ff
        else pl.BlockSpec(
            (capacity, value.shape[1]), lambda f, _, e: (e[0], 0), pipeline_mode=pl.Buffered(1)
        )
    )
    block = lambda value: ff_block if value.shape[1] == ff else value.shape[1]
    shape = (block(left[0]), block(right[0]))
    counts = (early_rows(shape[0]), shape[0] - early_rows(shape[0]))
    return pl.pallas_call(
        weight_grad_kernel,
        grid_spec=pltpu.PrefetchScalarGridSpec(
            num_scalar_prefetch=2,
            grid=(ff // ff_block,),
            in_specs=[spec(value) for value in (*left, *right)],
            out_specs=[
                pl.BlockSpec((1, count, shape[1]), lambda f, *_: (f, 0, 0)) for count in counts
            ],
        ),
        out_shape=[
            jax.ShapeDtypeStruct((ff // ff_block, count, shape[1]), BF16) for count in counts
        ],
        compiler_params=params(40),
        cost_estimate=lasting(9),
        name="weight_grad",
    )(full, expert, *left, *right)


def hidden_back_kernel(
    bit_ref,
    own_a,
    own_b,
    sent_a,
    sent_b,
    hidden_ref,
    second_ref,
    att_ref,
    cot_ref,
    own_gate,
    sent_gate,
    route_ref,
    router_ref,
    w_ref,
    gain_ref,
    grad_hidden_ref,
    grad_att_ref,
    aug_ref,
    gate_out_ref,
    keep_ref,
    give_ref,
    total,
    router_grad_ref,
    gain_grad_ref,
    *,
    experts,
):
    step, steps = pl.program_id(0), pl.num_programs(0)

    @pl.when(step == 0)
    def _():
        router_grad_ref[...] = jnp.zeros_like(router_grad_ref)
        gain_grad_ref[...] = jnp.zeros_like(gain_grad_ref)
        total[...] = jnp.zeros_like(total)

    early = step < steps // 2
    of = lambda low, high: jnp.where(early, low[...], high[...])
    hidden, second, attended = hidden_ref[...], second_ref[...], att_ref[...]
    cot = cot_ref[...].astype(F32)
    scale = lax.rsqrt(jnp.mean(hidden * hidden, axis=1, keepdims=True) + EPSILON)
    probs, chosen, gate = routed_gate(
        second, router_ref[...], column_of(route_ref[...]), experts
    )
    inner = own_gate[0:1, :] + sent_gate[0:1, :]
    inner = jnp.broadcast_to(inner, (LANES, inner.shape[1])).T
    gate_out_ref[...] = jnp.broadcast_to(gate, gate_out_ref.shape)
    grad_logits = (probs * (jnp.where(chosen, inner, 0.0) - gate * inner)).astype(BF16)
    router_grad_ref[...] += dot(grad_logits, second, TN)
    grad_second = of(own_a, own_b).astype(F32) + of(sent_a, sent_b).astype(F32)
    grad_second = grad_second + dot(grad_logits, router_ref[...], NT)
    scaled_hidden = hidden * scale
    gain_grad_ref[...] += jnp.sum(grad_second * scaled_hidden, axis=0, keepdims=True)
    scaled = grad_second * gain_ref[...]
    mean = jnp.mean(scaled * scaled_hidden, axis=1, keepdims=True)
    grad_hidden = cot + scale * (scaled - scaled_hidden * mean)
    branch = grad_hidden.astype(BF16)
    grad_hidden_ref[...] = grad_hidden
    grad_att = dot(branch, w_ref[...], NT).astype(BF16)
    grad_att_ref[...] = grad_att
    total[...] += dot(attended, branch, TN)
    product = grad_att.astype(F32) * attended.astype(F32)
    rows, width = product.shape
    feature = lax.broadcasted_iota(jnp.int32, (width, LANES), 0)
    lane = lax.broadcasted_iota(jnp.int32, (width, LANES), 1)
    head = (lane & 15) == feature // 64
    collect = jnp.where(head & (lane < 48), 1.0, 0.0).astype(BF16)
    high = product.astype(BF16)
    rest = product - high.astype(F32)
    middle = rest.astype(BF16)
    low = (rest - middle.astype(F32)).astype(BF16)
    stats = dot(high, collect) + dot(middle, collect) + dot(low, collect)
    row_lane = lax.broadcasted_iota(jnp.int32, (rows, LANES), 1)
    aug_ref[...] = jnp.where(row_lane < 48, lane_parts(stats, row_lane), 0.0).astype(BF16)

    @pl.when(step == steps - 1)
    def _():
        keep_and_give(bit_ref[0], total[...], keep_ref, give_ref)
        lane = lax.broadcasted_iota(jnp.int32, (width, LANES), 1)
        gains = jnp.broadcast_to(gain_grad_ref[...], (LANES, width)).T
        small = jnp.where(lane == LANES - 1, gains, router_grad_ref[...].T)
        keep_and_give(bit_ref[0], small, keep_ref, give_ref, width)


def hidden_back(bit, hidden, second, own, sent, att, cot, gates, route_row, out_full, gain, shards, experts, room, block=256):
    rows, width = cot.shape
    steps = rows // block
    half = steps // 2
    part = width // shards // 2
    own_columns = width + 3 * LANES
    here = lambda i, _: (i, 0)
    wide = lambda index: pl.BlockSpec((block, width), index)
    low = wide(lambda i, _: (jnp.minimum(i, half - 1), 0))
    high = wide(lambda i, _: (jnp.maximum(i - half, 0), 0))
    along = lambda height: pl.BlockSpec((height, block), lambda i, _: (0, i))
    return pl.pallas_call(
        functools.partial(hidden_back_kernel, experts=experts),
        grid_spec=pltpu.PrefetchScalarGridSpec(
            num_scalar_prefetch=1,
            grid=(steps,),
            in_specs=[low, high] * 2
            + [wide(here)] * 4
            + [
                along(8),
                along(8),
                along(1),
                pl.BlockSpec((width, LANES), lambda *_: (0, width // LANES)),
                pl.BlockSpec((width, width), lambda *_: (0, 0)),
                whole_spec((1, width)),
            ],
            out_specs=[
                wide(here),
                wide(here),
                pl.BlockSpec((block, LANES), here),
                pl.BlockSpec((block, LANES), here),
                whole_spec((shards, part, own_columns)),
                whole_spec((shards, part, own_columns)),
            ],
            scratch_shapes=[
                pltpu.VMEM((width, width), F32),
                pltpu.VMEM((LANES, width), F32),
                pltpu.VMEM((1, width), F32),
            ],
        ),
        out_shape=[
            jax.ShapeDtypeStruct((rows, width), F32),
            jax.ShapeDtypeStruct((rows, width), BF16),
            jax.ShapeDtypeStruct((rows, LANES), BF16),
            jax.ShapeDtypeStruct((rows, LANES), F32),
            jax.ShapeDtypeStruct((shards, part, room * 3 * LANES), BF16),
            jax.ShapeDtypeStruct((shards, part, room * 3 * LANES), BF16),
        ],
        compiler_params=params(40),
        cost_estimate=lasting(12),
        name="hidden_back",
    )(bit, *own, *sent, hidden, second, att, cot, *gates, route_row, out_full, out_full, gain)


def token_back_kernel(tok_ref, grad_ref, gain_ref, *refs):
    weights, triples, out_ref = refs[:GATHERS], refs[GATHERS:-1], refs[-1]
    rows = tok_ref[...].astype(F32)
    scale = lax.rsqrt(jnp.mean(rows * rows, axis=1, keepdims=True) + EPSILON)
    grads = jnp.concatenate([t[p] for p in range(3) for t in triples], axis=1)
    span = grads.shape[1] // len(weights)
    grad_normed = jnp.zeros(rows.shape, F32)
    for at, weight in enumerate(weights):
        grad_normed += dot(grads[:, at * span : (at + 1) * span], weight[...], NT)
    scaled_rows = rows * scale
    scaled = grad_normed * gain_ref[...]
    mean = jnp.mean(scaled * scaled_rows, axis=1, keepdims=True)
    out_ref[...] = (grad_ref[...] + scale * (scaled - scaled_rows * mean)).astype(BF16)


def token_back(tokens, grad_hidden, grad_triples, weights, gain_row, block=256):
    rows, width = tokens.shape
    here = lambda i: (i, 0)
    return pl.pallas_call(
        token_back_kernel,
        grid=(rows // block,),
        in_specs=[
            pl.BlockSpec((block, width), here),
            pl.BlockSpec((block, width), here),
            whole_spec((1, width)),
        ]
        + [whole_spec((width, 3 * width // len(weights))) for w in weights]
        + [pl.BlockSpec((3, block, t.shape[2]), lambda i: (0, i, 0)) for t in grad_triples],
        out_specs=pl.BlockSpec((block, width), here),
        out_shape=jax.ShapeDtypeStruct((rows, width), BF16),
        compiler_params=params(20),
        cost_estimate=lasting(9),
        name="token_back",
    )(tokens, grad_hidden, gain_row, *weights, *grad_triples)


def swap(value, axis, step=1):
    size = lax.axis_size(axis)
    return lax.ppermute(value, axis, [(i, i ^ step) for i in range(size)])


def bit_of(axis, step):
    return lax.axis_index(axis) // step % 2


def bits(size, first=1):
    return [1 << n for n in range(first.bit_length() - 1, size.bit_length() - 1)]


def rounded(parts):
    return sum(part.astype(F32) for part in parts).astype(BF16)


def exchange(parts, axis, step, pick):
    bit = bit_of(axis, step)
    give = rounded([pick(part, 1 - bit) for part in parts])
    return [pick(part, bit) for part in parts] + [swap(give, axis, step)]


def halve(parts, axis, step):
    def pick(part, bit):
        parted = part.reshape((part.shape[0], 2, part.shape[1] // 2) + part.shape[2:])
        return lax.dynamic_index_in_dim(parted, bit, 1, keepdims=False)

    return exchange(parts, axis, step, pick)


def to_owner(parts, steps):
    def pick(part, bit):
        parted = part.reshape((part.shape[0] // 2, 2) + part.shape[1:])
        return lax.dynamic_index_in_dim(parted, bit, 1, keepdims=False)

    for step in steps:
        parts = exchange(parts, "shard", step, pick)
    return parts


def to_owner_early(parts):
    return to_owner(parts, bits(lax.axis_size("shard"))[:-1])


def to_owner_last(parts):
    return to_owner(parts, bits(lax.axis_size("shard"))[-1:])


def both(parts, axis, step):
    mine = rounded(parts)
    return [mine, swap(mine, axis, step)]


def unhalve(value, axis, step, dim):
    other = swap(value, axis, step)
    first = bit_of(axis, step) == 0
    low = jnp.where(first, value, other)
    high = jnp.where(first, other, value)
    return jnp.concatenate([low, high], axis=dim)


def neighbours(parts):
    return halve(parts, "dp", 1) if lax.axis_size("dp") > 1 else parts


def spread(parts):
    for step in bits(lax.axis_size("dp"), 2):
        parts = halve(parts, "dp", step)
    return parts


def unspread(value):
    for step in reversed(bits(lax.axis_size("dp"), 2)):
        value = unhalve(value, "dp", step, 0)
    return value


def summed(parts):
    for step in bits(lax.axis_size("dp"), 2):
        parts = both(parts, "dp", step)
    return parts


def finish_expert(early, late, local):
    early, late = rounded(early)[0], rounded(late)[0]
    whole = jnp.concatenate([unspread(early), rounded(summed([late]))], axis=0)
    if lax.axis_size("dp") > 1:
        whole = unhalve(whole, "dp", 1, 0)
    return whole.reshape((local, -1) + whole.shape[1:]).astype(F32)


def tie(value, *sums):
    value, *last = lax.optimization_barrier((value,) + tuple(parts[-1] for parts in sums))
    return (value, *(parts[:-1] + [part] for parts, part in zip(sums, last)))


def plane_axes():
    return [(axis, step) for axis, step in (("dp", 2), ("expert", 1)) if lax.axis_size(axis) > step]


def plane_send(value, other):
    sizes = [lax.axis_size("dp"), lax.axis_size("expert")]
    flips = [0, 0]
    for n, (axis, step) in enumerate(plane_axes()):
        flips[axis == "expert"] |= step * (other >> n & 1)
    perm = [
        (d * sizes[1] + e, (d ^ flips[0]) * sizes[1] + (e ^ flips[1]))
        for d in range(sizes[0])
        for e in range(sizes[1])
    ]
    return lax.ppermute(value, ("dp", "expert"), perm)


def plane_index():
    return sum(bit_of(axis, step) << n for n, (axis, step) in enumerate(plane_axes()))


def dense_across(parts):
    count = 1 << len(plane_axes())
    me = plane_index()

    def pick(part, index):
        parted = part.reshape((part.shape[0], count, -1) + part.shape[2:])
        return lax.dynamic_index_in_dim(parted, index, 1, keepdims=False)

    got = [
        plane_send(rounded([pick(part, me ^ other) for part in parts]), other)
        for other in range(1, count)
    ]
    return [pick(part, me) for part in parts] + got


def dense_owner(parts):
    me, count = lax.axis_index("shard"), lax.axis_size("shard")
    pick = lambda part, index: lax.dynamic_index_in_dim(part, index, 0, keepdims=False)
    got = []
    for other in range(1, count):
        give = rounded([pick(part, me ^ other) for part in parts])
        got.append(swap(give, "shard", other))
    return [pick(part, me) for part in parts] + got


def dense_finish(parts):
    for step in bits(lax.axis_size("expert"), 2):
        parts = both(parts, "expert", step)
    for step in bits(lax.axis_size("dp"), 4):
        parts = both(parts, "dp", step)
    mine = rounded(parts)
    count = 1 << len(plane_axes())
    me = plane_index()
    pieces = [mine] + [plane_send(mine, other) for other in range(1, count)]
    rows = []
    for index in range(count):
        row = pieces[0]
        for other in range(1, count):
            row = jnp.where(me ^ index == other, pieces[other], row)
        rows.append(row)
    value = jnp.concatenate(rows, axis=0)
    return unhalve(value, "dp", 1, 0).astype(F32)


def gather_far(value):
    shards, parts = lax.axis_size("shard"), lax.axis_size("dp")
    rows, columns = value.shape
    parted = value.reshape(parts, rows // parts, columns)
    mine = lax.dynamic_index_in_dim(parted, lax.axis_index("dp"), 0, keepdims=False)
    me = lax.axis_index("shard")
    whole = lax.dynamic_update_index_in_dim(
        jnp.zeros((shards,) + mine.shape, value.dtype), mine, me, 0
    )
    for away in range(1, shards):
        piece = lax.ppermute(mine, "shard", [(i, (i + away) % shards) for i in range(shards)])
        whole = lax.dynamic_update_index_in_dim(whole, piece, (me - away) % shards, 0)
    return whole[:, None]


def gather_step(whole, step):
    other = swap(whole, "dp", step)
    first = bit_of("dp", step) == 0
    low, high = jnp.where(first, whole, other), jnp.where(first, other, whole)
    whole = jnp.stack([low, high], axis=2)
    return whole.reshape((whole.shape[0], -1) + whole.shape[3:])


def gather_near(whole, steps):
    for step in steps:
        whole = gather_step(whole, step)
    return whole


def places_of(route_ids, first, local, capacity):
    owned = route_ids - first
    choose = owned[:, None] == jnp.arange(local, dtype=jnp.int32)[None, :]
    rank = jnp.cumsum(choose.astype(jnp.int32), axis=0) - 1
    slot = jnp.sum(jnp.where(choose, rank, 0), axis=1) + owned * capacity
    full = (rank[-1] >= capacity // 2).astype(jnp.int32)
    return jnp.where(jnp.any(choose, axis=1), slot, -1), full


def experts_of_pairs(second, cotangent, routes, out_full, expert_in, expert_out, experts, early):
    rows, width = cotangent.shape
    local, _, ff = expert_in.shape
    capacity = 2 * rows // experts
    ff_block = ff // lax.axis_size("shard")
    other_cot, other_routes = early
    other_second = swap(second, "expert")
    first_own = lax.axis_index("expert") * local
    results, flags = [], []
    for rows_of, cot, route_ids in (
        (second, cotangent, routes),
        (other_second, other_cot, other_routes),
    ):
        place, full = places_of(route_ids, first_own, local, capacity)
        if results:
            rows_of, _ = lax.optimization_barrier((rows_of, results[0][7]))
        results.append(
            expert_rows(
                full[None],
                rows_of,
                cot,
                route_ids[None, :],
                out_full,
                place,
                expert_in,
                expert_out,
                capacity,
                experts,
                ff_block,
            )
        )
        flags.append(full)
    own, other = results
    full = jnp.stack(flags)
    keep = bit_of("dp", 1)
    one = lambda expert: expert[None].astype(jnp.int32)
    grad = lambda expert, left, right: weight_grad(
        full, one(expert), left, right, capacity, ff_block
    )
    acts, grads = (own[0], other[0]), (own[3], other[3])
    xs, grad_pres = (own[2], other[2]), (own[1], other[1])
    back_a = swap(other[5], "expert")
    sent_gate = swap(other[7], "expert")
    out_give = grad(1 - keep, acts, grads)
    full, *out_give = lax.optimization_barrier((full, *out_give))
    out_keep = grad(keep, acts, grads)
    full, back_a, sent_gate, back_b, *out_both = lax.optimization_barrier(
        (full, back_a, sent_gate, other[6], *out_keep, *out_give)
    )
    back_b = swap(back_b, "expert")
    out_keep, out_sent = out_both[:2], [swap(part, "dp") for part in out_both[2:]]
    in_give = grad(1 - keep, xs, grad_pres)
    full, *out_sent = lax.optimization_barrier((full, *out_sent, *in_give))
    out_sent, in_give = out_sent[:2], out_sent[2:]
    in_sent = [swap(part, "dp") for part in in_give]
    out_early = spread([out_keep[0], out_sent[0]])
    out_late = to_owner_early([out_keep[1], out_sent[1]])
    in_keep = grad(keep, xs, grad_pres)
    gate, *in_keep = lax.optimization_barrier((own[7], *in_keep))
    in_near = tuple([mine, sent] for mine, sent in zip(in_keep, in_sent))
    return (own[4], other[4]), (own[5:7], (back_a, back_b)), (gate, sent_gate), in_near, (out_early, out_late)


def experts_of_many(second, cotangent, route_ids, router, expert_in, expert_out):
    tok_rows, width = second.shape
    experts_all = router.shape[1]
    local, _, ff = expert_in.shape
    groups = lax.axis_size("expert")
    shards = lax.axis_size("shard")
    capacity = 2 * tok_rows // experts_all
    choose = route_ids[:, None] == jnp.arange(experts_all, dtype=jnp.int32)[None, :]
    rank = jnp.cumsum(choose.astype(jnp.int32), axis=0) - 1
    slot_index = route_ids * capacity + jnp.sum(jnp.where(choose, rank, 0), axis=1)
    probs = jax.nn.softmax(dot(second, router), axis=-1)
    gate = jnp.sum(jnp.where(choose, probs, 0.0), axis=1)

    def across(value):
        return lax.all_to_all(value, "expert", split_axis=0, concat_axis=0, tiled=True)

    def to_slots(token_rows):
        filled = jnp.zeros((experts_all * capacity, width), token_rows.dtype)
        filled = filled.at[slot_index].set(token_rows)
        return across(filled.reshape(groups, local, capacity, width))

    def from_slots(value):
        return across(value).reshape(experts_all * capacity, width)[slot_index]

    def einsum(form, left, right):
        return jnp.einsum(form, left, right, preferred_element_type=F32)

    def gelu(value):
        return jax.nn.gelu(value, approximate=True)

    grad_out = cotangent.astype(F32)
    arrived = to_slots(second)
    pre_act, pull = jax.vjp(gelu, einsum("aecd,edf->aecf", arrived, expert_in))
    activated = pre_act.astype(BF16)
    produced = einsum("aecf,efd->aecd", activated, expert_out).astype(BF16)
    returned = from_slots(produced)
    inner = jnp.sum(grad_out * returned.astype(F32), axis=1)
    grad_arrived = to_slots((gate[:, None] * grad_out).astype(BF16))
    grad_act = einsum("aecd,efd->aecf", grad_arrived, expert_out)
    grad_pre = pull(grad_act)[0].astype(BF16)
    grad_w_out = einsum("aecf,aecd->efd", activated, grad_arrived).astype(BF16)
    grad_w_in = einsum("aecd,aecf->edf", arrived, grad_pre).astype(BF16)
    back = from_slots(einsum("aecf,edf->aecd", grad_pre, expert_in).astype(BF16))
    grad_w_in = grad_w_in.reshape(local, width, shards, ff // shards).transpose(2, 0, 1, 3)
    grad_w_out = grad_w_out.reshape(local, shards, ff // shards, width).transpose(1, 0, 2, 3)
    def near(value):
        parts = neighbours([value.reshape((shards, -1) + value.shape[3:])])
        cut = early_rows(parts[0].shape[1])
        return [part[:, :cut] for part in parts], [part[:, cut:] for part in parts]

    out_early, out_late = near(grad_w_out)
    back = jnp.split(back, 2, axis=0)
    nothing = [jnp.zeros_like(part) for part in back]
    inner = jnp.broadcast_to(inner[None, :], (8, tok_rows))
    return (
        (returned, jnp.zeros_like(returned)),
        (back, nothing),
        (inner, jnp.zeros_like(inner)),
        near(grad_w_in),
        (spread(out_early), to_owner_early(out_late)),
    )


def body(
    tokens,
    segments,
    routes,
    cotangent,
    attn_in,
    attn_out,
    router,
    gain_one,
    gain_two,
    expert_in,
    expert_out,
):
    rows, width = tokens.shape
    experts = router.shape[1]
    local = expert_in.shape[0]
    lanes_of = lambda value: jnp.pad(value[:, None], ((0, 0), (0, LANES - 1)))
    padded = lambda value: jnp.pad(value, ((0, 0), (0, LANES - experts)))
    segment_col = segments[0][:, None]
    route_ids = routes.reshape(rows)
    bit = bit_of("dp", 1)[None].astype(jnp.int32)
    shards = lax.axis_size("shard")
    pairs_only = lax.axis_size("expert") == local == 2
    early = None

    span = 3 * width // GATHERS
    pieces = [attn_in[:, g * span : (g + 1) * span] for g in range(GATHERS)]
    pieces[0] = jnp.concatenate([pieces[0], lanes_of(gain_one)], axis=1)
    shares = [gather_far(piece) for piece in pieces]
    source = jnp.concatenate([attn_out, padded(router), lanes_of(gain_two)], axis=1)
    source, *shares = lax.optimization_barrier((source, *shares))
    near_steps = bits(lax.axis_size("dp"))[::-1]
    join = lambda whole: whole.reshape(-1, whole.shape[-1])
    weights = [join(gather_near(share, near_steps)) for share in shares]
    share = gather_far(source)
    first_gain = weights[0][:, span].astype(F32)[None, :]
    share, *weights = lax.optimization_barrier((share, *weights))
    share = gather_near(share, near_steps[:-1])
    if pairs_only:
        early = (swap(cotangent, "expert"), swap(route_ids, "expert"))

    normed, triple = qkv(tokens, first_gain, weights, span)
    triple, share = lax.optimization_barrier((triple, share))
    out_full = join(gather_near(share, near_steps[-1:]))
    second_gain = out_full[:, width + LANES].astype(F32)[None, :]
    attended, qaug = attend_forward(triple, segment_col)
    hidden, second = project(tokens, attended, out_full, second_gain)
    if pairs_only:
        done = experts_of_pairs(
            second, cotangent, route_ids, out_full, expert_in, expert_out, experts, early
        )
    else:
        full_router = out_full[:, width : width + experts]
        done = experts_of_many(
            second, cotangent, route_ids, full_router, expert_in, expert_out
        )
    returned, (own_back, sent_back), inner, in_near, (out_early, out_late) = done

    in_early, in_late = in_near
    gate, out_late, in_early, in_late = tie(inner[0], out_late, in_early, in_late)
    out_late = to_owner_last(out_late)
    in_late = to_owner_early(in_late)
    heads = width // 64 // GROUPS
    pieces = heads // 2
    rooms = (width // LANES // 3 + 1 + pieces, (GROUPS - 1) * pieces)
    grad_hidden, grad_att, gaug, gates, *dense_a = hidden_back(
        bit,
        hidden,
        second,
        own_back,
        sent_back,
        attended,
        cotangent,
        (gate, inner[1]),
        route_ids[None, :],
        out_full,
        second_gain,
        shards,
        experts,
        rooms[0],
    )

    def back(grad, group, place, room, halves=()):
        return attend_backward(
            bit, triple, grad, segment_col, qaug, gaug, normed, shards, group * heads, heads, place, room, halves
        )

    grad_att, out_early, in_late, (made,) = tie(grad_att, out_early, in_late, [returned[1]])
    made = swap(made, "expert") if pairs_only else made
    out_early = to_owner_early(out_early)
    in_early = spread(in_early)
    grads_0, *dense_a = back(grad_att, 0, rooms[0] - pieces, rooms[0], dense_a)

    grad_att, out_early, out_late, *dense_a = tie(grad_att, out_early, out_late, *([d] for d in (*dense_a, grads_0)))
    (keep_a,), (give_a,), (grads_0,) = dense_a
    dense_a = [keep_a, swap(give_a, "dp")]
    out_early = to_owner_last(out_early)
    in_late = to_owner_last(in_late)
    grads_1, *dense_b = back(grad_att, 1, 0, rooms[1])

    grad_att, in_early, dense_a, (grads_1,) = tie(grad_att, in_early, dense_a, [grads_1])
    in_early = to_owner_early(in_early)
    dense_a = dense_across(dense_a)
    grads_2, *dense_b = back(grad_att, 2, pieces, rooms[1], dense_b)
    dense_b = [dense_b[0], swap(dense_b[1], "dp")]

    grad_hidden, in_early, out_early, in_late, dense_a, (grads_2,) = tie(
        grad_hidden, in_early, out_early, in_late, dense_a, [grads_2]
    )
    in_early = to_owner_last(in_early)
    final_out = finish_expert(out_early, out_late, local)
    dense_a = dense_owner(dense_a)
    grad_tokens = token_back(
        tokens, grad_hidden, (grads_0, grads_1, grads_2), weights, first_gain
    )
    dense_b = dense_across(dense_b)
    dense_a = dense_finish(dense_a)
    dense_b = dense_finish(dense_owner(dense_b))
    final_in = finish_expert(in_early, in_late, local)

    start = width + 3 * LANES
    pair_columns = lambda value, start: [
        value[:, c : c + LANES] for c in range(start, value.shape[1], LANES)
    ]
    columns = pair_columns(dense_a, start) + pair_columns(dense_b, 0)
    grad_attn_in = jnp.concatenate(columns[0::3] + columns[1::3] + columns[2::3], axis=1)
    grad_gain_one = jnp.sum(attn_in.astype(F32) * grad_attn_in, axis=1) / gain_one.astype(F32)

    wide = returned[0].astype(F32) + made.astype(F32)
    layer = hidden + gates[:, :1] * wide
    return (
        layer.astype(BF16),
        grad_tokens,
        grad_attn_in,
        dense_a[:, :width],
        dense_a[:, width : width + experts],
        grad_gain_one,
        dense_a[:, width + LANES - 1],
        final_in,
        final_out,
    )


def solution(mesh):
    everywhere = P(("dp", "expert", "shard"), None)
    placed = (everywhere,) * 4 + (P("shard", None),) * 3 + (P("shard"),) * 2
    placed = placed + (P("expert", None, None),) * 2
    outs = (everywhere,) * 2 + (P("shard", None),) * 3 + (P("shard"),) * 2
    outs = outs + (P("expert", None, "shard"), P("expert", "shard", None))
    return jax.shard_map(
        body, mesh=mesh, in_specs=placed, out_specs=outs, check_vma=False
    )
```

```python
import functools
import math

import jax
import jax.numpy as jnp
from jax import lax
from jax.experimental import pallas as pl
from jax.experimental.pallas import tpu as pltpu
from jax.sharding import PartitionSpec as P

HEADS = 12
LANES = 128
EPSILON = 1e-06
MASKED = -1e30
BF16 = jnp.bfloat16
F32 = jnp.float32
NN = (((1,), (0,)), ((), ()))
NT = (((1,), (1,)), ((), ()))
TN = (((0,), (0,)), ((), ()))
GROUPS = 3
GATHERS = 2
SHARE = 0.05
GELU_C = math.sqrt(2.0 / math.pi)
GELU_A = 0.044715


def dot(left, right, dims=NN):
    return lax.dot_general(left, right, dims, preferred_element_type=F32)


def column_of(row):
    wide = jnp.broadcast_to(row.astype(F32), (LANES, row.shape[1]))
    return wide.T.astype(jnp.int32)


def params(mebibytes=60):
    return pltpu.CompilerParams(vmem_limit_bytes=mebibytes << 20)


def lasting(microseconds):
    return pl.CostEstimate(
        flops=int(microseconds * SHARE * 1.15e9), bytes_accessed=0, transcendentals=0
    )


def whole_spec(shape, buffers=1):
    return pl.BlockSpec(
        shape, lambda *_: (0,) * len(shape), pipeline_mode=pl.Buffered(buffers)
    )


def lane_parts(value, lane):
    high = value.astype(BF16).astype(F32)
    middle = (value - high).astype(BF16).astype(F32)
    low = value - high - middle
    return jnp.where(lane < 16, high, jnp.where(lane < 32, middle, low))


def attend_kernel(q_ref, k_ref, v_ref, seg_ref, out_ref, qaug_ref, lse_ref, *, block):
    pair, pairs = pl.program_id(0), pl.num_programs(0)
    rows, keys = q_ref.shape[0], k_ref.shape[0]
    lane_k = lax.broadcasted_iota(jnp.int32, (keys, LANES), 1)
    lane_q = lax.broadcasted_iota(jnp.int32, (rows, LANES), 1)
    k_mark = jnp.where((lane_k - 48) == seg_ref[...], 1.0, 0.0).astype(BF16)
    zone = (lane_q >= 48) & (lane_q < 56)
    q_mark = jnp.where(zone & ((lane_q - 48) != seg_ref[...]), MASKED, 0.0)

    @pl.when(pair == 0)
    def _():
        lse_ref[...] = jnp.zeros_like(lse_ref)

    k_mark = jnp.where((lane_k >= 48) & (lane_k < 56), k_mark, jnp.asarray(0, BF16))
    k_wide = jnp.concatenate([k_ref[...], k_mark], axis=1)
    v_wide = jnp.concatenate([v_ref[...], jnp.ones((keys, LANES), BF16)], axis=1)
    lane = lane_q[:block]
    for start in range(0, rows, block):
        part = slice(start, start + block)
        query = q_ref[part] * jnp.asarray(0.125, BF16)
        outs = []
        stats = lse_ref[part]
        for side in range(2):
            own = (lane >= 64) if side else (lane < 64)
            picked = jnp.where(own, query, jnp.asarray(0, BF16))
            scores = dot(
                jnp.concatenate([picked, q_mark[part].astype(BF16)], axis=1), k_wide, NT
            )
            row_max = jnp.max(scores, axis=1, keepdims=True)
            raised = jnp.exp(scores - row_max).astype(BF16)
            summed = dot(raised, v_wide)
            total = summed[:, LANES:]
            outs.append(summed[:, :LANES] / total)
            mine = ((lane & 15) == 2 * pair + side) & (lane < 48)
            stats = jnp.where(mine, row_max + jnp.log(total), stats)
        out_ref[part] = jnp.where(lane < 64, outs[0], outs[1]).astype(BF16)
        lse_ref[part] = stats

    @pl.when(pair == pairs - 1)
    def _():
        stats = lane_parts(lse_ref[...], lane_q)
        qaug_ref[...] = jnp.where(lane_q < 48, stats, q_mark).astype(BF16)


def attend_forward(triple, segment_col, block=256):
    rows, width = triple.shape[0], triple.shape[1] // 3
    pairs = width // LANES
    return pl.pallas_call(
        functools.partial(attend_kernel, block=block),
        grid=(pairs,),
        in_specs=[
            pl.BlockSpec((rows, LANES), lambda p: (0, p)),
            pl.BlockSpec((rows, LANES), lambda p: (0, pairs + p)),
            pl.BlockSpec((rows, LANES), lambda p: (0, 2 * pairs + p)),
            whole_spec((rows, 1)),
        ],
        out_specs=[
            pl.BlockSpec((rows, LANES), lambda p: (0, p)),
            pl.BlockSpec((rows, LANES), lambda p: (0, 0)),
        ],
        out_shape=[
            jax.ShapeDtypeStruct((rows, width), BF16),
            jax.ShapeDtypeStruct((rows, LANES), BF16),
        ],
        scratch_shapes=[pltpu.VMEM((rows, LANES), F32)],
        compiler_params=params(60),
        cost_estimate=lasting(24),
        name="attend_forward",
    )(triple, triple, triple, segment_col)


def keep_and_give(bit, result, keep_ref, give_ref, start=0):
    shards, half = keep_ref.shape[0], keep_ref.shape[1]
    result = result.astype(BF16)
    part = slice(start, start + result.shape[1])
    for shard in range(shards):
        low = result[2 * half * shard : 2 * half * shard + half]
        high = result[2 * half * shard + half : 2 * half * shard + 2 * half]
        keep_ref[shard, :, part] = jnp.where(bit == 0, low, high)
        give_ref[shard, :, part] = jnp.where(bit == 0, high, low)


def attend_back_kernel(
    bit_ref,
    q_ref,
    k_ref,
    v_ref,
    g_ref,
    seg_ref,
    qaug_ref,
    gaug_ref,
    normed_ref,
    *refs,
    block,
    first_head,
):
    out_ref, keep_ref, give_ref = refs[-3:]
    pair = pl.program_id(0)
    rows = q_ref.shape[0]
    lane = lax.broadcasted_iota(jnp.int32, (block, LANES), 1)
    zero = jnp.asarray(0, BF16)
    query = q_ref[...] * jnp.asarray(0.125, BF16)
    grad = g_ref[...]
    q_wide = jnp.concatenate([query, qaug_ref[...]], axis=1)
    g_wide = jnp.concatenate([grad, gaug_ref[...]], axis=1)
    zone = (lane >= 48) & (lane < 56)
    grad_q = [jnp.zeros((64, rows), F32), jnp.zeros((64, rows), F32)]
    for start in range(0, rows, block):
        part = slice(start, start + block)
        key, value = k_ref[part], v_ref[part]
        key_turned = key.T
        doc = zone & ((lane - 48) == seg_ref[part])
        grads_k, grads_v = [], []
        for side in range(2):
            own = (lane >= 64) if side else (lane < 64)
            stat = ((lane & 15) == first_head + 2 * pair + side) & (lane < 48)
            k_mark = jnp.where(stat, -1.0, jnp.where(doc, 1.0, 0.0)).astype(BF16)
            v_mark = jnp.where(stat, -1.0, 0.0).astype(BF16)
            k_wide = jnp.concatenate([jnp.where(own, key, zero), k_mark], axis=1)
            v_wide = jnp.concatenate([jnp.where(own, value, zero), v_mark], axis=1)
            probs = jnp.exp(dot(k_wide, q_wide, NT))
            grad_scores = (probs * dot(v_wide, g_wide, NT)).astype(BF16)
            grads_v.append(dot(probs.astype(BF16), grad))
            grads_k.append(dot(grad_scores, query))
            grad_q[side] = grad_q[side] + dot(
                key_turned[64 * side : 64 * side + 64], grad_scores
            )
        out_ref[1, part] = jnp.where(lane < 64, grads_k[0], grads_k[1]).astype(BF16)
        out_ref[2, part] = jnp.where(lane < 64, grads_v[0], grads_v[1]).astype(BF16)
    out_ref[0] = (jnp.concatenate(grad_q, axis=0) * 0.125).T.astype(BF16)
    grads = jnp.concatenate([out_ref[0], out_ref[1], out_ref[2]], axis=1)
    keep_and_give(bit_ref[0], dot(normed_ref[...], grads, TN), keep_ref, give_ref)


def attend_backward(
    bit, triple, grad, segment_col, qaug, gaug, normed, shards, first_head, heads, place, room, halves=(), block=512
):
    rows, width = normed.shape
    pairs, first, half = width // LANES, first_head // 2, width // shards // 2
    pair_of = lambda offset: pl.BlockSpec((rows, LANES), lambda p, _: (0, offset + p))
    weight_half = pl.BlockSpec((shards, half, 3 * LANES), lambda p, _: (0, 0, place + p))
    kept = jax.ShapeDtypeStruct((shards, half, room * 3 * LANES), BF16)
    return pl.pallas_call(
        functools.partial(attend_back_kernel, block=block, first_head=first_head),
        grid_spec=pltpu.PrefetchScalarGridSpec(
            num_scalar_prefetch=1,
            grid=(heads // 2,),
            in_specs=[
                pair_of(first),
                pair_of(pairs + first),
                pair_of(2 * pairs + first),
                pair_of(first),
                whole_spec((rows, 1)),
                whole_spec((rows, LANES)),
                whole_spec((rows, LANES)),
                whole_spec((rows, width)),
            ]
            + [pl.BlockSpec(memory_space=pl.ANY)] * len(halves),
            out_specs=[
                pl.BlockSpec((3, rows, LANES), lambda p, _: (0, 0, p)),
                weight_half,
                weight_half,
            ],
        ),
        out_shape=[
            jax.ShapeDtypeStruct((3, rows, heads * 64), BF16),
            kept,
            kept,
        ],
        input_output_aliases={9 + n: 1 + n for n in range(len(halves))},
        compiler_params=params(30),
        cost_estimate=lasting(14),
        name="attend_backward",
    )(bit, triple, triple, triple, grad, segment_col, qaug, gaug, normed, *halves)


def qkv_kernel(tok_ref, gain_ref, *refs):
    weights, (normed_ref, triple_ref) = refs[:-2], refs[-2:]
    rows = tok_ref[...].astype(F32)
    scale = lax.rsqrt(jnp.mean(rows * rows, axis=1, keepdims=True) + EPSILON)
    normed = (rows * scale * gain_ref[...]).astype(BF16)
    normed_ref[...] = normed
    span = triple_ref.shape[1] // len(weights)
    for at, weight in enumerate(weights):
        triple_ref[:, at * span : (at + 1) * span] = dot(normed, weight[...]).astype(BF16)


def qkv(tokens, gain_row, weights, span, block=256):
    rows, width = tokens.shape
    return pl.pallas_call(
        qkv_kernel,
        grid=(rows // block,),
        in_specs=[pl.BlockSpec((block, width), lambda i: (i, 0)), whole_spec((1, width))]
        + [whole_spec((width, span)) for weight in weights],
        out_specs=[
            pl.BlockSpec((block, width), lambda i: (i, 0)),
            pl.BlockSpec((block, 3 * width), lambda i: (i, 0)),
        ],
        out_shape=[
            jax.ShapeDtypeStruct((rows, width), BF16),
            jax.ShapeDtypeStruct((rows, 3 * width), BF16),
        ],
        compiler_params=params(14),
        cost_estimate=lasting(8),
        name="qkv",
    )(tokens, gain_row, *weights)


def project_kernel(tok_ref, att_ref, w_ref, gain_ref, hidden_ref, second_ref):
    hidden = tok_ref[...].astype(F32) + dot(att_ref[...], w_ref[...])
    scale = lax.rsqrt(jnp.mean(hidden * hidden, axis=1, keepdims=True) + EPSILON)
    hidden_ref[...] = hidden
    second_ref[...] = (hidden * scale * gain_ref[...]).astype(BF16)


def project(tokens, attended, out_full, gain_row, block=256):
    rows, width = tokens.shape
    wide = pl.BlockSpec((block, width), lambda i: (i, 0))
    return pl.pallas_call(
        project_kernel,
        grid=(rows // block,),
        in_specs=[wide, wide, whole_spec((width, width)), whole_spec((1, width))],
        out_specs=[wide, wide],
        out_shape=[
            jax.ShapeDtypeStruct((rows, width), F32),
            jax.ShapeDtypeStruct((rows, width), BF16),
        ],
        compiler_params=params(10),
        cost_estimate=lasting(7),
        name="project",
    )(tokens, attended, out_full, gain_row)


def routed_gate(second, router, route_wide, experts):
    logits = dot(second, router)
    lane = lax.broadcasted_iota(jnp.int32, logits.shape, 1)
    logits = jnp.where(lane < experts, logits, MASKED)
    raised = jnp.exp(logits - jnp.max(logits, axis=1, keepdims=True))
    probs = raised / jnp.sum(raised, axis=1, keepdims=True)
    chosen = lane == route_wide
    gate = jnp.sum(jnp.where(chosen, probs, 0.0), axis=1, keepdims=True)
    return probs, chosen, gate


def on_rows(full, run, capacity):
    pl.when(full == 1)(functools.partial(run, capacity))
    pl.when(full == 0)(functools.partial(run, capacity // 2))


def expert_kernel(
    full_ref,
    rows_ref,
    cot_ref,
    route_ref,
    router_ref,
    place_ref,
    w_in_ref,
    w_out_ref,
    act_ref,
    grad_pre_ref,
    x_ref,
    g_ref,
    ret_ref,
    back_a,
    back_b,
    gate_ref,
    produced,
    grad_rows,
    *,
    experts,
):
    ff, expert = pl.program_id(0), pl.program_id(1)
    slots = x_ref.shape[0]
    capacity = slots // full_ref.shape[1]
    half = capacity // 2

    @pl.when((ff == 0) & (expert == 0))
    def _():
        produced[...] = jnp.zeros_like(produced)
        grad_rows[...] = jnp.zeros_like(grad_rows)
        second = rows_ref[...]
        _, _, gate = routed_gate(second, router_ref[...], column_of(route_ref[...]), experts)
        gated = (gate * cot_ref[...].astype(F32)).astype(BF16)

        def pack(start):
            part = slice(start, start + half)
            slot = start + lax.broadcasted_iota(jnp.int32, (half, second.shape[0]), 0)
            pick = jnp.where(slot == place_ref[...], 1.0, 0.0).astype(BF16)
            x_ref[part, :] = dot(pick, second).astype(BF16)
            g_ref[part, :] = dot(pick, gated).astype(BF16)

        for owner in range(slots // capacity):
            pack(owner * capacity)
            pl.when(full_ref[0, owner] == 1)(
                functools.partial(pack, owner * capacity + half)
            )

    def run(rows):
        part = pl.ds(pl.multiple_of(expert * capacity, capacity), rows)
        pre = dot(x_ref[part, :], w_in_ref[0])
        grad_act = dot(g_ref[part, :], w_out_ref[0], NT)
        square = pre * pre
        bend = jnp.tanh(pre * (GELU_C + GELU_C * GELU_A * square))
        upper = 0.5 + 0.5 * bend
        act = (pre * upper).astype(BF16)
        inner = pre * (GELU_C + 3.0 * GELU_C * GELU_A * square)
        slope = upper + inner * (0.5 - 0.5 * bend * bend)
        grad_pre = (grad_act * slope).astype(BF16)
        act_ref[part, :] = act
        grad_pre_ref[part, :] = grad_pre
        produced[part, :] += dot(act, w_out_ref[0])
        grad_rows[part, :] += dot(grad_pre, w_in_ref[0], NT)

    on_rows(full_ref[0, expert], run, capacity)

    @pl.when((ff == pl.num_programs(0) - 1) & (expert == pl.num_programs(1) - 1))
    def _():
        count = ret_ref.shape[0]
        slot = lax.broadcasted_iota(jnp.int32, (count, slots), 1)
        place_col = column_of(place_ref[...])[:, :1]
        pick = jnp.where(slot == place_col, 1.0, 0.0).astype(BF16)
        returned = dot(pick, produced[...].astype(BF16))
        ret_ref[...] = returned.astype(BF16)
        grads = grad_rows[...].astype(BF16)
        back_a[...] = dot(pick[: count // 2], grads).astype(BF16)
        back_b[...] = dot(pick[count // 2 :], grads).astype(BF16)
        inner = jnp.sum(cot_ref[...].astype(F32) * returned, axis=1, keepdims=True)
        gate_ref[...] = jnp.broadcast_to(inner, (count, LANES)).T[:8]


def expert_rows(full, rows, cot, route_row, router, place, w_in, w_out, capacity, experts, ff_block):
    count, width = cot.shape
    local, _, ff = w_in.shape
    slots = local * capacity
    column = lambda f, e, _: (0, f)
    return pl.pallas_call(
        functools.partial(expert_kernel, experts=experts),
        grid_spec=pltpu.PrefetchScalarGridSpec(
            num_scalar_prefetch=1,
            grid=(ff // ff_block, local),
            in_specs=[
                whole_spec((count, width)),
                whole_spec((count, width)),
                whole_spec((1, count)),
                pl.BlockSpec((width, LANES), lambda *_: (0, width // LANES)),
                whole_spec((1, count)),
                pl.BlockSpec((1, width, ff_block), lambda f, e, _: (e, 0, f)),
                pl.BlockSpec((1, ff_block, width), lambda f, e, _: (e, f, 0)),
            ],
            out_specs=[
                pl.BlockSpec((slots, ff_block), column),
                pl.BlockSpec((slots, ff_block), column),
                whole_spec((slots, width)),
                whole_spec((slots, width)),
                whole_spec((count, width)),
                whole_spec((count // 2, width)),
                whole_spec((count // 2, width)),
                whole_spec((8, count)),
            ],
            scratch_shapes=[
                pltpu.VMEM((slots, width), F32),
                pltpu.VMEM((slots, width), F32),
            ],
        ),
        out_shape=[
            jax.ShapeDtypeStruct((slots, ff), BF16),
            jax.ShapeDtypeStruct((slots, ff), BF16),
            jax.ShapeDtypeStruct((slots, width), BF16),
            jax.ShapeDtypeStruct((slots, width), BF16),
            jax.ShapeDtypeStruct((count, width), BF16),
            jax.ShapeDtypeStruct((count // 2, width), BF16),
            jax.ShapeDtypeStruct((count // 2, width), BF16),
            jax.ShapeDtypeStruct((8, count), F32),
        ],
        compiler_params=params(),
        cost_estimate=lasting(28),
        name="expert_rows",
    )(full, rows, cot, route_row, router, place[None, :], w_in, w_out)


def weight_grad_kernel(full_ref, expert_ref, left_a, left_b, right_a, right_b, early_ref, late_ref):
    expert = expert_ref[0]
    capacity = left_a.shape[0]

    def run(rows_a, rows_b):
        total = (
            dot(left_a[:rows_a, :], right_a[:rows_a, :], TN)
            + dot(left_b[:rows_b, :], right_b[:rows_b, :], TN)
        ).astype(BF16)
        early_ref[0] = total[: early_ref.shape[1]]
        late_ref[0] = total[early_ref.shape[1] :]

    for full_a in range(2):
        for full_b in range(2):
            pl.when((full_ref[0, expert] == full_a) & (full_ref[1, expert] == full_b))(
                functools.partial(
                    run, capacity // (2 - full_a), capacity // (2 - full_b)
                )
            )


def early_rows(rows):
    return rows // 3 * 2


def weight_grad(full, expert, left, right, capacity, ff_block):
    slots, width = left[0].shape
    ff = max(width, right[0].shape[1])
    spec = lambda value: (
        pl.BlockSpec((capacity, ff_block), lambda f, _, e: (e[0], f))
        if value.shape[1] == ff
        else pl.BlockSpec(
            (capacity, value.shape[1]), lambda f, _, e: (e[0], 0), pipeline_mode=pl.Buffered(1)
        )
    )
    block = lambda value: ff_block if value.shape[1] == ff else value.shape[1]
    shape = (block(left[0]), block(right[0]))
    counts = (early_rows(shape[0]), shape[0] - early_rows(shape[0]))
    return pl.pallas_call(
        weight_grad_kernel,
        grid_spec=pltpu.PrefetchScalarGridSpec(
            num_scalar_prefetch=2,
            grid=(ff // ff_block,),
            in_specs=[spec(value) for value in (*left, *right)],
            out_specs=[
                pl.BlockSpec((1, count, shape[1]), lambda f, *_: (f, 0, 0)) for count in counts
            ],
        ),
        out_shape=[
            jax.ShapeDtypeStruct((ff // ff_block, count, shape[1]), BF16) for count in counts
        ],
        compiler_params=params(40),
        cost_estimate=lasting(9),
        name="weight_grad",
    )(full, expert, *left, *right)


def hidden_back_kernel(
    bit_ref,
    own_a,
    own_b,
    sent_a,
    sent_b,
    hidden_ref,
    second_ref,
    att_ref,
    cot_ref,
    own_gate,
    sent_gate,
    route_ref,
    router_ref,
    w_ref,
    gain_ref,
    grad_hidden_ref,
    grad_att_ref,
    aug_ref,
    gate_out_ref,
    keep_ref,
    give_ref,
    total,
    router_grad_ref,
    gain_grad_ref,
    *,
    experts,
):
    step, steps = pl.program_id(0), pl.num_programs(0)

    @pl.when(step == 0)
    def _():
        router_grad_ref[...] = jnp.zeros_like(router_grad_ref)
        gain_grad_ref[...] = jnp.zeros_like(gain_grad_ref)
        total[...] = jnp.zeros_like(total)

    early = step < steps // 2
    of = lambda low, high: jnp.where(early, low[...], high[...])
    hidden, second, attended = hidden_ref[...], second_ref[...], att_ref[...]
    cot = cot_ref[...].astype(F32)
    scale = lax.rsqrt(jnp.mean(hidden * hidden, axis=1, keepdims=True) + EPSILON)
    probs, chosen, gate = routed_gate(
        second, router_ref[...], column_of(route_ref[...]), experts
    )
    inner = own_gate[0:1, :] + sent_gate[0:1, :]
    inner = jnp.broadcast_to(inner, (LANES, inner.shape[1])).T
    gate_out_ref[...] = jnp.broadcast_to(gate, gate_out_ref.shape)
    grad_logits = (probs * (jnp.where(chosen, inner, 0.0) - gate * inner)).astype(BF16)
    router_grad_ref[...] += dot(grad_logits, second, TN)
    grad_second = of(own_a, own_b).astype(F32) + of(sent_a, sent_b).astype(F32)
    grad_second = grad_second + dot(grad_logits, router_ref[...], NT)
    scaled_hidden = hidden * scale
    gain_grad_ref[...] += jnp.sum(grad_second * scaled_hidden, axis=0, keepdims=True)
    scaled = grad_second * gain_ref[...]
    mean = jnp.mean(scaled * scaled_hidden, axis=1, keepdims=True)
    grad_hidden = cot + scale * (scaled - scaled_hidden * mean)
    branch = grad_hidden.astype(BF16)
    grad_hidden_ref[...] = grad_hidden
    grad_att = dot(branch, w_ref[...], NT).astype(BF16)
    grad_att_ref[...] = grad_att
    total[...] += dot(attended, branch, TN)
    product = grad_att.astype(F32) * attended.astype(F32)
    rows, width = product.shape
    feature = lax.broadcasted_iota(jnp.int32, (width, LANES), 0)
    lane = lax.broadcasted_iota(jnp.int32, (width, LANES), 1)
    head = (lane & 15) == feature // 64
    collect = jnp.where(head & (lane < 48), 1.0, 0.0).astype(BF16)
    high = product.astype(BF16)
    rest = product - high.astype(F32)
    middle = rest.astype(BF16)
    low = (rest - middle.astype(F32)).astype(BF16)
    stats = dot(high, collect) + dot(middle, collect) + dot(low, collect)
    row_lane = lax.broadcasted_iota(jnp.int32, (rows, LANES), 1)
    aug_ref[...] = jnp.where(row_lane < 48, lane_parts(stats, row_lane), 0.0).astype(BF16)

    @pl.when(step == steps - 1)
    def _():
        keep_and_give(bit_ref[0], total[...], keep_ref, give_ref)
        lane = lax.broadcasted_iota(jnp.int32, (width, LANES), 1)
        gains = jnp.broadcast_to(gain_grad_ref[...], (LANES, width)).T
        small = jnp.where(lane == LANES - 1, gains, router_grad_ref[...].T)
        keep_and_give(bit_ref[0], small, keep_ref, give_ref, width)


def hidden_back(bit, hidden, second, own, sent, att, cot, gates, route_row, out_full, gain, shards, experts, room, block=256):
    rows, width = cot.shape
    steps = rows // block
    half = steps // 2
    part = width // shards // 2
    own_columns = width + 3 * LANES
    here = lambda i, _: (i, 0)
    wide = lambda index: pl.BlockSpec((block, width), index)
    low = wide(lambda i, _: (jnp.minimum(i, half - 1), 0))
    high = wide(lambda i, _: (jnp.maximum(i - half, 0), 0))
    along = lambda height: pl.BlockSpec((height, block), lambda i, _: (0, i))
    return pl.pallas_call(
        functools.partial(hidden_back_kernel, experts=experts),
        grid_spec=pltpu.PrefetchScalarGridSpec(
            num_scalar_prefetch=1,
            grid=(steps,),
            in_specs=[low, high] * 2
            + [wide(here)] * 4
            + [
                along(8),
                along(8),
                along(1),
                pl.BlockSpec((width, LANES), lambda *_: (0, width // LANES)),
                pl.BlockSpec((width, width), lambda *_: (0, 0)),
                whole_spec((1, width)),
            ],
            out_specs=[
                wide(here),
                wide(here),
                pl.BlockSpec((block, LANES), here),
                pl.BlockSpec((block, LANES), here),
                whole_spec((shards, part, own_columns)),
                whole_spec((shards, part, own_columns)),
            ],
            scratch_shapes=[
                pltpu.VMEM((width, width), F32),
                pltpu.VMEM((LANES, width), F32),
                pltpu.VMEM((1, width), F32),
            ],
        ),
        out_shape=[
            jax.ShapeDtypeStruct((rows, width), F32),
            jax.ShapeDtypeStruct((rows, width), BF16),
            jax.ShapeDtypeStruct((rows, LANES), BF16),
            jax.ShapeDtypeStruct((rows, LANES), F32),
            jax.ShapeDtypeStruct((shards, part, room * 3 * LANES), BF16),
            jax.ShapeDtypeStruct((shards, part, room * 3 * LANES), BF16),
        ],
        compiler_params=params(40),
        cost_estimate=lasting(12),
        name="hidden_back",
    )(bit, *own, *sent, hidden, second, att, cot, *gates, route_row, out_full, out_full, gain)


def token_back_kernel(tok_ref, grad_ref, gain_ref, *refs):
    weights, triples, out_ref = refs[:GATHERS], refs[GATHERS:-1], refs[-1]
    rows = tok_ref[...].astype(F32)
    scale = lax.rsqrt(jnp.mean(rows * rows, axis=1, keepdims=True) + EPSILON)
    grads = jnp.concatenate([t[p] for p in range(3) for t in triples], axis=1)
    span = grads.shape[1] // len(weights)
    grad_normed = jnp.zeros(rows.shape, F32)
    for at, weight in enumerate(weights):
        grad_normed += dot(grads[:, at * span : (at + 1) * span], weight[...], NT)
    scaled_rows = rows * scale
    scaled = grad_normed * gain_ref[...]
    mean = jnp.mean(scaled * scaled_rows, axis=1, keepdims=True)
    out_ref[...] = (grad_ref[...] + scale * (scaled - scaled_rows * mean)).astype(BF16)


def token_back(tokens, grad_hidden, grad_triples, weights, gain_row, block=256):
    rows, width = tokens.shape
    here = lambda i: (i, 0)
    return pl.pallas_call(
        token_back_kernel,
        grid=(rows // block,),
        in_specs=[
            pl.BlockSpec((block, width), here),
            pl.BlockSpec((block, width), here),
            whole_spec((1, width)),
        ]
        + [whole_spec((width, 3 * width // len(weights))) for w in weights]
        + [pl.BlockSpec((3, block, t.shape[2]), lambda i: (0, i, 0)) for t in grad_triples],
        out_specs=pl.BlockSpec((block, width), here),
        out_shape=jax.ShapeDtypeStruct((rows, width), BF16),
        compiler_params=params(20),
        cost_estimate=lasting(9),
        name="token_back",
    )(tokens, grad_hidden, gain_row, *weights, *grad_triples)


def swap(value, axis, step=1):
    size = lax.axis_size(axis)
    return lax.ppermute(value, axis, [(i, i ^ step) for i in range(size)])


def bit_of(axis, step):
    return lax.axis_index(axis) // step % 2


def bits(size, first=1):
    return [1 << n for n in range(first.bit_length() - 1, size.bit_length() - 1)]


def rounded(parts):
    return sum(part.astype(F32) for part in parts).astype(BF16)


def exchange(parts, axis, step, pick):
    bit = bit_of(axis, step)
    give = rounded([pick(part, 1 - bit) for part in parts])
    return [pick(part, bit) for part in parts] + [swap(give, axis, step)]


def halve(parts, axis, step):
    def pick(part, bit):
        parted = part.reshape((part.shape[0], 2, part.shape[1] // 2) + part.shape[2:])
        return lax.dynamic_index_in_dim(parted, bit, 1, keepdims=False)

    return exchange(parts, axis, step, pick)


def to_owner(parts, steps):
    def pick(part, bit):
        parted = part.reshape((part.shape[0] // 2, 2) + part.shape[1:])
        return lax.dynamic_index_in_dim(parted, bit, 1, keepdims=False)

    for step in steps:
        parts = exchange(parts, "shard", step, pick)
    return parts


def to_owner_early(parts):
    return to_owner(parts, bits(lax.axis_size("shard"))[:-1])


def to_owner_last(parts):
    return to_owner(parts, bits(lax.axis_size("shard"))[-1:])


def both(parts, axis, step):
    mine = rounded(parts)
    return [mine, swap(mine, axis, step)]


def unhalve(value, axis, step, dim):
    other = swap(value, axis, step)
    first = bit_of(axis, step) == 0
    low = jnp.where(first, value, other)
    high = jnp.where(first, other, value)
    return jnp.concatenate([low, high], axis=dim)


def neighbours(parts):
    return halve(parts, "dp", 1) if lax.axis_size("dp") > 1 else parts


def spread(parts):
    for step in bits(lax.axis_size("dp"), 2):
        parts = halve(parts, "dp", step)
    return parts


def unspread(value):
    for step in reversed(bits(lax.axis_size("dp"), 2)):
        value = unhalve(value, "dp", step, 0)
    return value


def summed(parts):
    for step in bits(lax.axis_size("dp"), 2):
        parts = both(parts, "dp", step)
    return parts


def finish_expert(early, late, local):
    early, late = rounded(early)[0], rounded(late)[0]
    whole = jnp.concatenate([unspread(early), rounded(summed([late]))], axis=0)
    if lax.axis_size("dp") > 1:
        whole = unhalve(whole, "dp", 1, 0)
    return whole.reshape((local, -1) + whole.shape[1:]).astype(F32)


def tie(value, *sums):
    value, *last = lax.optimization_barrier((value,) + tuple(parts[-1] for parts in sums))
    return (value, *(parts[:-1] + [part] for parts, part in zip(sums, last)))


def plane_axes():
    return [(axis, step) for axis, step in (("dp", 2), ("expert", 1)) if lax.axis_size(axis) > step]


def plane_send(value, other):
    sizes = [lax.axis_size("dp"), lax.axis_size("expert")]
    flips = [0, 0]
    for n, (axis, step) in enumerate(plane_axes()):
        flips[axis == "expert"] |= step * (other >> n & 1)
    perm = [
        (d * sizes[1] + e, (d ^ flips[0]) * sizes[1] + (e ^ flips[1]))
        for d in range(sizes[0])
        for e in range(sizes[1])
    ]
    return lax.ppermute(value, ("dp", "expert"), perm)


def plane_index():
    return sum(bit_of(axis, step) << n for n, (axis, step) in enumerate(plane_axes()))


def dense_across(parts):
    count = 1 << len(plane_axes())
    me = plane_index()

    def pick(part, index):
        parted = part.reshape((part.shape[0], count, -1) + part.shape[2:])
        return lax.dynamic_index_in_dim(parted, index, 1, keepdims=False)

    got = [
        plane_send(rounded([pick(part, me ^ other) for part in parts]), other)
        for other in range(1, count)
    ]
    return [pick(part, me) for part in parts] + got


def dense_owner(parts):
    me, count = lax.axis_index("shard"), lax.axis_size("shard")
    pick = lambda part, index: lax.dynamic_index_in_dim(part, index, 0, keepdims=False)
    got = []
    for other in range(1, count):
        give = rounded([pick(part, me ^ other) for part in parts])
        got.append(swap(give, "shard", other))
    return [pick(part, me) for part in parts] + got


def dense_finish(parts):
    for step in bits(lax.axis_size("expert"), 2):
        parts = both(parts, "expert", step)
    for step in bits(lax.axis_size("dp"), 4):
        parts = both(parts, "dp", step)
    mine = rounded(parts)
    count = 1 << len(plane_axes())
    me = plane_index()
    pieces = [mine] + [plane_send(mine, other) for other in range(1, count)]
    rows = []
    for index in range(count):
        row = pieces[0]
        for other in range(1, count):
            row = jnp.where(me ^ index == other, pieces[other], row)
        rows.append(row)
    value = jnp.concatenate(rows, axis=0)
    return unhalve(value, "dp", 1, 0).astype(F32)


def gather_far(value):
    shards, parts = lax.axis_size("shard"), lax.axis_size("dp")
    rows, columns = value.shape
    parted = value.reshape(parts, rows // parts, columns)
    mine = lax.dynamic_index_in_dim(parted, lax.axis_index("dp"), 0, keepdims=False)
    me = lax.axis_index("shard")
    whole = lax.dynamic_update_index_in_dim(
        jnp.zeros((shards,) + mine.shape, value.dtype), mine, me, 0
    )
    for away in range(1, shards):
        piece = lax.ppermute(mine, "shard", [(i, (i + away) % shards) for i in range(shards)])
        whole = lax.dynamic_update_index_in_dim(whole, piece, (me - away) % shards, 0)
    return whole[:, None]


def gather_step(whole, step):
    other = swap(whole, "dp", step)
    first = bit_of("dp", step) == 0
    low, high = jnp.where(first, whole, other), jnp.where(first, other, whole)
    whole = jnp.stack([low, high], axis=2)
    return whole.reshape((whole.shape[0], -1) + whole.shape[3:])


def gather_near(whole, steps):
    for step in steps:
        whole = gather_step(whole, step)
    return whole


def places_of(route_ids, first, local, capacity):
    owned = route_ids - first
    choose = owned[:, None] == jnp.arange(local, dtype=jnp.int32)[None, :]
    rank = jnp.cumsum(choose.astype(jnp.int32), axis=0) - 1
    slot = jnp.sum(jnp.where(choose, rank, 0), axis=1) + owned * capacity
    full = (rank[-1] >= capacity // 2).astype(jnp.int32)
    return jnp.where(jnp.any(choose, axis=1), slot, -1), full


def experts_of_pairs(second, cotangent, routes, out_full, expert_in, expert_out, experts, early):
    rows, width = cotangent.shape
    local, _, ff = expert_in.shape
    capacity = 2 * rows // experts
    ff_block = ff // lax.axis_size("shard")
    other_cot, other_routes, own_place, other_place = early
    other_second = swap(second, "expert")
    results, flags = [], []
    for rows_of, cot, route_ids, (place, full) in (
        (second, cotangent, routes, own_place),
        (other_second, other_cot, other_routes, other_place),
    ):
        if results:
            rows_of, _ = lax.optimization_barrier((rows_of, results[0][7]))
        results.append(
            expert_rows(
                full[None],
                rows_of,
                cot,
                route_ids[None, :],
                out_full,
                place,
                expert_in,
                expert_out,
                capacity,
                experts,
                ff_block,
            )
        )
        flags.append(full)
    own, other = results
    full = jnp.stack(flags)
    keep = bit_of("dp", 1)
    one = lambda expert: expert[None].astype(jnp.int32)
    grad = lambda expert, left, right: weight_grad(
        full, one(expert), left, right, capacity, ff_block
    )
    acts, grads = (own[0], other[0]), (own[3], other[3])
    xs, grad_pres = (own[2], other[2]), (own[1], other[1])
    back_a = swap(other[5], "expert")
    sent_gate = swap(other[7], "expert")
    out_give = grad(1 - keep, acts, grads)
    full, *out_give = lax.optimization_barrier((full, *out_give))
    out_keep = grad(keep, acts, grads)
    full, back_a, sent_gate, back_b, *out_both = lax.optimization_barrier(
        (full, back_a, sent_gate, other[6], *out_keep, *out_give)
    )
    back_b = swap(back_b, "expert")
    out_keep, out_sent = out_both[:2], [swap(part, "dp") for part in out_both[2:]]
    in_give = grad(1 - keep, xs, grad_pres)
    full, *out_sent = lax.optimization_barrier((full, *out_sent, *in_give))
    out_sent, in_give = out_sent[:2], out_sent[2:]
    in_sent = [swap(part, "dp") for part in in_give]
    out_early = spread([out_keep[0], out_sent[0]])
    out_late = to_owner_early([out_keep[1], out_sent[1]])
    in_keep = grad(keep, xs, grad_pres)
    gate, *in_keep = lax.optimization_barrier((own[7], *in_keep))
    in_near = tuple([mine, sent] for mine, sent in zip(in_keep, in_sent))
    return (own[4], other[4]), (own[5:7], (back_a, back_b)), (gate, sent_gate), in_near, (out_early, out_late)


def experts_of_many(second, cotangent, route_ids, router, expert_in, expert_out):
    tok_rows, width = second.shape
    experts_all = router.shape[1]
    local, _, ff = expert_in.shape
    groups = lax.axis_size("expert")
    shards = lax.axis_size("shard")
    capacity = 2 * tok_rows // experts_all
    choose = route_ids[:, None] == jnp.arange(experts_all, dtype=jnp.int32)[None, :]
    rank = jnp.cumsum(choose.astype(jnp.int32), axis=0) - 1
    slot_index = route_ids * capacity + jnp.sum(jnp.where(choose, rank, 0), axis=1)
    probs = jax.nn.softmax(dot(second, router), axis=-1)
    gate = jnp.sum(jnp.where(choose, probs, 0.0), axis=1)

    def across(value):
        return lax.all_to_all(value, "expert", split_axis=0, concat_axis=0, tiled=True)

    def to_slots(token_rows):
        filled = jnp.zeros((experts_all * capacity, width), token_rows.dtype)
        filled = filled.at[slot_index].set(token_rows)
        return across(filled.reshape(groups, local, capacity, width))

    def from_slots(value):
        return across(value).reshape(experts_all * capacity, width)[slot_index]

    def einsum(form, left, right):
        return jnp.einsum(form, left, right, preferred_element_type=F32)

    def gelu(value):
        return jax.nn.gelu(value, approximate=True)

    grad_out = cotangent.astype(F32)
    arrived = to_slots(second)
    pre_act, pull = jax.vjp(gelu, einsum("aecd,edf->aecf", arrived, expert_in))
    activated = pre_act.astype(BF16)
    produced = einsum("aecf,efd->aecd", activated, expert_out).astype(BF16)
    returned = from_slots(produced)
    inner = jnp.sum(grad_out * returned.astype(F32), axis=1)
    grad_arrived = to_slots((gate[:, None] * grad_out).astype(BF16))
    grad_act = einsum("aecd,efd->aecf", grad_arrived, expert_out)
    grad_pre = pull(grad_act)[0].astype(BF16)
    grad_w_out = einsum("aecf,aecd->efd", activated, grad_arrived).astype(BF16)
    grad_w_in = einsum("aecd,aecf->edf", arrived, grad_pre).astype(BF16)
    back = from_slots(einsum("aecf,edf->aecd", grad_pre, expert_in).astype(BF16))
    grad_w_in = grad_w_in.reshape(local, width, shards, ff // shards).transpose(2, 0, 1, 3)
    grad_w_out = grad_w_out.reshape(local, shards, ff // shards, width).transpose(1, 0, 2, 3)
    def near(value):
        parts = neighbours([value.reshape((shards, -1) + value.shape[3:])])
        cut = early_rows(parts[0].shape[1])
        return [part[:, :cut] for part in parts], [part[:, cut:] for part in parts]

    out_early, out_late = near(grad_w_out)
    back = jnp.split(back, 2, axis=0)
    nothing = [jnp.zeros_like(part) for part in back]
    inner = jnp.broadcast_to(inner[None, :], (8, tok_rows))
    return (
        (returned, jnp.zeros_like(returned)),
        (back, nothing),
        (inner, jnp.zeros_like(inner)),
        near(grad_w_in),
        (spread(out_early), to_owner_early(out_late)),
    )


def body(
    tokens,
    segments,
    routes,
    cotangent,
    attn_in,
    attn_out,
    router,
    gain_one,
    gain_two,
    expert_in,
    expert_out,
):
    rows, width = tokens.shape
    experts = router.shape[1]
    local = expert_in.shape[0]
    lanes_of = lambda value: jnp.pad(value[:, None], ((0, 0), (0, LANES - 1)))
    padded = lambda value: jnp.pad(value, ((0, 0), (0, LANES - experts)))
    segment_col = segments[0][:, None]
    route_ids = routes.reshape(rows)
    bit = bit_of("dp", 1)[None].astype(jnp.int32)
    shards = lax.axis_size("shard")
    pairs_only = lax.axis_size("expert") == local == 2
    early = None

    span = 3 * width // GATHERS
    pieces = [attn_in[:, g * span : (g + 1) * span] for g in range(GATHERS)]
    pieces[0] = jnp.concatenate([pieces[0], lanes_of(gain_one)], axis=1)
    shares = [gather_far(piece) for piece in pieces]
    source = jnp.concatenate([attn_out, padded(router), lanes_of(gain_two)], axis=1)
    own_place, other_place = (), ()
    if pairs_only:
        other_routes = swap(route_ids, "expert")
        slots = (lax.axis_index("expert") * local, local, 2 * rows // experts)
        own_place = places_of(route_ids, *slots)
        other_place = places_of(other_routes, *slots)
    source, own_place, *shares = lax.optimization_barrier((source, own_place, *shares))
    near_steps = bits(lax.axis_size("dp"))[::-1]
    join = lambda whole: whole.reshape(-1, whole.shape[-1])
    weights = [join(gather_near(share, near_steps)) for share in shares]
    share = gather_far(source)
    first_gain = weights[0][:, span].astype(F32)[None, :]
    share, other_place, *weights = lax.optimization_barrier((share, other_place, *weights))
    share = gather_near(share, near_steps[:-1])
    if pairs_only:
        early = (swap(cotangent, "expert"), other_routes, own_place, other_place)

    normed, triple = qkv(tokens, first_gain, weights, span)
    triple, share = lax.optimization_barrier((triple, share))
    out_full = join(gather_near(share, near_steps[-1:]))
    second_gain = out_full[:, width + LANES].astype(F32)[None, :]
    attended, qaug = attend_forward(triple, segment_col)
    if pairs_only:
        attended, other_cot = lax.optimization_barrier((attended, early[0]))
        early = (other_cot,) + early[1:]
    hidden, second = project(tokens, attended, out_full, second_gain)
    if pairs_only:
        done = experts_of_pairs(
            second, cotangent, route_ids, out_full, expert_in, expert_out, experts, early
        )
    else:
        full_router = out_full[:, width : width + experts]
        done = experts_of_many(
            second, cotangent, route_ids, full_router, expert_in, expert_out
        )
    returned, (own_back, sent_back), inner, in_near, (out_early, out_late) = done

    in_early, in_late = in_near
    gate, out_late, in_early, in_late = tie(inner[0], out_late, in_early, in_late)
    out_late = to_owner_last(out_late)
    in_late = to_owner_early(in_late)
    heads = width // 64 // GROUPS
    pieces = heads // 2
    rooms = (width // LANES // 3 + 1 + pieces, (GROUPS - 1) * pieces)
    grad_hidden, grad_att, gaug, gates, *dense_a = hidden_back(
        bit,
        hidden,
        second,
        own_back,
        sent_back,
        attended,
        cotangent,
        (gate, inner[1]),
        route_ids[None, :],
        out_full,
        second_gain,
        shards,
        experts,
        rooms[0],
    )

    def back(grad, group, place, room, halves=()):
        return attend_backward(
            bit, triple, grad, segment_col, qaug, gaug, normed, shards, group * heads, heads, place, room, halves
        )

    grad_att, out_early, in_late, (made,) = tie(grad_att, out_early, in_late, [returned[1]])
    made = swap(made, "expert") if pairs_only else made
    out_early = to_owner_early(out_early)
    in_early = spread(in_early)
    grads_0, *dense_a = back(grad_att, 0, rooms[0] - pieces, rooms[0], dense_a)

    grad_att, out_early, out_late, *dense_a = tie(grad_att, out_early, out_late, *([d] for d in (*dense_a, grads_0)))
    (keep_a,), (give_a,), (grads_0,) = dense_a
    dense_a = [keep_a, swap(give_a, "dp")]
    out_early = to_owner_last(out_early)
    in_late = to_owner_last(in_late)
    grads_1, *dense_b = back(grad_att, 1, 0, rooms[1])

    grad_att, in_early, dense_a, (grads_1,) = tie(grad_att, in_early, dense_a, [grads_1])
    in_early = to_owner_early(in_early)
    dense_a = dense_across(dense_a)
    grads_2, *dense_b = back(grad_att, 2, pieces, rooms[1], dense_b)
    dense_b = [dense_b[0], swap(dense_b[1], "dp")]

    grad_hidden, in_early, out_early, in_late, dense_a, (grads_2,) = tie(
        grad_hidden, in_early, out_early, in_late, dense_a, [grads_2]
    )
    in_early = to_owner_last(in_early)
    final_out = finish_expert(out_early, out_late, local)
    dense_a = dense_owner(dense_a)
    grad_tokens = token_back(
        tokens, grad_hidden, (grads_0, grads_1, grads_2), weights, first_gain
    )
    dense_b = dense_across(dense_b)
    dense_a = dense_finish(dense_a)
    dense_b = dense_finish(dense_owner(dense_b))
    final_in = finish_expert(in_early, in_late, local)

    start = width + 3 * LANES
    pair_columns = lambda value, start: [
        value[:, c : c + LANES] for c in range(start, value.shape[1], LANES)
    ]
    columns = pair_columns(dense_a, start) + pair_columns(dense_b, 0)
    grad_attn_in = jnp.concatenate(columns[0::3] + columns[1::3] + columns[2::3], axis=1)
    grad_gain_one = jnp.sum(attn_in.astype(F32) * grad_attn_in, axis=1) / gain_one.astype(F32)

    wide = returned[0].astype(F32) + made.astype(F32)
    layer = hidden + gates[:, :1] * wide
    return (
        layer.astype(BF16),
        grad_tokens,
        grad_attn_in,
        dense_a[:, :width],
        dense_a[:, width : width + experts],
        grad_gain_one,
        dense_a[:, width + LANES - 1],
        final_in,
        final_out,
    )


def solution(mesh):
    everywhere = P(("dp", "expert", "shard"), None)
    placed = (everywhere,) * 4 + (P("shard", None),) * 3 + (P("shard"),) * 2
    placed = placed + (P("expert", None, None),) * 2
    outs = (everywhere,) * 2 + (P("shard", None),) * 3 + (P("shard"),) * 2
    outs = outs + (P("expert", None, "shard"), P("expert", "shard", None))
    return jax.shard_map(
        body, mesh=mesh, in_specs=placed, out_specs=outs, check_vma=False
    )
```
